32 devices in a mesh: dp: 8 (over z, y), mp: 4 (over x, core).
Axes of the slice: x: 2, y: 2, z: 4, core: 2. Of those that a mesh axis runs over, the one named last changes fastest.
Arguments:
- patches: bfloat16 [192, 49, 3072], P(('dp', 'mp')), may hold values from -6 to 6
- keep_list: int32 [192, 49], P(('dp', 'mp')), may hold values from 0 to 48, each once within a row
- keep_count: int32 [192], P(('dp', 'mp')), may hold values from 24 to 49, as said below
- labels: int32 [192], P(('dp', 'mp')), may hold values from 0 to 999
- patch_weight: float32 [3072, 1024], P(('dp', 'mp')), may hold values from -0.109375 to 0.109375
- vector_table: float32 [66, 1024], replicated, may hold values from -2 to 2
- head_table: float32 [1025, 1000], replicated, may hold values from -0.1875 to 0.1875
- joint_weight: float32 [2, 1024, 3, 1024], P(None, 'dp', None, 'mp'), may hold values from -0.1875 to 0.1875
- shift_table: float32 [2, 2, 1024], replicated, may hold values from -4 to 4
- output_weight: float32 [2, 1024, 1024], P(None, 'mp', 'dp'), may hold values from -0.5 to 0.5
- expand_weight: float32 [2, 1024, 4096], P(None, 'dp', 'mp'), may hold values from -0.1875 to 0.1875
- raise_table: float32 [2, 4096], replicated, may hold values from -4 to 4
- shrink_weight: float32 [2, 4096, 1024], P(None, 'mp', 'dp'), may hold values from -0.09375 to 0.09375
- patch_first: float32 [3072, 1024], P(('dp', 'mp')), may hold values from -5.722046e-06 to 5.722046e-06
- vector_first: float32 [66, 1024], replicated, may hold values from -5.722046e-06 to 5.722046e-06
- head_first: float32 [1025, 1000], replicated, may hold values from -5.722046e-06 to 5.722046e-06
- joint_first: float32 [2, 1024, 3, 1024], P(None, 'dp', None, 'mp'), may hold values from -5.722046e-06 to 5.722046e-06
- shift_first: float32 [2, 2, 1024], replicated, may hold values from -5.722046e-06 to 5.722046e-06
- output_first: float32 [2, 1024, 1024], P(None, 'mp', 'dp'), may hold values from -5.722046e-06 to 5.722046e-06
- expand_first: float32 [2, 1024, 4096], P(None, 'dp', 'mp'), may hold values from -5.722046e-06 to 5.722046e-06
- raise_first: float32 [2, 4096], replicated, may hold values from -5.722046e-06 to 5.722046e-06
- shrink_first: float32 [2, 4096, 1024], P(None, 'mp', 'dp'), may hold values from -5.722046e-06 to 5.722046e-06
- patch_second: float32 [3072, 1024], P(('dp', 'mp')), may hold values from 3.53544e-13 to 2.8555476e-12
- vector_second: float32 [66, 1024], replicated, may hold values from 3.53544e-13 to 2.8555476e-12
- head_second: float32 [1025, 1000], replicated, may hold values from 3.53544e-13 to 2.8555476e-12
- joint_second: float32 [2, 1024, 3, 1024], P(None, 'dp', None, 'mp'), may hold values from 3.53544e-13 to 2.8555476e-12
- shift_second: float32 [2, 2, 1024], replicated, may hold values from 3.53544e-13 to 2.8555476e-12
- output_second: float32 [2, 1024, 1024], P(None, 'mp', 'dp'), may hold values from 3.53544e-13 to 2.8555476e-12
- expand_second: float32 [2, 1024, 4096], P(None, 'dp', 'mp'), may hold values from 3.53544e-13 to 2.8555476e-12
- raise_second: float32 [2, 4096], replicated, may hold values from 3.53544e-13 to 2.8555476e-12
- shrink_second: float32 [2, 4096, 1024], P(None, 'mp', 'dp'), may hold values from 3.53544e-13 to 2.8555476e-12
Outputs:
- loss_total: float32 [], replicated
- gradient_norm: float32 [], replicated
- patch_update: float32 [3072, 1024], P(('dp', 'mp'))
- patch_momentum: float32 [3072, 1024], P(('dp', 'mp'))
- patch_variance: float32 [3072, 1024], P(('dp', 'mp'))
- vector_update: float32 [66, 1024], replicated
- vector_momentum: float32 [66, 1024], replicated
- vector_variance: float32 [66, 1024], replicated
- head_update: float32 [1025, 1000], replicated
- head_momentum: float32 [1025, 1000], replicated
- head_variance: float32 [1025, 1000], replicated
- joint_update: float32 [2, 1024, 3, 1024], P(None, 'dp', None, 'mp')
- joint_momentum: float32 [2, 1024, 3, 1024], P(None, 'dp', None, 'mp')
- joint_variance: float32 [2, 1024, 3, 1024], P(None, 'dp', None, 'mp')
- shift_update: float32 [2, 2, 1024], replicated
- shift_momentum: float32 [2, 2, 1024], replicated
- shift_variance: float32 [2, 2, 1024], replicated
- output_update: float32 [2, 1024, 1024], P(None, 'mp', 'dp')
- output_momentum: float32 [2, 1024, 1024], P(None, 'mp', 'dp')
- output_variance: float32 [2, 1024, 1024], P(None, 'mp', 'dp')
- expand_update: float32 [2, 1024, 4096], P(None, 'dp', 'mp')
- expand_momentum: float32 [2, 1024, 4096], P(None, 'dp', 'mp')
- expand_variance: float32 [2, 1024, 4096], P(None, 'dp', 'mp')
- raise_update: float32 [2, 4096], replicated
- raise_momentum: float32 [2, 4096], replicated
- raise_variance: float32 [2, 4096], replicated
- shrink_update: float32 [2, 4096, 1024], P(None, 'mp', 'dp')
- shrink_momentum: float32 [2, 4096, 1024], P(None, 'mp', 'dp')
- shrink_variance: float32 [2, 4096, 1024], P(None, 'mp', 'dp')
The draws below stay inside these ranges and needn't reach their ends.
Inputs may be any that keep to these rules, and one draw needn't show every extreme that they name: `keep_list`: each row is an ordering of the patch numbers; the first keep_count entries of a row are the kept patches. `keep_count`: some image keeps all 49 patches and some exactly 24.
All inputs are finite; a program needn't handle non-finite values.
Results may differ from the reference program's by a relative error of at most 0.012.
Values may be sent and summed in bfloat16 or wider, within the bound.
No kernel may reach another device: no remote copies, remote signals or barrier semaphores. Data moves between devices by JAX's collectives and lax.ppermute only.
A program may use at most 256 MiB of HBM per device.

```python
import math
import jax
import jax.numpy as jnp
from jax import lax

D = 1024
HEADS = 16
HEAD_DIM = 64
FF = 4096
CLASSES = 1000
PIX = 3072
PATCHES = 49
MIN_KEEP = 24
LAYERS = 2
STEP = 10
IMG_DEV = 24
SLOTS = 50
IMAGES = 192
VROWS = 66
PARAMS = 29416424


def draw_keep_count(key, part):
    key = jax.random.fold_in(key, 11)
    count_key, place_key, offset_key = jax.random.split(key, 3)
    counts = jax.random.randint(count_key, (IMAGES,), MIN_KEEP, PATCHES + 1)
    full_spot = jax.random.randint(place_key, (), 0, IMAGES)
    least_spot = (full_spot + 1 + jax.random.randint(offset_key, (), 0, IMAGES - 1)) % IMAGES
    counts = counts.at[full_spot].set(PATCHES).at[least_spot].set(MIN_KEEP)
    return counts.astype(jnp.int32)


def draw_vector_table(key, part):
    key = jax.random.fold_in(key, 23)
    row_ids = jnp.arange(VROWS)[:, None]
    row_offset = row_ids - (SLOTS + 4)
    is_gain = (row_ids == SLOTS + 2) | (row_offset >= 0) & ((row_offset % 6 == 0) | (row_offset % 6 == 2))
    noise_draw = jnp.clip(jax.random.normal(key, (VROWS, D), jnp.float32), -4.0, 4.0)
    row_scale = jnp.where(row_ids < SLOTS, 0.5, 0.3)
    return jnp.where(is_gain, 1.0 + 0.2 * noise_draw, row_scale * noise_draw).astype(jnp.float32)


def touch_ends(drawn, rng, least, high):
    longest = drawn.shape.index(max(drawn.shape))
    spots = []
    for shift in (0, 1):
        where = [jax.random.randint(jax.random.fold_in(rng, axis), (), 0, length) for axis, length in enumerate(drawn.shape)]
        where[longest] = (where[longest] + shift) % drawn.shape[longest]
        spots.append(tuple(where))
    return drawn.at[spots[0]].set(least).at[spots[1]].set(high)


def shard_levels(own_key, extent, cuts, least, high):
    def one(axis_at, parts):
        steps = jax.random.uniform(jax.random.fold_in(jax.random.fold_in(own_key, 6), axis_at), (parts,), jnp.float32, least / len(cuts), high / len(cuts))
        return jnp.repeat(jnp.exp(steps), extent[axis_at] // parts).reshape((-1,) + (1,) * (len(extent) - axis_at - 1))

    level = one(*cuts[0])
    for cut in cuts[1:]:
        level = level * one(*cut)
    return level


def normal_values(rng, extent, deviation, bound, cuts=(), kind=jnp.bfloat16):
    array = jax.random.normal(rng, extent, jnp.float32) * deviation
    if len(cuts) > 0:
        array = shard_levels(rng, extent, cuts, -0.22, 0.18) * array
    return jnp.clip(array, min=-bound, max=bound).astype(kind)


def setup_inputs(seed: int = 0) -> dict:
    streams_of = jax.random.split(jax.random.key(seed), 32)
    patches = normal_values(streams_of[0], (IMAGES, PATCHES, PIX), 1.0, 6.0, ((0, 32),))
    keep_list = jax.vmap(lambda own: jax.random.permutation(own, PATCHES))(jax.random.split(streams_of[1], IMAGES)).reshape((IMAGES, PATCHES)).astype(jnp.int32)
    keep_count = draw_keep_count(jax.random.fold_in(streams_of[31], 71), 0)
    labels = touch_ends(jax.random.randint(streams_of[3], (IMAGES,), 0, CLASSES), jax.random.fold_in(streams_of[3], 1), 0, CLASSES - 1).astype(jnp.int32)
    patch_weight = normal_values(streams_of[4], (PIX, D), PIX ** -0.5, 0.109375, ((0, 32),), jnp.float32)
    vector_table = draw_vector_table(jax.random.fold_in(streams_of[31], 71), 0)
    head_table = normal_values(streams_of[6], (D + 1, CLASSES), D ** -0.5, 0.1875, (), jnp.float32)
    joint_weight = normal_values(streams_of[7], (LAYERS, D, 3, D), D ** -0.5, 0.1875, ((1, 8), (3, 4)), jnp.float32)
    shift_table = normal_values(streams_of[8], (LAYERS, 2, D), 0.3, 4.0, (), jnp.float32)
    output_weight = normal_values(streams_of[9], (LAYERS, D, D), (D // 8) ** -0.5, 0.5, ((1, 4), (2, 8)), jnp.float32)
    expand_weight = normal_values(streams_of[10], (LAYERS, D, FF), D ** -0.5, 0.1875, ((1, 8), (2, 4)), jnp.float32)
    raise_table = normal_values(streams_of[11], (LAYERS, FF), 0.3, 4.0, (), jnp.float32)
    shrink_weight = normal_values(streams_of[12], (LAYERS, FF, D), FF ** -0.5, 0.09375, ((1, 4), (2, 8)), jnp.float32)
    patch_first = normal_values(streams_of[13], (PIX, D), (0.0022 * PARAMS ** -0.5), 5.7220458984375e-06, ((0, 32),), jnp.float32)
    vector_first = normal_values(streams_of[14], (VROWS, D), (0.0022 * PARAMS ** -0.5), 5.7220458984375e-06, (), jnp.float32)
    head_first = normal_values(streams_of[15], (D + 1, CLASSES), (0.0022 * PARAMS ** -0.5), 5.7220458984375e-06, (), jnp.float32)
    joint_first = normal_values(streams_of[16], (LAYERS, D, 3, D), (0.0022 * PARAMS ** -0.5), 5.7220458984375e-06, ((1, 8), (3, 4)), jnp.float32)
    shift_first = normal_values(streams_of[17], (LAYERS, 2, D), (0.0022 * PARAMS ** -0.5), 5.7220458984375e-06, (), jnp.float32)
    output_first = normal_values(streams_of[18], (LAYERS, D, D), (0.0022 * PARAMS ** -0.5), 5.7220458984375e-06, ((1, 4), (2, 8)), jnp.float32)
    expand_first = normal_values(streams_of[19], (LAYERS, D, FF), (0.0022 * PARAMS ** -0.5), 5.7220458984375e-06, ((1, 8), (2, 4)), jnp.float32)
    raise_first = normal_values(streams_of[20], (LAYERS, FF), (0.0022 * PARAMS ** -0.5), 5.7220458984375e-06, (), jnp.float32)
    shrink_first = normal_values(streams_of[21], (LAYERS, FF, D), (0.0022 * PARAMS ** -0.5), 5.7220458984375e-06, ((1, 4), (2, 8)), jnp.float32)
    patch_second = jnp.clip(jnp.exp(math.log(2.8555476126040924e-12) - 2.089011 * jax.random.uniform(streams_of[22], (PIX, D), jnp.float32) ** shard_levels(streams_of[22], (PIX, D), ((0, 32),), -0.2, 0.2)), 3.535439898737919e-13, 2.8555476126040924e-12)
    vector_second = jnp.clip(jnp.exp(jax.random.uniform(streams_of[23], (VROWS, D), jnp.float32, math.log(3.535439898737919e-13), math.log(2.8555476126040924e-12))), 3.535439898737919e-13, 2.8555476126040924e-12)
    head_second = jnp.clip(jnp.exp(jax.random.uniform(streams_of[24], (D + 1, CLASSES), jnp.float32, math.log(3.535439898737919e-13), math.log(2.8555476126040924e-12))), 3.535439898737919e-13, 2.8555476126040924e-12)
    joint_second = jnp.clip(jnp.exp(math.log(2.8555476126040924e-12) - 2.089011 * jax.random.uniform(streams_of[25], (LAYERS, D, 3, D), jnp.float32) ** shard_levels(streams_of[25], (LAYERS, D, 3, D), ((1, 8), (3, 4)), -0.2, 0.2)), 3.535439898737919e-13, 2.8555476126040924e-12)
    shift_second = jnp.clip(jnp.exp(jax.random.uniform(streams_of[26], (LAYERS, 2, D), jnp.float32, math.log(3.535439898737919e-13), math.log(2.8555476126040924e-12))), 3.535439898737919e-13, 2.8555476126040924e-12)
    output_second = jnp.clip(jnp.exp(math.log(2.8555476126040924e-12) - 2.089011 * jax.random.uniform(streams_of[27], (LAYERS, D, D), jnp.float32) ** shard_levels(streams_of[27], (LAYERS, D, D), ((1, 4), (2, 8)), -0.2, 0.2)), 3.535439898737919e-13, 2.8555476126040924e-12)
    expand_second = jnp.clip(jnp.exp(math.log(2.8555476126040924e-12) - 2.089011 * jax.random.uniform(streams_of[28], (LAYERS, D, FF), jnp.float32) ** shard_levels(streams_of[28], (LAYERS, D, FF), ((1, 8), (2, 4)), -0.2, 0.2)), 3.535439898737919e-13, 2.8555476126040924e-12)
    raise_second = jnp.clip(jnp.exp(jax.random.uniform(streams_of[29], (LAYERS, FF), jnp.float32, math.log(3.535439898737919e-13), math.log(2.8555476126040924e-12))), 3.535439898737919e-13, 2.8555476126040924e-12)
    shrink_second = jnp.clip(jnp.exp(math.log(2.8555476126040924e-12) - 2.089011 * jax.random.uniform(streams_of[30], (LAYERS, FF, D), jnp.float32) ** shard_levels(streams_of[30], (LAYERS, FF, D), ((1, 4), (2, 8)), -0.2, 0.2)), 3.535439898737919e-13, 2.8555476126040924e-12)
    return {"patches": patches, "keep_list": keep_list, "keep_count": keep_count, "labels": labels, "patch_weight": patch_weight, "vector_table": vector_table, "head_table": head_table, "joint_weight": joint_weight, "shift_table": shift_table, "output_weight": output_weight, "expand_weight": expand_weight, "raise_table": raise_table, "shrink_weight": shrink_weight, "patch_first": patch_first, "vector_first": vector_first, "head_first": head_first, "joint_first": joint_first, "shift_first": shift_first, "output_first": output_first, "expand_first": expand_first, "raise_first": raise_first, "shrink_first": shrink_first, "patch_second": patch_second, "vector_second": vector_second, "head_second": head_second, "joint_second": joint_second, "shift_second": shift_second, "output_second": output_second, "expand_second": expand_second, "raise_second": raise_second, "shrink_second": shrink_second}


@jax.custom_vjp
def low(v):
    return lax.optimization_barrier(v.astype(jnp.bfloat16)).astype(jnp.float32)

@jax.custom_vjp
def low_back(v):
    return v

def low_keep(v):
    return (low(v), None)

def low_pass(kept, grad):
    return (grad,)

def back_keep(v):
    return (v, None)

def back_low(kept, grad):
    return (low(grad),)
low.defvjp(low_keep, low_pass)
low_back.defvjp(back_keep, back_low)
group_rates = (0.01, 0.2, 0.01, 0.01, 0.1, 0.03, 0.01, 0.1, 0.01)
beta_one = 0.9
beta_two = 0.95
adam_eps = 1e-08
decay_rate = 0.1
clip_limit = 0.02
norm_eps = 1e-06
highest = lax.Precision.HIGHEST

def layer_norm(values, gain_row, shift_row):
    centre = values - lax.optimization_barrier(jnp.mean(values, -1, keepdims=True))
    spread = lax.optimization_barrier(jnp.mean(centre * centre, -1, keepdims=True))
    return centre * lax.rsqrt(spread + norm_eps) * gain_row + shift_row

def contract(form, left, right):
    return jnp.einsum(form, left, right, precision=highest)

def forward(params, pixels, keep_rows, counts, targets):
    patch_weight, vector_table, head_table, joint_weight, shift_table, output_weight, expand_weight, raise_table, shrink_weight = params
    images = pixels.shape[0]
    model_width = vector_table.shape[1]
    patch_ids = jnp.arange(PATCHES, dtype=jnp.int32)
    kept_slot = patch_ids[None, :] < counts[:, None]
    selector = ((keep_rows[:, :, None] == patch_ids[None, None, :]) & kept_slot[:, :, None]).astype(jnp.float32)
    chosen = contract('nsp,npc->nsc', selector, pixels)
    embedded = low_back(contract('nsc,cd->nsd', chosen, low(patch_weight)))
    tokens = embedded + kept_slot[:, :, None].astype(jnp.float32) * vector_table[SLOTS + 1] + contract('nsp,pd->nsd', selector, vector_table[1:SLOTS])
    leading = jnp.broadcast_to(vector_table[SLOTS] + vector_table[0], (images, 1, model_width))
    stream = jnp.concatenate([leading, tokens], 1)
    key_live = jnp.concatenate([jnp.ones((images, 1), bool), kept_slot], 1)
    for layer_index in range(LAYERS):
        row_base = SLOTS + 4 + 6 * layer_index
        normed = low(layer_norm(stream, vector_table[row_base], vector_table[row_base + 1]))
        joined = contract('ntd,dke->ntke', normed, low(joint_weight[layer_index]))
        query_rows = low(low_back(joined[:, :, 0]) + shift_table[layer_index, 0]).reshape(images, SLOTS, HEADS, HEAD_DIM)
        key_rows = low(low_back(joined[:, :, 1])).reshape(images, SLOTS, HEADS, HEAD_DIM)
        values = low(low_back(joined[:, :, 2]) + shift_table[layer_index, 1]).reshape(images, SLOTS, HEADS, HEAD_DIM)
        scores = low_back(contract('nqhe,nkhe->nhqk', query_rows, key_rows)) * 0.125
        scores = jnp.where(key_live[:, None, None, :], scores, -1e+30)
        attention = low(jax.nn.softmax(scores, -1))
        mixed_heads = low(low_back(contract('nhqk,nkhe->nqhe', attention, values))).reshape(images, SLOTS, model_width)
        stream = stream + low_back(contract('nte,ed->ntd', mixed_heads, low(output_weight[layer_index]))) + vector_table[row_base + 4]
        normed_two = low(layer_norm(stream, vector_table[row_base + 2], vector_table[row_base + 3]))
        hidden = low_back(contract('ntd,df->ntf', normed_two, low(expand_weight[layer_index]))) + raise_table[layer_index]
        active = low(jax.nn.gelu(hidden))
        stream = stream + low_back(contract('ntf,fd->ntd', active, low(shrink_weight[layer_index]))) + vector_table[row_base + 5]
    final_rows = low(layer_norm(stream[:, 0], vector_table[SLOTS + 2], vector_table[SLOTS + 3]))
    logits = low_back(contract('nd,dc->nc', final_rows, low(head_table[:model_width]))) + head_table[model_width]
    target_hot = (targets[:, None] == jnp.arange(CLASSES, dtype=jnp.int32)[None, :]).astype(jnp.float32)
    picked = lax.optimization_barrier(jnp.sum(logits * target_hot, -1))
    return jnp.sum(jax.nn.logsumexp(logits, -1) - picked)

def adamw(weight, moment_one, moment_two, gradient, rate):
    first_new = beta_one * moment_one + (1.0 - beta_one) * gradient
    second_new = beta_two * moment_two + (1.0 - beta_two) * gradient * gradient
    corrected = first_new / (1.0 - beta_one ** STEP)
    scaled = second_new / (1.0 - beta_two ** STEP)
    weight_new = weight - rate * (corrected / (jnp.sqrt(scaled) + adam_eps) + decay_rate * weight)
    return (weight_new, first_new, second_new)

def reference(patches, keep_list, keep_count, labels, patch_weight, vector_table, head_table, joint_weight, shift_table, output_weight, expand_weight, raise_table, shrink_weight, patch_first, vector_first, head_first, joint_first, shift_first, output_first, expand_first, raise_first, shrink_first, patch_second, vector_second, head_second, joint_second, shift_second, output_second, expand_second, raise_second, shrink_second):
    weights_in = (patch_weight, vector_table, head_table, joint_weight, shift_table, output_weight, expand_weight, raise_table, shrink_weight)
    firsts = (patch_first, vector_first, head_first, joint_first, shift_first, output_first, expand_first, raise_first, shrink_first)
    seconds = (patch_second, vector_second, head_second, joint_second, shift_second, output_second, expand_second, raise_second, shrink_second)
    groups = IMAGES // IMG_DEV
    pixel_groups = patches.astype(jnp.float32).reshape(groups, IMG_DEV, PATCHES, PIX)
    list_groups = keep_list.reshape(groups, IMG_DEV, PATCHES)
    count_groups = keep_count.reshape(groups, IMG_DEV)
    label_groups = labels.reshape(groups, IMG_DEV)

    def one_group(carried, group_item):
        loss_sum, gradients = carried
        pixels, keep_rows, counts, targets = group_item

        def partial_loss(*params):
            return forward(params, pixels, keep_rows, counts, targets)
        loss_value, pullback = jax.vjp(partial_loss, *weights_in)
        group_terms = pullback(jnp.asarray(1.0 / IMAGES, jnp.float32))
        return ((loss_sum + loss_value, tuple((total + term for total, term in zip(gradients, group_terms)))), None)
    zeros = tuple((jnp.zeros_like(weight) for weight in weights_in))
    (loss_total, gradients), unused = lax.scan(one_group, (jnp.zeros((), jnp.float32), zeros), (pixel_groups, list_groups, count_groups, label_groups))
    squares = jnp.zeros((), jnp.float32)
    for gradient in gradients:
        squares = squares + jnp.sum(gradient * gradient)
    gradient_norm = jnp.sqrt(squares)
    factor = jnp.minimum(1.0, clip_limit / (gradient_norm + norm_eps))
    updated = [adamw(weight, moment_one, moment_two, gradient * factor, rate) for weight, moment_one, moment_two, gradient, rate in zip(weights_in, firsts, seconds, gradients, group_rates)]
    return (loss_total, gradient_norm, updated[0][0], updated[0][1], updated[0][2], updated[1][0], updated[1][1], updated[1][2], updated[2][0], updated[2][1], updated[2][2], updated[3][0], updated[3][1], updated[3][2], updated[4][0], updated[4][1], updated[4][2], updated[5][0], updated[5][1], updated[5][2], updated[6][0], updated[6][1], updated[6][2], updated[7][0], updated[7][1], updated[7][2], updated[8][0], updated[8][1], updated[8][2])
```

```python
import jax
import jax.numpy as jnp
from jax import lax
from jax.sharding import PartitionSpec as P

HEAD_DIM = 64
FF = 4096
CLASSES = 1000
PATCHES = 49
LAYERS = 2
STEP = 10
SLOTS = 50


group_rates = (0.01, 0.2, 0.01, 0.01, 0.1, 0.03, 0.01, 0.1, 0.01)
beta_one = 0.9
beta_two = 0.95
adam_eps = 1e-08
decay_rate = 0.1
clip_limit = 0.02
norm_eps = 1e-06
highest = lax.Precision.HIGHEST


def layer_norm(values, gain_row, shift_row):
    centre = values - jnp.mean(values, -1, keepdims=True)
    spread = jnp.mean(centre * centre, -1, keepdims=True)
    return centre * lax.rsqrt(spread + norm_eps) * gain_row + shift_row


def product(form, left, right):
    return jnp.einsum(form, left, right, preferred_element_type=jnp.float32)


def adamw(weight, moment_one, moment_two, gradient, rate):
    first_new = beta_one * moment_one + (1.0 - beta_one) * gradient
    second_new = beta_two * moment_two + (1.0 - beta_two) * gradient * gradient
    corrected = first_new / (1.0 - beta_one**STEP)
    scaled = second_new / (1.0 - beta_two**STEP)
    weight_new = weight - rate * (corrected / (jnp.sqrt(scaled) + adam_eps) + decay_rate * weight)
    return (weight_new, first_new, second_new)


def attention_scores(query_rows, key_rows, key_live):
    scores = product("nqhe,nkhe->nhqk", query_rows, key_rows) * 0.125
    return jnp.where(key_live[:, None, None, :], scores, -1e30)

AXES = ("dp", "mp")


def swap(values, mask):
    count = lax.axis_size("dp") * lax.axis_size("mp")
    return lax.ppermute(values, AXES, [(n, n ^ mask) for n in range(count)])


def device_index():
    return lax.axis_index("dp") * lax.axis_size("mp") + lax.axis_index("mp")


def bit_masks():
    model, data = lax.axis_size("mp"), lax.axis_size("dp")
    wide = 1 << ((data.bit_length() - 1) // 2)
    z_masks = [m for m in (model * wide << b for b in range(16)) if m < model * data]
    y_masks = [m for m in (model << b for b in range(16)) if m < model * wide]
    x_masks = [m for m in (2 << b for b in range(16)) if m < model]
    return (z_masks, y_masks, x_masks, [1])


def offsets(masks):
    table = [0]
    for mask in masks:
        table = table + [entry ^ mask for entry in table]
    return table


def gather_blocks(values, masks):
    blocks = values[None]
    for mask in masks:
        blocks = jnp.concatenate([blocks, swap(blocks, mask)], 0)
    return blocks


def from_position(masks, shift):
    table = offsets(masks)
    inverse = [0] * len(table)
    for place, entry in enumerate(table):
        inverse[entry >> shift] = place
    here = (device_index() & sum(masks)) >> shift
    return jnp.take(jnp.array(inverse, jnp.int32), jnp.arange(len(table)) ^ here)


def to_position(masks, shift):
    here = (device_index() & sum(masks)) >> shift
    return jnp.array([entry >> shift for entry in offsets(masks)], jnp.int32) ^ here


def gather_ordered(values, masks, shift):
    return jnp.take(gather_blocks(values, masks), from_position(masks, shift), axis=0)


def reduce_blocks(blocks, masks):
    for mask in reversed(masks):
        half = blocks.shape[0] // 2
        blocks = blocks[:half] + swap(blocks[half:].astype(jnp.bfloat16), mask).astype(jnp.float32)
    return blocks[0]


def reduce_ordered(blocks, masks, shift):
    return reduce_blocks(jnp.take(blocks, to_position(masks, shift), axis=0), masks)


def sum_all(values):
    for masks in reversed(bit_masks()):
        for mask in masks:
            values = jax.tree.map(lambda v: v + swap(v, mask), values)
    return values


def group_gather(values):
    z_masks, y_masks, x_masks, c_masks = bit_masks()
    blocks = gather_blocks(values, x_masks + c_masks)
    return blocks.reshape((-1,) + values.shape[1:])


def group_reduce(values):
    z_masks, y_masks, x_masks, c_masks = bit_masks()
    model = lax.axis_size("mp")
    return reduce_blocks(values.reshape((model, -1) + values.shape[1:]), x_masks + c_masks)


def layer_forward(
    stream, key_share, layer_index, weights_now, vector_table, shift_table, raise_table
):
    joint, output, expand, shrink = weights_now
    row_base = SLOTS + 4 + 6 * layer_index
    local_width = joint.shape[2]
    local_hidden = expand.shape[1]
    heads_here = local_width // HEAD_DIM
    model_index = lax.axis_index("mp")
    shift_here = lax.dynamic_slice_in_dim(
        shift_table[layer_index], model_index * local_width, local_width, 1
    )
    raise_here = lax.dynamic_slice_in_dim(
        raise_table[layer_index], model_index * local_hidden, local_hidden, 0
    )
    normed = layer_norm(stream, vector_table[row_base], vector_table[row_base + 1]).astype(
        jnp.bfloat16
    )
    normed_all, key_all = (
        group_gather(normed),
        group_gather(key_share),
    )
    group_images = normed_all.shape[0]
    key_live = key_all > 0
    joined = product("ntd,dke->ntke", normed_all, joint)
    head_shape = (group_images, SLOTS, heads_here, HEAD_DIM)
    query_rows = (joined[:, :, 0] + shift_here[0]).astype(jnp.bfloat16).reshape(head_shape)
    key_rows = joined[:, :, 1].astype(jnp.bfloat16).reshape(head_shape)
    value_rows = (joined[:, :, 2] + shift_here[1]).astype(jnp.bfloat16).reshape(head_shape)
    scores = attention_scores(query_rows, key_rows, key_live)
    summary = jax.nn.logsumexp(scores, -1, keepdims=True)
    attention = jax.nn.softmax(scores, -1).astype(jnp.bfloat16)
    mixed_heads = (
        product("nhqk,nkhe->nqhe", attention, value_rows)
        .astype(jnp.bfloat16)
        .reshape(group_images, SLOTS, local_width)
    )
    attention_out = group_reduce(product("nte,ed->ntd", mixed_heads, output))
    middle = stream + attention_out + vector_table[row_base + 4]
    normed_two = layer_norm(middle, vector_table[row_base + 2], vector_table[row_base + 3]).astype(
        jnp.bfloat16
    )
    normed_two_all = group_gather(normed_two)
    hidden = product("ntd,df->ntf", normed_two_all, expand) + raise_here
    active = jax.nn.gelu(hidden).astype(jnp.bfloat16)
    result = (
        middle
        + group_reduce(product("ntf,fd->ntd", active, shrink))
        + vector_table[row_base + 5]
    )
    return (
        result,
        (
            stream,
            normed_all,
            key_live,
            query_rows,
            key_rows,
            value_rows,
            summary,
            mixed_heads,
            middle,
            normed_two_all,
            hidden,
            active,
        ),
    )


def layer_backward(grad_out, kept_values, layer_index, weights_now, vector_table):
    joint, output, expand, shrink = weights_now
    (
        stream,
        normed_all,
        key_live,
        query_rows,
        key_rows,
        value_rows,
        summary,
        mixed_heads,
        middle,
        normed_two_all,
        hidden,
        active,
    ) = kept_values
    row_base = SLOTS + 4 + 6 * layer_index
    model_width = vector_table.shape[1]
    local_width = joint.shape[2]
    local_hidden = expand.shape[1]
    group_images = normed_all.shape[0]
    model_index = lax.axis_index("mp")
    down_low = group_gather(grad_out.astype(jnp.bfloat16))
    shrink_grad = product("ntf,ntd->fd", active, down_low)
    active_grad = product("ntd,fd->ntf", down_low, shrink)
    unused, gelu_pull = jax.vjp(jax.nn.gelu, hidden)
    hidden_grad = gelu_pull(active_grad)[0]
    raise_grad = jnp.sum(hidden_grad, (0, 1))
    hidden_low = hidden_grad.astype(jnp.bfloat16)
    expand_grad = product("ntd,ntf->df", normed_two_all, hidden_low)
    normed_two_grad = group_reduce(product("ntf,df->ntd", hidden_low, expand))
    unused, second_pull = jax.vjp(
        layer_norm, middle, vector_table[row_base + 2], vector_table[row_base + 3]
    )
    middle_part, gain_two, shift_two = second_pull(normed_two_grad)
    middle_grad = grad_out + middle_part
    up_low = group_gather(middle_grad.astype(jnp.bfloat16))
    output_grad = product("nte,ntd->ed", mixed_heads, up_low)
    mixed_grad = (
        product("ntd,ed->nte", up_low, output).astype(jnp.bfloat16).reshape(query_rows.shape)
    )
    scores = attention_scores(query_rows, key_rows, key_live)
    attention = jnp.exp(scores - summary)
    value_grad = product("nhqk,nqhe->nkhe", attention.astype(jnp.bfloat16), mixed_grad)
    attention_grad = product("nqhe,nkhe->nhqk", mixed_grad, value_rows)
    score_grad = (
        attention
        * (attention_grad - jnp.sum(attention_grad * attention, -1, keepdims=True))
        * 0.125
    ).astype(jnp.bfloat16)
    query_grad = product("nhqk,nkhe->nqhe", score_grad, key_rows)
    key_grad = product("nhqk,nqhe->nkhe", score_grad, query_rows)
    flat_shape = (group_images, SLOTS, local_width)
    shift_local = jnp.stack(
        [
            jnp.sum(query_grad, (0, 1)).reshape(local_width),
            jnp.sum(value_grad, (0, 1)).reshape(local_width),
        ]
    )
    shift_grad = lax.dynamic_update_slice_in_dim(
        jnp.zeros((2, model_width), jnp.float32), shift_local, model_index * local_width, 1
    )
    raise_full = lax.dynamic_update_slice_in_dim(
        jnp.zeros((FF,), jnp.float32), raise_grad, model_index * local_hidden, 0
    )
    joined_grad = jnp.stack(
        [
            query_grad.reshape(flat_shape),
            key_grad.reshape(flat_shape),
            value_grad.reshape(flat_shape),
        ],
        2,
    ).astype(jnp.bfloat16)
    joint_grad = product("ntd,ntke->dke", normed_all, joined_grad)
    normed_grad = group_reduce(product("ntke,dke->ntd", joined_grad, joint))
    unused, first_pull = jax.vjp(
        layer_norm, stream, vector_table[row_base], vector_table[row_base + 1]
    )
    stream_part, gain_one, shift_one = first_pull(normed_grad)
    vector_rows = jnp.stack(
        [
            gain_one,
            shift_one,
            gain_two,
            shift_two,
            jnp.sum(middle_grad, (0, 1)),
            jnp.sum(grad_out, (0, 1)),
        ]
    )
    return (
        middle_grad + stream_part,
        (joint_grad, output_grad, expand_grad, shrink_grad, shift_grad, raise_full, vector_rows),
    )


def on_device(
    patches,
    keep_list,
    keep_count,
    labels,
    patch_weight,
    vector_table,
    head_table,
    joint_weight,
    shift_table,
    output_weight,
    expand_weight,
    raise_table,
    shrink_weight,
    patch_first,
    vector_first,
    head_first,
    joint_first,
    shift_first,
    output_first,
    expand_first,
    raise_first,
    shrink_first,
    patch_second,
    vector_second,
    head_second,
    joint_second,
    shift_second,
    output_second,
    expand_second,
    raise_second,
    shrink_second,
):
    share_images = patches.shape[0]
    model_width = vector_table.shape[1]
    total_images = share_images * lax.axis_size("dp") * lax.axis_size("mp")
    z_masks, y_masks, x_masks, c_masks = bit_masks()
    dp_masks = z_masks + y_masks
    all_masks = dp_masks + x_masks + c_masks
    dp_shift = lax.axis_size("mp").bit_length() - 1
    patch_full = gather_ordered(patch_weight.astype(jnp.bfloat16), all_masks, 0).reshape(-1, model_width)

    def layer_weights(layer_index):
        def over_rows(shard):
            blocks = gather_ordered(shard.astype(jnp.bfloat16), dp_masks, dp_shift)
            return blocks.reshape((-1,) + shard.shape[1:])

        return (
            over_rows(joint_weight[layer_index]),
            over_rows(output_weight[layer_index].T).T,
            over_rows(expand_weight[layer_index]),
            over_rows(shrink_weight[layer_index].T).T,
        )

    weights_of = [layer_weights(layer_index) for layer_index in range(LAYERS)]

    patch_ids = jnp.arange(PATCHES, dtype=jnp.int32)
    kept_slot = patch_ids[None, :] < keep_count[:, None]
    selector = ((keep_list[:, :, None] == patch_ids[None, None, :]) & kept_slot[:, :, None]).astype(
        jnp.float32
    )
    chosen = product("nsp,npc->nsc", selector.astype(jnp.bfloat16), patches).astype(jnp.bfloat16)
    slot_bias = kept_slot[:, :, None].astype(jnp.float32) * vector_table[SLOTS + 1]
    placed = jnp.einsum("nsp,pd->nsd", selector, vector_table[1:SLOTS], precision=highest)
    tokens = product("nsc,cd->nsd", chosen, patch_full) + slot_bias + placed
    leading = jnp.broadcast_to(
        vector_table[SLOTS] + vector_table[0], (share_images, 1, model_width)
    )
    stream = jnp.concatenate([leading, tokens], 1)
    key_share = (jnp.arange(SLOTS, dtype=jnp.int32)[None, :] <= keep_count[:, None]).astype(
        jnp.bfloat16
    )
    saved_layers = []
    for layer_index in range(LAYERS):
        stream, kept_values = layer_forward(
            stream,
            key_share,
            layer_index,
            weights_of[layer_index],
            vector_table,
            shift_table,
            raise_table,
        )
        saved_layers.append(kept_values)
    final_out, final_pull = jax.vjp(
        layer_norm, stream[:, 0], vector_table[SLOTS + 2], vector_table[SLOTS + 3]
    )
    final_low = final_out.astype(jnp.bfloat16)
    head_low = head_table[:model_width].astype(jnp.bfloat16)
    logits = (
        jnp.dot(final_low, head_low, preferred_element_type=jnp.float32) + head_table[model_width]
    )
    target_hot = (labels[:, None] == jnp.arange(CLASSES, dtype=jnp.int32)[None, :]).astype(
        jnp.float32
    )
    loss_local = jnp.sum(jax.nn.logsumexp(logits, -1) - jnp.sum(logits * target_hot, -1))
    logit_grad = (jax.nn.softmax(logits, -1) - target_hot) / total_images
    logit_low = logit_grad.astype(jnp.bfloat16)
    final_every = gather_ordered(final_low, all_masks, 0).reshape(-1, model_width)
    logit_every = gather_ordered(logit_grad, all_masks, 0).reshape(-1, CLASSES)
    head_sum = jnp.concatenate(
        [
            product("nd,nc->dc", final_every, logit_every.astype(jnp.bfloat16)),
            jnp.sum(logit_every, 0)[None],
        ],
        0,
    )
    final_grad = product("nc,dc->nd", logit_low, head_low)
    lead_grad, gain_final, shift_final = final_pull(final_grad)
    back_stream = jnp.zeros_like(stream).at[:, 0].set(lead_grad)
    layer_parts = [None] * LAYERS
    for layer_index in reversed(range(LAYERS)):
        back_stream, layer_parts[layer_index] = layer_backward(
            back_stream,
            saved_layers[layer_index],
            layer_index,
            weights_of[layer_index],
            vector_table,
        )
    stacked = {
        position: jnp.stack([parts[position] for parts in layer_parts]) for position in (4, 5, 6)
    }
    token_grad = back_stream[:, 1:]
    lead_total = jnp.sum(back_stream[:, 0], 0)
    bias_grad = jnp.sum(kept_slot[:, :, None].astype(jnp.float32) * token_grad, (0, 1))
    place_grad = jnp.einsum("nsp,nsd->pd", selector, token_grad, precision=highest)
    patch_grad = product("nsc,nsd->cd", chosen, token_grad.astype(jnp.bfloat16))
    vector_grad = jnp.concatenate(
        [
            lead_total[None],
            place_grad,
            lead_total[None],
            bias_grad[None],
            gain_final[None],
            shift_final[None],
            stacked[6].reshape(6 * LAYERS, model_width),
        ],
        0,
    )
    def scatter_rows(grads):
        blocks = grads.reshape((lax.axis_size("dp"), -1) + grads.shape[1:])
        return reduce_ordered(blocks, dp_masks, dp_shift)

    joint_sum = jnp.stack([scatter_rows(parts[0]) for parts in layer_parts])
    output_sum = jnp.stack([scatter_rows(parts[1].T).T for parts in layer_parts])
    expand_sum = jnp.stack([scatter_rows(parts[2]) for parts in layer_parts])
    shrink_sum = jnp.stack([scatter_rows(parts[3].T).T for parts in layer_parts])
    patch_blocks = patch_grad.reshape(lax.axis_size("dp") * lax.axis_size("mp"), -1, model_width)
    patch_sum = reduce_ordered(patch_blocks, all_masks, 0)
    vector_sum, shift_sum, raise_sum, loss_total = sum_all(
        (vector_grad, stacked[4], stacked[5], loss_local)
    )
    sharded_sq = jnp.zeros((), jnp.float32)
    for member in (patch_sum, joint_sum, output_sum, expand_sum, shrink_sum):
        sharded_sq = sharded_sq + jnp.sum(member * member)
    shared_sq = jnp.zeros((), jnp.float32)
    for member in (vector_sum, head_sum, shift_sum, raise_sum):
        shared_sq = shared_sq + jnp.sum(member * member)
    lead_device = (lax.axis_index("dp") == 0) & (lax.axis_index("mp") == 0)
    total_sq = sum_all(sharded_sq + jnp.where(lead_device, shared_sq, 0.0))
    gradient_norm = jnp.sqrt(total_sq)
    factor = jnp.minimum(1.0, clip_limit / (gradient_norm + norm_eps))
    weights_in = (
        patch_weight,
        vector_table,
        head_table,
        joint_weight,
        shift_table,
        output_weight,
        expand_weight,
        raise_table,
        shrink_weight,
    )
    firsts = (
        patch_first,
        vector_first,
        head_first,
        joint_first,
        shift_first,
        output_first,
        expand_first,
        raise_first,
        shrink_first,
    )
    seconds = (
        patch_second,
        vector_second,
        head_second,
        joint_second,
        shift_second,
        output_second,
        expand_second,
        raise_second,
        shrink_second,
    )
    reduced = (
        patch_sum,
        vector_sum,
        head_sum,
        joint_sum,
        shift_sum,
        output_sum,
        expand_sum,
        raise_sum,
        shrink_sum,
    )
    updated = [
        adamw(weight, moment_one, moment_two, gradient * factor, rate)
        for weight, moment_one, moment_two, gradient, rate in zip(
            weights_in, firsts, seconds, reduced, group_rates
        )
    ]
    return (
        loss_total,
        gradient_norm,
        updated[0][0],
        updated[0][1],
        updated[0][2],
        updated[1][0],
        updated[1][1],
        updated[1][2],
        updated[2][0],
        updated[2][1],
        updated[2][2],
        updated[3][0],
        updated[3][1],
        updated[3][2],
        updated[4][0],
        updated[4][1],
        updated[4][2],
        updated[5][0],
        updated[5][1],
        updated[5][2],
        updated[6][0],
        updated[6][1],
        updated[6][2],
        updated[7][0],
        updated[7][1],
        updated[7][2],
        updated[8][0],
        updated[8][1],
        updated[8][2],
    )


def solution(mesh):
    in_specs = (
        P(("dp", "mp"), None, None),
        P(("dp", "mp"), None),
        P(("dp", "mp")),
        P(("dp", "mp")),
        P(("dp", "mp"), None),
        P(),
        P(),
        P(None, "dp", None, "mp"),
        P(),
        P(None, "mp", "dp"),
        P(None, "dp", "mp"),
        P(),
        P(None, "mp", "dp"),
        P(("dp", "mp"), None),
        P(),
        P(),
        P(None, "dp", None, "mp"),
        P(),
        P(None, "mp", "dp"),
        P(None, "dp", "mp"),
        P(),
        P(None, "mp", "dp"),
        P(("dp", "mp"), None),
        P(),
        P(),
        P(None, "dp", None, "mp"),
        P(),
        P(None, "mp", "dp"),
        P(None, "dp", "mp"),
        P(),
        P(None, "mp", "dp"),
    )
    out_specs = (
        P(),
        P(),
        P(("dp", "mp"), None),
        P(("dp", "mp"), None),
        P(("dp", "mp"), None),
        P(),
        P(),
        P(),
        P(),
        P(),
        P(),
        P(None, "dp", None, "mp"),
        P(None, "dp", None, "mp"),
        P(None, "dp", None, "mp"),
        P(),
        P(),
        P(),
        P(None, "mp", "dp"),
        P(None, "mp", "dp"),
        P(None, "mp", "dp"),
        P(None, "dp", "mp"),
        P(None, "dp", "mp"),
        P(None, "dp", "mp"),
        P(),
        P(),
        P(),
        P(None, "mp", "dp"),
        P(None, "mp", "dp"),
        P(None, "mp", "dp"),
    )
    return jax.shard_map(
        on_device, mesh=mesh, in_specs=in_specs, out_specs=out_specs, check_vma=False
    )
```

```python
import functools

import jax
import jax.numpy as jnp
from jax import lax
from jax.experimental import pallas as pl
from jax.experimental.pallas import tpu as pltpu
from jax.sharding import PartitionSpec as P

HEAD_DIM = 64
CLASSES = 1000
PATCHES = 49
LAYERS = 2
STEP = 10
SLOTS = 50
AXES = ("dp", "mp")

group_rates = (0.01, 0.2, 0.01, 0.01, 0.1, 0.03, 0.01, 0.1, 0.01)
beta_one = 0.9
beta_two = 0.95
adam_eps = 1e-08
decay_rate = 0.1
clip_limit = 0.02
norm_eps = 1e-06
highest = lax.Precision.HIGHEST
low_type = jnp.bfloat16
wide_type = jnp.float32


def swap(values, mask):
    count = lax.axis_size("dp") * lax.axis_size("mp")
    return lax.ppermute(values, AXES, [(n, n ^ mask) for n in range(count)])


def device_index():
    return lax.axis_index("dp") * lax.axis_size("mp") + lax.axis_index("mp")


def bit_masks():
    model, data = lax.axis_size("mp"), lax.axis_size("dp")
    wide = 1 << ((data.bit_length() - 1) // 2)
    z_masks = [m for m in (model * wide << b for b in range(16)) if m < model * data]
    y_masks = [m for m in (model << b for b in range(16)) if m < model * wide]
    x_masks = [m for m in (2 << b for b in range(16)) if m < model]
    return (z_masks, y_masks, x_masks, [1])


def offsets(masks):
    table = [0]
    for mask in masks:
        table = table + [entry ^ mask for entry in table]
    return table


def gather_halves(values, masks):
    blocks = values[None]
    for mask in masks[:-1]:
        blocks = jnp.concatenate([blocks, swap(blocks, mask)], 0)
    return blocks, swap(blocks, masks[-1])


def gather_ordered(values, masks):
    blocks = jnp.concatenate(gather_halves(values, masks), 0)
    inverse = [0] * len(offsets(masks))
    for place, entry in enumerate(offsets(masks)):
        inverse[entry] = place
    places = jnp.array(inverse, jnp.int32)
    order = places.at[jnp.arange(len(inverse)) ^ device_index()].get(mode="promise_in_bounds")
    return blocks.at[order].get(mode="promise_in_bounds")


def reduce_halves(kept, sent, masks):
    total = kept.astype(wide_type) + swap(sent, masks[-1]).astype(wide_type)
    for mask in reversed(masks[:-1]):
        half = total.shape[0] // 2
        total = total[:half] + swap(total[half:].astype(low_type), mask).astype(wide_type)
    return total[0]


def sum_all(values):
    for masks in reversed(bit_masks()):
        for mask in masks:
            values = jax.tree.map(lambda v: v + swap(v, mask), values)
    return values


def group_pieces(values, x_masks):
    pieces = [values]
    for mask in x_masks:
        pieces = pieces + [swap(piece, mask) for piece in pieces]
    return pieces + [swap(piece, 1) for piece in pieces]


def group_sum(partials, x_masks):
    sums = [kept + swap(sent, 1).astype(wide_type) for kept, sent in partials]
    for mask in reversed(x_masks):
        half = len(sums) // 2
        sums = [
            near + swap(far.astype(low_type), mask).astype(wide_type)
            for near, far in zip(sums[:half], sums[half:])
        ]
    return sums[0]


def dot_nn(left, right):
    return jnp.dot(left, right, preferred_element_type=wide_type)


def dot_nt(left, right):
    return lax.dot_general(left, right, (((1,), (1,)), ((), ())), preferred_element_type=wide_type)


def dot_tn(left, right):
    return lax.dot_general(left, right, (((0,), (0,)), ((), ())), preferred_element_type=wide_type)


def normalise(values):
    centre = values - jnp.mean(values, -1, keepdims=True)
    spread = jnp.mean(centre * centre, -1, keepdims=True)
    scale = lax.rsqrt(spread + norm_eps)
    return centre * scale, scale


def normalise_back(hat, scale, gain, grad):
    lifted = grad * gain
    return scale * (
        lifted
        - jnp.mean(lifted, -1, keepdims=True)
        - hat * jnp.mean(lifted * hat, -1, keepdims=True)
    )


def start_weights(tab_ref, halves, w_ref, sems):
    count, width, rows, columns = halves[0].shape
    for side, half in enumerate(halves):

        def step(r, carry):
            row = pl.multiple_of(tab_ref[0, side * count + r] * rows, rows)
            column = pl.multiple_of(tab_ref[1, side * count + r] * columns, columns)
            for k in range(width):
                pltpu.make_async_copy(
                    half.at[r, k],
                    w_ref.at[k, pl.ds(row, rows), pl.ds(column, columns)],
                    sems.at[k],
                ).start()
            return carry

        lax.fori_loop(0, count, step, 0)


def wait_weights(w_ref, sems, k):
    pltpu.make_async_copy(w_ref.at[k], w_ref.at[k], sems.at[k]).wait()


def store_grads(tab_ref, g_ref, halves, sem, k):
    count, width, rows, columns = halves[0].shape
    for side, half in enumerate(halves):

        def step(r, carry):
            row = pl.multiple_of(tab_ref[0, side * count + r] * rows, rows)
            column = pl.multiple_of(tab_ref[1, side * count + r] * columns, columns)
            pltpu.make_async_copy(
                g_ref.at[k, pl.ds(row, rows), pl.ds(column, columns)], half.at[r, k], sem.at[k]
            ).start()
            return carry

        lax.fori_loop(0, count, step, 0)


def lane_masks():
    lane = lax.broadcasted_iota(jnp.int32, (1, 2 * HEAD_DIM), 1)
    return (lane < HEAD_DIM, lane >= HEAD_DIM)


def softmax_rows(query, keys, bias):
    scores = dot_nt(query, keys) * 0.125 + bias
    powers = jnp.exp(scores - jnp.max(scores, -1, keepdims=True))
    return powers / jnp.sum(powers, -1, keepdims=True)


def attention_forward_kernel(
    tab_ref, stream_ref, vec_ref, shift_ref, bias_ref, half_a, half_b,
    middle_ref, second_ref, first_ref, qkv_ref, mixed_ref, w_ref, sems,
):
    start_weights(tab_ref, (half_a, half_b), w_ref, sems)
    width = stream_ref.shape[1]
    hat, scale = normalise(stream_ref[...])
    first_ref[...] = (hat * vec_ref[0:1, :] + vec_ref[1:2, :]).astype(low_type)
    for k in range(3):
        wait_weights(w_ref, sems, k)
        for c in range(0, width, 256):
            part = dot_nn(first_ref[...], w_ref[k, :, c : c + 256]) + shift_ref[k : k + 1, c : c + 256]
            qkv_ref[k, :, c : c + 256] = part.astype(low_type)

    def pair(h, carry):
        at = pl.ds(pl.multiple_of(h * 128, 128), 128)
        query, keys, values = qkv_ref[0, :, at], qkv_ref[1, :, at], qkv_ref[2, :, at]
        outs = []
        for lanes in lane_masks():
            own = jnp.where(lanes, query, jnp.zeros_like(query))
            probs = softmax_rows(own, keys, bias_ref[...]).astype(low_type)
            outs.append(dot_nn(probs, values))
        mixed_ref[:, at] = jnp.where(lane_masks()[0], outs[0], outs[1]).astype(low_type)
        return carry

    lax.fori_loop(0, width // 128, pair, 0)
    wait_weights(w_ref, sems, 3)
    for c in range(0, width, 256):
        middle_ref[:, c : c + 256] = (
            stream_ref[:, c : c + 256]
            + dot_nt(mixed_ref[...], w_ref[3, c : c + 256, :])
            + vec_ref[4:5, c : c + 256]
        )
    hat, scale = normalise(middle_ref[...])
    second_ref[...] = (hat * vec_ref[2:3, :] + vec_ref[3:4, :]).astype(low_type)


def attention_chain_kernel(
    tab_ref, upper_ref, pull_ref, middle_ref, stream_ref, vec_ref, bias_ref, qkv_ref, half_a, half_b,
    below_ref, below_low_ref, up_ref, joined_ref, rows_ref, w_ref, sems, mixed_grad_ref, mid_grad_ref, norm_grad_ref,
):
    start_weights(tab_ref, (half_a, half_b), w_ref, sems)
    width = stream_ref.shape[1]
    upper = upper_ref[...]
    rows_ref[5:6, :] = jnp.sum(upper, 0, keepdims=True)
    pull = pull_ref[...]
    hat, scale = normalise(middle_ref[...])
    rows_ref[2:3, :] = jnp.sum(pull * hat, 0, keepdims=True)
    rows_ref[3:4, :] = jnp.sum(pull, 0, keepdims=True)
    mid_grad = upper + normalise_back(hat, scale, vec_ref[2:3, :], pull)
    mid_grad_ref[...] = mid_grad
    rows_ref[4:5, :] = jnp.sum(mid_grad, 0, keepdims=True)
    up_ref[...] = mid_grad.astype(low_type)
    wait_weights(w_ref, sems, 3)
    for c in range(0, width, 256):
        mixed_grad_ref[:, c : c + 256] = dot_nn(up_ref[...], w_ref[3, :, c : c + 256]).astype(low_type)

    def pair(h, carry):
        at = pl.ds(pl.multiple_of(h * 128, 128), 128)
        query, keys, values = qkv_ref[0, :, at], qkv_ref[1, :, at], qkv_ref[2, :, at]
        grads = mixed_grad_ref[:, at]
        outs = []
        for lanes in lane_masks():
            own = jnp.where(lanes, query, jnp.zeros_like(query))
            own_grad = jnp.where(lanes, grads, jnp.zeros_like(grads))
            probs = softmax_rows(own, keys, bias_ref[...])
            value_grad = dot_tn(probs.astype(low_type), grads)
            prob_grad = dot_nt(own_grad, values)
            weighted = probs * prob_grad
            score_grad = (
                (weighted - probs * jnp.sum(weighted, -1, keepdims=True)) * 0.125
            ).astype(low_type)
            outs.append((dot_nn(score_grad, keys), dot_tn(score_grad, query), value_grad))
        for k in range(3):
            part = jnp.where(lane_masks()[0], outs[0][k], outs[1][k])
            joined_ref[k, :, at] = part.astype(low_type)
            if k != 1:
                rows_ref[6 + k // 2 : 7 + k // 2, at] = jnp.sum(part, 0, keepdims=True)
        return carry

    lax.fori_loop(0, width // 128, pair, 0)
    for k in range(3):
        wait_weights(w_ref, sems, k)
    for c in range(0, width, 256):
        norm_grad_ref[:, c : c + 256] = (
            dot_nt(joined_ref[0], w_ref[0, c : c + 256, :])
            + dot_nt(joined_ref[1], w_ref[1, c : c + 256, :])
            + dot_nt(joined_ref[2], w_ref[2, c : c + 256, :])
        )
    hat, scale = normalise(stream_ref[...])
    norm_grad = norm_grad_ref[...]
    rows_ref[0:1, :] = jnp.sum(norm_grad * hat, 0, keepdims=True)
    rows_ref[1:2, :] = jnp.sum(norm_grad, 0, keepdims=True)
    below = mid_grad_ref[...] + normalise_back(hat, scale, vec_ref[0:1, :], norm_grad)
    below_ref[...] = below
    below_low_ref[...] = below.astype(low_type)


def attention_weights_kernel(
    tab_ref, first_ref, joined_ref, up_ref, mixed_ref, half_a, half_b, g_ref, sems
):
    width = first_ref.shape[1]
    for k in range(4):
        for c in range(0, width, 256):
            if k < 3:
                part = dot_tn(first_ref[...], joined_ref[k, :, c : c + 256])
            else:
                part = dot_tn(up_ref[...], mixed_ref[:, c : c + 256])
            g_ref[k, :, c : c + 256] = part.astype(low_type)
        store_grads(tab_ref, g_ref, (half_a, half_b), sems, k)
    for k in range(4):
        wait_weights(g_ref, sems, k)


gelu_scale = 0.7978845608028654
gelu_cube = 0.044715


def hidden_forward_kernel(
    tab_ref, here_ref, there_ref, raise_ref, half_a, half_b, kept_ref, sent_ref, w_ref, active_ref, sems
):
    start_weights(tab_ref, (half_a, half_b), w_ref, sems)
    rows, width = here_ref.shape
    hidden_width = active_ref.shape[1]
    wait_weights(w_ref, sems, 0)
    for side, source in enumerate((here_ref, there_ref)):
        for c in range(0, hidden_width, 256):
            hidden = dot_nn(source[...], w_ref[0, :, c : c + 256]) + raise_ref[0:1, c : c + 256]
            bent = jnp.tanh(gelu_scale * (hidden + gelu_cube * (hidden * hidden * hidden)))
            active_ref[side * rows : (side + 1) * rows, c : c + 256] = (
                hidden * (0.5 * (1.0 + bent))
            ).astype(low_type)
    wait_weights(w_ref, sems, 1)
    for c in range(0, width, 256):
        kept_ref[:, c : c + 256] = dot_nt(active_ref[0:rows, :], w_ref[1, c : c + 256, :])
        sent_ref[:, c : c + 256] = dot_nt(active_ref[rows : 2 * rows, :], w_ref[1, c : c + 256, :]).astype(low_type)


def hidden_chain_kernel(
    tab_ref, here_ref, there_ref, down_here_ref, down_there_ref, raise_ref, half_a, half_b,
    kept_ref, sent_ref, active_ref, grad_ref, raise_grad_ref, w_ref, sems,
):
    start_weights(tab_ref, (half_a, half_b), w_ref, sems)
    rows, width = here_ref.shape
    hidden_width = active_ref.shape[1]
    wait_weights(w_ref, sems, 0)
    wait_weights(w_ref, sems, 1)
    pairs = ((here_ref, down_here_ref), (there_ref, down_there_ref))
    for c in range(0, hidden_width, 256):
        total = jnp.zeros((1, 256), wide_type)
        for side, (source, down) in enumerate(pairs):
            hidden = dot_nn(source[...], w_ref[0, :, c : c + 256]) + raise_ref[0:1, c : c + 256]
            pulled = dot_nn(down[...], w_ref[1, :, c : c + 256])
            square = hidden * hidden
            bent = jnp.tanh(gelu_scale * (hidden + gelu_cube * (square * hidden)))
            share = 0.5 * (1.0 + bent)
            active_ref[side * rows : (side + 1) * rows, c : c + 256] = (hidden * share).astype(low_type)
            slope = share + (0.5 * hidden) * (1.0 - bent * bent) * (
                gelu_scale + (3.0 * gelu_scale * gelu_cube) * square
            )
            grad = pulled * slope
            grad_ref[side * rows : (side + 1) * rows, c : c + 256] = grad.astype(low_type)
            total = total + jnp.sum(grad, 0, keepdims=True)
        raise_grad_ref[0:1, c : c + 256] = total
    for c in range(0, width, 256):
        kept_ref[:, c : c + 256] = dot_nt(grad_ref[0:rows, :], w_ref[0, c : c + 256, :])
        sent_ref[:, c : c + 256] = dot_nt(grad_ref[rows : 2 * rows, :], w_ref[0, c : c + 256, :]).astype(low_type)


def hidden_weights_kernel(count, tab_ref, *refs):
    groups = [refs[6 * g : 6 * g + 6] for g in range(count)]
    half_a, half_b, g_ref, inputs_ref, down_ref, active_ref, grad_ref, sems = refs[6 * count :]
    rows, width = groups[0][0].shape
    hidden_width = active_ref.shape[1]
    for g, (here, there, down_here, down_there, active, grad) in enumerate(groups):
        at = 2 * g * rows
        inputs_ref[at : at + rows, :] = here[...]
        inputs_ref[at + rows : at + 2 * rows, :] = there[...]
        down_ref[at : at + rows, :] = down_here[...]
        down_ref[at + rows : at + 2 * rows, :] = down_there[...]
        active_ref[at : at + 2 * rows, :] = active[...]
        grad_ref[at : at + 2 * rows, :] = grad[...]
    for k, (left, right) in enumerate(((inputs_ref, grad_ref), (down_ref, active_ref))):
        for c in range(0, hidden_width, 256):
            g_ref[k, :, c : c + 256] = dot_tn(left[...], right[:, c : c + 256]).astype(low_type)
        store_grads(tab_ref, g_ref, (half_a, half_b), sems, k)
    for k in range(2):
        wait_weights(g_ref, sems, k)


def head_kernel(final_ref, logit_ref, out_ref):
    width = final_ref.shape[1]
    logit = logit_ref[...]
    out_ref[0:width, :] = dot_tn(final_ref[...], logit.astype(low_type))
    out_ref[width : width + 1, :] = jnp.sum(logit, 0, keepdims=True)


smem = pl.BlockSpec(memory_space=pltpu.SMEM)
vmem = pl.BlockSpec(memory_space=pltpu.VMEM)
anywhere = pl.BlockSpec(memory_space=pl.ANY)


def call(kernel, in_specs, outs, scratch, flops, moved):
    return pl.pallas_call(
        kernel,
        out_shape=tuple(jax.ShapeDtypeStruct(shape, kind) for shape, kind, spec in outs),
        in_specs=in_specs,
        out_specs=tuple(spec for shape, kind, spec in outs),
        scratch_shapes=scratch,
        compiler_params=pltpu.CompilerParams(vmem_limit_bytes=48 * 1024 * 1024),
        cost_estimate=pl.CostEstimate(flops=flops, bytes_accessed=moved, transcendentals=0),
    )


def attention_forward(tab, stream, vec, shift, bias, halves):
    rows, width = stream.shape
    return call(
        attention_forward_kernel,
        [smem] + [vmem] * 4 + [anywhere] * 2,
        [
            ((rows, width), wide_type, vmem),
            ((rows, width), low_type, vmem),
            ((rows, width), low_type, vmem),
            ((3, rows, width), low_type, vmem),
            ((rows, width), low_type, vmem),
        ],
        [pltpu.VMEM((4, width, width), low_type), pltpu.SemaphoreType.DMA((4,))],
        20 * rows * width * width,
        20 * width * width,
    )(tab, stream, vec, shift, bias, *halves)


def attention_chain(tab, upper, pull, middle, stream, vec, bias, qkv, halves):
    rows, width = stream.shape
    return call(
        attention_chain_kernel,
        [smem] + [vmem] * 7 + [anywhere] * 2,
        [
            ((rows, width), wide_type, vmem),
            ((rows, width), low_type, vmem),
            ((rows, width), low_type, vmem),
            ((3, rows, width), low_type, vmem),
            ((8, width), wide_type, vmem),
        ],
        [
            pltpu.VMEM((4, width, width), low_type),
            pltpu.SemaphoreType.DMA((4,)),
            pltpu.VMEM((rows, width), low_type),
            pltpu.VMEM((rows, width), wide_type),
            pltpu.VMEM((rows, width), wide_type),
        ],
        30 * rows * width * width,
        30 * width * width,
    )(tab, upper, pull, middle, stream, vec, bias, qkv, *halves)


def attention_weights(tab, first, joined, up, mixed, half_shape):
    rows, width = first.shape
    return call(
        attention_weights_kernel,
        [smem] + [vmem] * 4,
        [(half_shape, low_type, anywhere)] * 2,
        [pltpu.VMEM((4, width, width), low_type), pltpu.SemaphoreType.DMA((4,))],
        16 * rows * width * width,
        16 * width * width,
    )(tab, first, joined, up, mixed)


def hidden_forward(tab, here, there, raise_row, halves):
    rows, width = here.shape
    hidden_width = raise_row.shape[1]
    return call(
        hidden_forward_kernel,
        [smem] + [vmem] * 3 + [anywhere] * 2,
        [((rows, width), wide_type, vmem), ((rows, width), low_type, vmem)],
        [
            pltpu.VMEM((2, width, hidden_width), low_type),
            pltpu.VMEM((2 * rows, hidden_width), low_type),
            pltpu.SemaphoreType.DMA((2,)),
        ],
        16 * rows * width * hidden_width,
        10 * width * hidden_width,
    )(tab, here, there, raise_row, *halves)


def hidden_chain(tab, here, there, down_here, down_there, raise_row, halves):
    rows, width = here.shape
    hidden_width = raise_row.shape[1]
    return call(
        hidden_chain_kernel,
        [smem] + [vmem] * 5 + [anywhere] * 2,
        [
            ((rows, width), wide_type, vmem),
            ((rows, width), low_type, vmem),
            ((2 * rows, hidden_width), low_type, vmem),
            ((2 * rows, hidden_width), low_type, vmem),
            ((1, hidden_width), wide_type, vmem),
        ],
        [pltpu.VMEM((2, width, hidden_width), low_type), pltpu.SemaphoreType.DMA((2,))],
        20 * rows * width * hidden_width,
        20 * width * hidden_width,
    )(tab, here, there, down_here, down_there, raise_row, *halves)


def hidden_weights(tab, groups, half_shape):
    rows, width = groups[0][0].shape
    hidden_width = groups[0][4].shape[1]
    count = len(groups)
    return call(
        functools.partial(hidden_weights_kernel, count),
        [smem] + [vmem] * (6 * count),
        [(half_shape, low_type, anywhere)] * 2,
        [
            pltpu.VMEM((2, width, hidden_width), low_type),
            pltpu.VMEM((2 * count * rows, width), low_type),
            pltpu.VMEM((2 * count * rows, width), low_type),
            pltpu.VMEM((2 * count * rows, hidden_width), low_type),
            pltpu.VMEM((2 * count * rows, hidden_width), low_type),
            pltpu.SemaphoreType.DMA((2,)),
        ],
        16 * count * rows * width * hidden_width,
        20 * width * hidden_width,
    )(tab, *[member for group in groups for member in group])


def head_gradient(final_every, logit_every):
    width = final_every.shape[1]
    return call(
        head_kernel,
        [vmem] * 2,
        [((width + 1, logit_every.shape[1]), wide_type, vmem)],
        [],
        1 << 28,
        1 << 23,
    )(final_every, logit_every)[0]


def layer_norm(values, gain_row, shift_row):
    centre = values - jnp.mean(values, -1, keepdims=True)
    spread = jnp.mean(centre * centre, -1, keepdims=True)
    return centre * lax.rsqrt(spread + norm_eps) * gain_row + shift_row


def product(form, left, right):
    return jnp.einsum(form, left, right, preferred_element_type=wide_type)


def adamw(weight, moment_one, moment_two, gradient, rate):
    first_new = beta_one * moment_one + (1.0 - beta_one) * gradient
    second_new = beta_two * moment_two + (1.0 - beta_two) * gradient * gradient
    corrected = first_new / (1.0 - beta_one**STEP)
    scaled = second_new / (1.0 - beta_two**STEP)
    weight_new = weight - rate * (corrected / (jnp.sqrt(scaled) + adam_eps) + decay_rate * weight)
    return (weight_new, first_new, second_new)


def on_device(
    patches,
    keep_list,
    keep_count,
    labels,
    patch_weight,
    vector_table,
    head_table,
    joint_weight,
    shift_table,
    output_weight,
    expand_weight,
    raise_table,
    shrink_weight,
    *moments,
):
    share_images = patches.shape[0]
    model_width = vector_table.shape[1]
    data, model = lax.axis_size("dp"), lax.axis_size("mp")
    devices = data * model
    total_images = share_images * devices
    real_rows = share_images * SLOTS
    rows = -(-real_rows // 16) * 16
    z_masks, y_masks, x_masks, c_masks = bit_masks()
    dp_masks = z_masks + y_masks
    all_masks = dp_masks + x_masks + c_masks
    me = device_index()
    model_index = lax.axis_index("mp")
    local_hidden = expand_weight.shape[2]

    every = jnp.array(offsets(all_masks), jnp.int32) ^ me
    every_tab = jnp.stack([every // model, every % model])
    column = jnp.array(offsets(dp_masks), jnp.int32) ^ me
    column_tab = jnp.stack([column // model, jnp.zeros_like(column)])

    patch_full = gather_ordered(patch_weight.astype(low_type), all_masks).reshape(-1, model_width)
    attention_halves, hidden_halves = [], []
    for layer in range(LAYERS):
        pack = jnp.concatenate(
            [joint_weight[layer].transpose(1, 0, 2), output_weight[layer].T[None]], 0
        ).astype(low_type)
        attention_halves.append(gather_halves(pack, all_masks))
        pack = jnp.stack([expand_weight[layer], shrink_weight[layer].T]).astype(low_type)
        hidden_halves.append(gather_halves(pack, dp_masks))

    patch_ids = jnp.arange(PATCHES, dtype=jnp.int32)
    kept_slot = patch_ids[None, :] < keep_count[:, None]
    selector = ((keep_list[:, :, None] == patch_ids[None, None, :]) & kept_slot[:, :, None]).astype(
        wide_type
    )
    selector = jnp.pad(selector, ((0, 0), (1, 0), (0, 0)))
    chosen = product("nsp,npc->nsc", selector.astype(low_type), patches).astype(low_type)
    chosen = jnp.pad(chosen.reshape(real_rows, -1), ((0, rows - real_rows), (0, 0)))
    slot_kept = jnp.pad(kept_slot, ((0, 0), (1, 0))).astype(wide_type)
    slot_first = jnp.zeros((share_images, SLOTS), wide_type).at[:, 0].set(1.0)
    spread = jnp.concatenate(
        [selector, slot_kept[:, :, None], slot_first[:, :, None]], 2
    ).reshape(real_rows, PATCHES + 2)
    spread = jnp.pad(spread, ((0, rows - real_rows), (0, 0)))
    sources = jnp.concatenate(
        [
            vector_table[1:SLOTS],
            vector_table[SLOTS + 1 : SLOTS + 2],
            vector_table[SLOTS : SLOTS + 1] + vector_table[0:1],
        ],
        0,
    )
    stream = product("sc,cd->sd", chosen, patch_full) + jnp.dot(spread, sources, precision=highest)

    row_ids = jnp.arange(rows, dtype=jnp.int32)
    image_ids, slot_ids = row_ids // SLOTS, row_ids % SLOTS
    row_count = jnp.pad(jnp.repeat(keep_count, SLOTS), (0, rows - real_rows), constant_values=SLOTS)
    live = (image_ids[:, None] == image_ids[None, :]) & (slot_ids <= row_count)[None, :]
    bias = jnp.where(live, 0.0, -1e30).astype(wide_type)

    saved = []
    for layer in range(LAYERS):
        base = SLOTS + 4 + 6 * layer
        vec = vector_table[base : base + 6]
        shift = jnp.stack(
            [shift_table[layer, 0], jnp.zeros((model_width,), wide_type), shift_table[layer, 1]]
        )
        raise_row = lax.dynamic_slice_in_dim(
            raise_table[layer], model_index * local_hidden, local_hidden, 0
        )[None]
        middle, second, first, qkv, mixed = attention_forward(
            every_tab, stream, vec, shift, bias, attention_halves[layer]
        )
        pieces = group_pieces(second, x_masks)
        steps = len(pieces) // 2
        partials = [
            hidden_forward(column_tab, pieces[k], pieces[steps + k], raise_row, hidden_halves[layer])
            for k in range(steps)
        ]
        saved.append((stream, middle, first, qkv, mixed, pieces, vec, raise_row))
        stream = middle + group_sum(partials, x_masks) + vec[5:6]

    lead_rows = stream[:real_rows].reshape(share_images, SLOTS, model_width)[:, 0]
    final_out, final_pull = jax.vjp(
        layer_norm, lead_rows, vector_table[SLOTS + 2], vector_table[SLOTS + 3]
    )
    final_low = final_out.astype(low_type)
    head_low = head_table[:model_width].astype(low_type)
    logits = product("nd,dc->nc", final_low, head_low) + head_table[model_width]
    target_hot = (labels[:, None] == jnp.arange(CLASSES, dtype=jnp.int32)[None, :]).astype(
        wide_type
    )
    loss_local = jnp.sum(jax.nn.logsumexp(logits, -1) - jnp.sum(logits * target_hot, -1))
    logit_grad = (jax.nn.softmax(logits, -1) - target_hot) / total_images
    logit_low = logit_grad.astype(low_type)
    final_every = gather_ordered(final_low, all_masks).reshape(-1, model_width)
    logit_every = gather_ordered(logit_grad, all_masks).reshape(-1, CLASSES)
    head_sum = head_gradient(final_every, logit_every)
    final_grad = product("nc,dc->nd", logit_low, head_low)
    lead_grad, gain_final, shift_final = final_pull(final_grad)
    upper = jnp.zeros((share_images, SLOTS, model_width), wide_type).at[:, 0].set(lead_grad)
    upper = jnp.pad(upper.reshape(real_rows, model_width), ((0, rows - real_rows), (0, 0)))
    upper_low = upper.astype(low_type)

    vector_rows, shift_rows, raise_rows = [None] * LAYERS, [None] * LAYERS, [None] * LAYERS
    attention_sums, hidden_sums = [None] * LAYERS, [None] * LAYERS
    for layer in reversed(range(LAYERS)):
        stream_in, middle, first, qkv, mixed, pieces, vec, raise_row = saved[layer]
        downs = group_pieces(upper_low, x_masks)
        steps = len(pieces) // 2
        partials, groups, raise_sum = [], [], 0.0
        for k in range(steps):
            kept, sent, active, grad, raise_part = hidden_chain(
                column_tab,
                pieces[k],
                pieces[steps + k],
                downs[k],
                downs[steps + k],
                raise_row,
                hidden_halves[layer],
            )
            partials.append((kept, sent))
            groups.append((pieces[k], pieces[steps + k], downs[k], downs[steps + k], active, grad))
            raise_sum = raise_sum + raise_part
        hidden_grads = hidden_weights(column_tab, groups, hidden_halves[layer][0].shape)
        hidden_sums[layer] = reduce_halves(*hidden_grads, dp_masks)
        pull = group_sum(partials, x_masks)
        upper, upper_low, up, joined, tail = attention_chain(
            every_tab, upper, pull, middle, stream_in, vec, bias, qkv, attention_halves[layer]
        )
        attention_grads = attention_weights(
            every_tab, first, joined, up, mixed, attention_halves[layer][0].shape
        )
        attention_sums[layer] = reduce_halves(*attention_grads, all_masks)
        vector_rows[layer], shift_rows[layer] = tail[:6], tail[6:]
        raise_rows[layer] = lax.dynamic_update_slice_in_dim(
            jnp.zeros((model, local_hidden), wide_type), raise_sum, model_index, 0
        ).reshape(-1, model_width)

    place = lax.dot_general(
        spread, upper, (((0,), (0,)), ((), ())), precision=highest, preferred_element_type=wide_type
    )
    patch_grad = lax.dot_general(
        chosen, upper_low, (((0,), (0,)), ((), ())), preferred_element_type=wide_type
    ).astype(low_type)
    patch_blocks = patch_grad.reshape(devices, -1, model_width)
    patch_blocks = patch_blocks.at[every].get(mode="promise_in_bounds")
    half = devices // 2
    patch_sum = reduce_halves(patch_blocks[:half], patch_blocks[half:], all_masks)

    small = jnp.concatenate(
        [
            place[PATCHES + 1 :],
            place[:PATCHES],
            place[PATCHES + 1 :],
            place[PATCHES : PATCHES + 1],
            gain_final[None],
            shift_final[None],
        ]
        + vector_rows
        + shift_rows
        + raise_rows
        + [jnp.zeros((1, model_width), wide_type).at[0, 0].set(loss_local)],
        0,
    )
    small = sum_all(small)
    vector_count = vector_table.shape[0]
    vector_sum = small[:vector_count]
    shift_sum = small[vector_count : vector_count + 2 * LAYERS].reshape(shift_table.shape)
    raise_sum = small[vector_count + 2 * LAYERS : -1].reshape(raise_table.shape)
    loss_total = small[-1, 0]
    joint_sum = jnp.stack([total[:3].transpose(1, 0, 2) for total in attention_sums])
    output_sum = jnp.stack([total[3].T for total in attention_sums])
    expand_sum = jnp.stack([total[0] for total in hidden_sums])
    shrink_sum = jnp.stack([total[1].T for total in hidden_sums])

    sharded_sq = jnp.zeros((), wide_type)
    for member in [patch_sum] + attention_sums + hidden_sums:
        sharded_sq = sharded_sq + jnp.sum(member * member)
    shared_sq = jnp.sum(head_sum * head_sum) + jnp.sum(small[:-1] * small[:-1])
    total_sq = sum_all(sharded_sq) + shared_sq
    gradient_norm = jnp.sqrt(total_sq)
    factor = jnp.minimum(1.0, clip_limit / (gradient_norm + norm_eps))
    weights_in = (
        patch_weight,
        vector_table,
        head_table,
        joint_weight,
        shift_table,
        output_weight,
        expand_weight,
        raise_table,
        shrink_weight,
    )
    reduced = (
        patch_sum,
        vector_sum,
        head_sum,
        joint_sum,
        shift_sum,
        output_sum,
        expand_sum,
        raise_sum,
        shrink_sum,
    )
    outputs = [loss_total, gradient_norm]
    for weight, moment_one, moment_two, gradient, rate in zip(
        weights_in, moments[:9], moments[9:], reduced, group_rates
    ):
        outputs.extend(adamw(weight, moment_one, moment_two, gradient * factor, rate))
    return tuple(outputs)


def solution(mesh):
    params = (
        P(("dp", "mp"), None),
        P(),
        P(),
        P(None, "dp", None, "mp"),
        P(),
        P(None, "mp", "dp"),
        P(None, "dp", "mp"),
        P(),
        P(None, "mp", "dp"),
    )
    in_specs = (
        P(("dp", "mp"), None, None),
        P(("dp", "mp"), None),
        P(("dp", "mp")),
        P(("dp", "mp")),
    ) + 3 * params
    out_specs = (P(), P()) + tuple(spec for spec in params for _ in range(3))
    return jax.shard_map(
        on_device, mesh=mesh, in_specs=in_specs, out_specs=out_specs, check_vma=False
    )
```

```python
import functools

import jax
import jax.numpy as jnp
from jax import lax
from jax.experimental import pallas as pl
from jax.experimental.pallas import tpu as pltpu
from jax.sharding import PartitionSpec as P

HEAD_DIM = 64
CLASSES = 1000
PATCHES = 49
LAYERS = 2
STEP = 10
SLOTS = 50
AXES = ("dp", "mp")

group_rates = (0.01, 0.2, 0.01, 0.01, 0.1, 0.03, 0.01, 0.1, 0.01)
beta_one = 0.9
beta_two = 0.95
adam_eps = 1e-08
decay_rate = 0.1
clip_limit = 0.02
norm_eps = 1e-06
highest = lax.Precision.HIGHEST
low_type = jnp.bfloat16
wide_type = jnp.float32


def move(values, pairs):
    return lax.ppermute(values, AXES, pairs)


def across(mask):
    return [(n, n ^ mask) for n in range(lax.axis_size("dp") * lax.axis_size("mp"))]


def swap(values, mask):
    return move(values, across(mask))


def device_index():
    return lax.axis_index("dp") * lax.axis_size("mp") + lax.axis_index("mp")


def sizes():
    model, data = lax.axis_size("mp"), lax.axis_size("dp")
    wide = 1 << ((data.bit_length() - 1) // 2)
    return data // wide, wide, model // 2, wide * model


def bit_masks():
    deep, wide, across_x, stride = sizes()
    model = lax.axis_size("mp")
    z_masks = [stride << b for b in range(deep.bit_length() - 1)]
    y_masks = [model << b for b in range(wide.bit_length() - 1)]
    x_masks = [2 << b for b in range(across_x.bit_length() - 1)]
    return (z_masks, y_masks, x_masks, [1])


def offsets(masks):
    table = [0]
    for mask in masks:
        table = table + [entry ^ mask for entry in table]
    return table


def origins(masks):
    deep, wide, across_x, stride = sizes()
    me = device_index()
    places = [(flip, t) for flip in offsets(masks) for t in range(deep)]
    flips = jnp.array([flip for flip, t in places], jnp.int32)
    turns = jnp.array([t for flip, t in places], jnp.int32)
    return (me // stride + turns) % deep * stride + ((me % stride) ^ flips)


def along_z(shift, first, last):
    deep, wide, across_x, stride = sizes()
    return [
        (z * stride + n, (z + shift) * stride + n) for z in range(first, last + 1) for n in range(stride)
    ]


def gather_z(values):
    deep, wide, across_x, stride = sizes()
    z = device_index() // stride
    up, down, ups, downs = values, values, [], []
    for k in range(1, deep):
        up, down = yield [
            (up, along_z(1, k - 1, deep - 2)),
            (down, along_z(-1, 1, deep - k)),
        ]
        ups.append(up)
        downs.append(down)
    return jnp.stack(
        [values] + [jnp.where(z + t < deep, downs[t - 1], ups[deep - t - 1]) for t in range(1, deep)]
    )


def gather_flips(blocks, masks):
    for mask in masks[:-1]:
        (arrived,) = yield [(blocks, across(mask))]
        blocks = jnp.concatenate([blocks, arrived], 0)
    (arrived,) = yield [(blocks, across(masks[-1]))]
    return blocks, arrived


def gather_quarters(blocks, masks):
    for mask in masks[:-2]:
        (arrived,) = yield [(blocks, across(mask))]
        blocks = jnp.concatenate([blocks, arrived], 0)
    arrived, beside = yield [(blocks, across(masks[-2])), (blocks, across(masks[-1]))]
    (last,) = yield [(arrived, across(masks[-1]))]
    return blocks, arrived, beside, last


def gather_all(values, masks):
    blocks = yield from gather_z(values)
    return (yield from gather_flips(blocks, masks))


def reduce_quarters(parts, masks):
    kept, sent, kept_beside, sent_beside = parts
    beside, last = yield [(kept_beside, across(masks[-1])), (sent_beside, across(masks[-1]))]
    sent = (sent.astype(wide_type) + last.astype(wide_type)).astype(low_type)
    (arrived,) = yield [(sent, across(masks[-2]))]
    terms = [kept, beside, arrived]
    for mask in reversed(masks[:-2]):
        half = terms[0].shape[0] // 2
        sent = sum(term[half:].astype(wide_type) for term in terms).astype(low_type)
        kept = sum(term[:half].astype(wide_type) for term in terms)
        (arrived,) = yield [(sent, across(mask))]
        terms = [kept, arrived]
    return sum(term.astype(wide_type) for term in terms)


def reduce_z(blocks):
    deep = blocks.shape[0]
    up = down = None
    for k in range(deep - 1, 0, -1):
        rising, falling = blocks[k], blocks[deep - k]
        if up is not None:
            rising, falling = rising + up.astype(wide_type), falling + down.astype(wide_type)
        up, down = yield [
            (rising.astype(low_type), along_z(1, 0, deep - 1 - k)),
            (falling.astype(low_type), along_z(-1, k, deep - 1)),
        ]
    return blocks[0] + up.astype(wide_type) + down.astype(wide_type)


def reduce_all(parts, masks):
    blocks = yield from reduce_quarters(parts, masks)
    return (yield from reduce_z(blocks))


class Transfer:
    def __init__(self, steps):
        self.steps = steps
        self.wanted = next(steps)
        self.result = None

    def send(self):
        return [move(*item) for item in self.wanted]

    def receive(self, arrived):
        try:
            self.wanted = self.steps.send(arrived)
        except StopIteration as end:
            self.wanted, self.result = None, end.value

    def finish(self):
        while self.wanted is not None:
            self.receive(self.send())
        return self.result


def advance(transfers, others=()):
    moving = [t for t in transfers if t.wanted is not None]
    arrived, others = lax.optimization_barrier(([t.send() for t in moving], others))
    for transfer, values in zip(moving, arrived):
        transfer.receive(values)
    return others


def gather_ordered(values):
    z_masks, y_masks, x_masks, c_masks = bit_masks()
    masks = z_masks + y_masks + x_masks + c_masks
    blocks = values[None]
    for mask in masks:
        blocks = jnp.concatenate([blocks, swap(blocks, mask)], 0)
    inverse = [0] * blocks.shape[0]
    for place, entry in enumerate(offsets(masks)):
        inverse[entry] = place
    places = jnp.array(inverse, jnp.int32)
    order = places.at[jnp.arange(len(inverse)) ^ device_index()].get(mode="promise_in_bounds")
    return blocks.at[order].get(mode="promise_in_bounds").reshape((-1,) + values.shape[1:])


def together(*values):
    return lax.optimization_barrier(values)


def sum_steps(values):
    for masks in bit_masks():
        for mask in masks:
            (arrived,) = yield [(values, across(mask))]
            values = values + arrived
    return values


def sum_all(values):
    for masks in reversed(bit_masks()):
        for mask in masks:
            values = jax.tree.map(lambda v: v + swap(v, mask), values)
    return values


def near_far(values, x_masks):
    pieces = [values]
    for mask in x_masks:
        pieces = pieces + [swap(piece, mask) for piece in pieces]
    return pieces


def group_sum(partials, x_masks):
    sums = [kept + swap(sent, 1).astype(wide_type) for kept, sent in partials]
    for mask in reversed(x_masks):
        half = len(sums) // 2
        sums = [
            near + swap(far.astype(low_type), mask).astype(wide_type)
            for near, far in zip(sums[:half], sums[half:])
        ]
    return sums[0]


def dot_nn(left, right):
    return jnp.dot(left, right, preferred_element_type=wide_type)


def dot_nt(left, right):
    return lax.dot_general(left, right, (((1,), (1,)), ((), ())), preferred_element_type=wide_type)


def dot_tn(left, right):
    return lax.dot_general(left, right, (((0,), (0,)), ((), ())), preferred_element_type=wide_type)


def normalise(values):
    centre = values - jnp.mean(values, -1, keepdims=True)
    spread = jnp.mean(centre * centre, -1, keepdims=True)
    scale = lax.rsqrt(spread + norm_eps)
    return centre * scale, scale


def normalise_back(hat, scale, gain, grad):
    lifted = grad * gain
    return scale * (
        lifted
        - jnp.mean(lifted, -1, keepdims=True)
        - hat * jnp.mean(lifted * hat, -1, keepdims=True)
    )


def start_weights(tab_ref, halves, w_ref, sems):
    count, rows, columns = halves[0].shape
    width = w_ref.shape[0]
    columns = columns // width
    for side, half in enumerate(halves):

        def step(r, carry):
            row = pl.multiple_of(tab_ref[0, side * count + r] * rows, rows)
            column = pl.multiple_of(tab_ref[1, side * count + r] * columns, columns)
            for k in range(width):
                pltpu.make_async_copy(
                    half.at[r, :, pl.ds(k * columns, columns)],
                    w_ref.at[k, pl.ds(row, rows), pl.ds(column, columns)],
                    sems.at[k],
                ).start()
            return carry

        lax.fori_loop(0, count, step, 0)


def wait_weights(w_ref, sems, k):
    pltpu.make_async_copy(w_ref.at[k], w_ref.at[k], sems.at[k]).wait()


def store_grads(tab_ref, g_ref, halves, sem, k):
    count, rows, columns = halves[0].shape
    columns = columns // g_ref.shape[0]
    for side, half in enumerate(halves):

        def step(r, carry):
            row = pl.multiple_of(tab_ref[0, side * count + r] * rows, rows)
            column = pl.multiple_of(tab_ref[1, side * count + r] * columns, columns)
            pltpu.make_async_copy(
                g_ref.at[k, pl.ds(row, rows), pl.ds(column, columns)],
                half.at[r, :, pl.ds(k * columns, columns)],
                sem.at[k],
            ).start()
            return carry

        lax.fori_loop(0, count, step, 0)


def lane_masks():
    lane = lax.broadcasted_iota(jnp.int32, (1, 2 * HEAD_DIM), 1)
    return (lane < HEAD_DIM, lane >= HEAD_DIM)


def softmax_rows(query, keys, bias):
    scores = dot_nt(query, keys) * 0.125 + bias
    powers = jnp.exp(scores - jnp.max(scores, -1, keepdims=True))
    return powers / jnp.sum(powers, -1, keepdims=True)


def attention_forward_kernel(count, tab_ref, stream_ref, vec_ref, shift_ref, bias_ref, *refs):
    middle_ref, second_ref, first_ref, qkv_ref, mixed_ref, w_ref, sems = refs[count:]
    start_weights(tab_ref, refs[:count], w_ref, sems)
    width = stream_ref.shape[1]
    hat, scale = normalise(stream_ref[...])
    first_ref[...] = (hat * vec_ref[0:1, :] + vec_ref[1:2, :]).astype(low_type)
    for k in range(3):
        wait_weights(w_ref, sems, k)
        for c in range(0, width, 256):
            part = dot_nn(first_ref[...], w_ref[k, :, c : c + 256]) + shift_ref[k : k + 1, c : c + 256]
            qkv_ref[k, :, c : c + 256] = part.astype(low_type)

    def pair(h, carry):
        at = pl.ds(pl.multiple_of(h * 128, 128), 128)
        query, keys, values = qkv_ref[0, :, at], qkv_ref[1, :, at], qkv_ref[2, :, at]
        outs = []
        for lanes in lane_masks():
            own = jnp.where(lanes, query, jnp.zeros_like(query))
            probs = softmax_rows(own, keys, bias_ref[...]).astype(low_type)
            outs.append(dot_nn(probs, values))
        mixed_ref[:, at] = jnp.where(lane_masks()[0], outs[0], outs[1]).astype(low_type)
        return carry

    lax.fori_loop(0, width // 128, pair, 0)
    wait_weights(w_ref, sems, 3)
    for c in range(0, width, 256):
        middle_ref[:, c : c + 256] = (
            stream_ref[:, c : c + 256]
            + dot_nt(mixed_ref[...], w_ref[3, c : c + 256, :])
            + vec_ref[4:5, c : c + 256]
        )
    hat, scale = normalise(middle_ref[...])
    second_ref[...] = (hat * vec_ref[2:3, :] + vec_ref[3:4, :]).astype(low_type)


def attention_chain_kernel(
    count, tab_ref, upper_ref, pull_ref, middle_ref, stream_ref, vec_ref, bias_ref, qkv_ref, *refs
):
    below_ref, below_low_ref, up_ref, joined_ref, rows_ref, w_ref, sems = refs[count : count + 7]
    mixed_grad_ref, mid_grad_ref, norm_grad_ref = refs[count + 7 :]
    start_weights(tab_ref, refs[:count], w_ref, sems)
    width = stream_ref.shape[1]
    upper = upper_ref[...]
    rows_ref[5:6, :] = jnp.sum(upper, 0, keepdims=True)
    pull = pull_ref[...]
    hat, scale = normalise(middle_ref[...])
    rows_ref[2:3, :] = jnp.sum(pull * hat, 0, keepdims=True)
    rows_ref[3:4, :] = jnp.sum(pull, 0, keepdims=True)
    mid_grad = upper + normalise_back(hat, scale, vec_ref[2:3, :], pull)
    mid_grad_ref[...] = mid_grad
    rows_ref[4:5, :] = jnp.sum(mid_grad, 0, keepdims=True)
    up_ref[...] = mid_grad.astype(low_type)
    wait_weights(w_ref, sems, 3)
    for c in range(0, width, 256):
        mixed_grad_ref[:, c : c + 256] = dot_nn(up_ref[...], w_ref[3, :, c : c + 256]).astype(low_type)

    def pair(h, carry):
        at = pl.ds(pl.multiple_of(h * 128, 128), 128)
        query, keys, values = qkv_ref[0, :, at], qkv_ref[1, :, at], qkv_ref[2, :, at]
        grads = mixed_grad_ref[:, at]
        outs = []
        for lanes in lane_masks():
            own = jnp.where(lanes, query, jnp.zeros_like(query))
            own_grad = jnp.where(lanes, grads, jnp.zeros_like(grads))
            probs = softmax_rows(own, keys, bias_ref[...])
            value_grad = dot_tn(probs.astype(low_type), grads)
            prob_grad = dot_nt(own_grad, values)
            weighted = probs * prob_grad
            score_grad = (
                (weighted - probs * jnp.sum(weighted, -1, keepdims=True)) * 0.125
            ).astype(low_type)
            outs.append((dot_nn(score_grad, keys), dot_tn(score_grad, query), value_grad))
        for k in range(3):
            part = jnp.where(lane_masks()[0], outs[0][k], outs[1][k])
            joined_ref[k, :, at] = part.astype(low_type)
            if k != 1:
                rows_ref[6 + k // 2 : 7 + k // 2, at] = jnp.sum(part, 0, keepdims=True)
        return carry

    lax.fori_loop(0, width // 128, pair, 0)
    for k in range(3):
        wait_weights(w_ref, sems, k)
    for c in range(0, width, 256):
        norm_grad_ref[:, c : c + 256] = (
            dot_nt(joined_ref[0], w_ref[0, c : c + 256, :])
            + dot_nt(joined_ref[1], w_ref[1, c : c + 256, :])
            + dot_nt(joined_ref[2], w_ref[2, c : c + 256, :])
        )
    hat, scale = normalise(stream_ref[...])
    norm_grad = norm_grad_ref[...]
    rows_ref[0:1, :] = jnp.sum(norm_grad * hat, 0, keepdims=True)
    rows_ref[1:2, :] = jnp.sum(norm_grad, 0, keepdims=True)
    below = mid_grad_ref[...] + normalise_back(hat, scale, vec_ref[0:1, :], norm_grad)
    below_ref[...] = below
    below_low_ref[...] = below.astype(low_type)


def attention_weights_kernel(tab_ref, first_ref, joined_ref, up_ref, mixed_ref, *refs):
    g_ref, sems = refs[-2:]
    width = first_ref.shape[1]
    for k in range(4):
        for c in range(0, width, 256):
            if k < 3:
                part = dot_tn(first_ref[...], joined_ref[k, :, c : c + 256])
            else:
                part = dot_tn(up_ref[...], mixed_ref[:, c : c + 256])
            g_ref[k, :, c : c + 256] = part.astype(low_type)
        store_grads(tab_ref, g_ref, refs[:-2], sems, k)
    for k in range(4):
        wait_weights(g_ref, sems, k)


def pack_kernel(joint_ref, output_ref, expand_ref, shrink_ref, attention_ref, hidden_ref):
    cut, local_hidden = joint_ref.shape[3], expand_ref.shape[2]
    for layer in range(LAYERS):
        for k in range(3):
            attention_ref[layer, :, k * cut : (k + 1) * cut] = joint_ref[layer, k].astype(low_type)
        attention_ref[layer, :, 3 * cut :] = output_ref[layer].T.astype(low_type)
        hidden_ref[layer, :, :local_hidden] = expand_ref[layer].astype(low_type)
        hidden_ref[layer, :, local_hidden:] = shrink_ref[layer].T.astype(low_type)


def unpack_kernel(attention_ref, hidden_ref, joint_ref, output_ref, expand_ref, shrink_ref, square_ref):
    cut, local_hidden = joint_ref.shape[3], expand_ref.shape[2]
    total = jnp.zeros((1, 1), wide_type)
    for layer in range(LAYERS):
        for k in range(3):
            joint_ref[layer, k] = attention_ref[layer, :, k * cut : (k + 1) * cut]
        output_ref[layer] = attention_ref[layer, :, 3 * cut :].T
        expand_ref[layer] = hidden_ref[layer, :, :local_hidden]
        shrink_ref[layer] = hidden_ref[layer, :, local_hidden:].T
        for source in (attention_ref, hidden_ref):
            total = total + jnp.sum(source[layer] * source[layer], keepdims=True)
    square_ref[...] = total


def embed_kernel(tab_ref, chosen_ref, base_ref, *refs):
    out_ref, w_ref, sem = refs[-3:]
    count, rows, width = refs[0].shape
    for side, half in enumerate(refs[:-3]):

        def step(r, carry):
            row = pl.multiple_of(tab_ref[side * count + r] * rows, rows)
            pltpu.make_async_copy(half.at[r], w_ref.at[pl.ds(row, rows)], sem).start()
            return carry

        lax.fori_loop(0, count, step, 0)
    pltpu.make_async_copy(w_ref, w_ref, sem).wait()
    for c in range(0, width, 256):
        out_ref[:, c : c + 256] = base_ref[:, c : c + 256] + dot_nn(chosen_ref[...], w_ref[:, c : c + 256])


def embed_weights_kernel(tab_ref, chosen_ref, upper_ref, *refs):
    g_ref, sem = refs[-2:]
    count, rows, width = refs[0].shape
    for c in range(0, width, 256):
        g_ref[:, c : c + 256] = dot_tn(chosen_ref[...], upper_ref[:, c : c + 256]).astype(low_type)
    for side, half in enumerate(refs[:-2]):

        def step(r, carry):
            row = pl.multiple_of(tab_ref[side * count + r] * rows, rows)
            pltpu.make_async_copy(g_ref.at[pl.ds(row, rows)], half.at[r], sem).start()
            return carry

        lax.fori_loop(0, count, step, 0)
    pltpu.make_async_copy(g_ref, g_ref, sem).wait()


gelu_scale = 0.7978845608028654
gelu_cube = 0.044715


def hidden_forward_kernel(count, tab_ref, here_ref, there_ref, raise_ref, *refs):
    kept_ref, sent_ref, w_ref, active_ref, sems = refs[count:]
    start_weights(tab_ref, refs[:count], w_ref, sems)
    rows, width = here_ref.shape
    hidden_width = active_ref.shape[1]
    wait_weights(w_ref, sems, 0)
    for side, source in enumerate((here_ref, there_ref)):
        for c in range(0, hidden_width, 256):
            hidden = dot_nn(source[...], w_ref[0, :, c : c + 256]) + raise_ref[0:1, c : c + 256]
            bent = jnp.tanh(gelu_scale * (hidden + gelu_cube * (hidden * hidden * hidden)))
            active_ref[side * rows : (side + 1) * rows, c : c + 256] = (
                hidden * (0.5 * (1.0 + bent))
            ).astype(low_type)
    wait_weights(w_ref, sems, 1)
    for c in range(0, width, 256):
        kept_ref[:, c : c + 256] = dot_nt(active_ref[0:rows, :], w_ref[1, c : c + 256, :])
        sent_ref[:, c : c + 256] = dot_nt(active_ref[rows : 2 * rows, :], w_ref[1, c : c + 256, :]).astype(low_type)


def hidden_chain_kernel(
    count, tab_ref, here_ref, there_ref, down_here_ref, down_there_ref, raise_ref, *refs
):
    kept_ref, sent_ref, active_ref, grad_ref, raise_grad_ref, w_ref, sems = refs[count:]
    start_weights(tab_ref, refs[:count], w_ref, sems)
    rows, width = here_ref.shape
    hidden_width = active_ref.shape[1]
    wait_weights(w_ref, sems, 0)
    wait_weights(w_ref, sems, 1)
    pairs = ((here_ref, down_here_ref), (there_ref, down_there_ref))
    for c in range(0, hidden_width, 256):
        total = jnp.zeros((1, 256), wide_type)
        for side, (source, down) in enumerate(pairs):
            hidden = dot_nn(source[...], w_ref[0, :, c : c + 256]) + raise_ref[0:1, c : c + 256]
            pulled = dot_nn(down[...], w_ref[1, :, c : c + 256])
            square = hidden * hidden
            bent = jnp.tanh(gelu_scale * (hidden + gelu_cube * (square * hidden)))
            share = 0.5 * (1.0 + bent)
            active_ref[side * rows : (side + 1) * rows, c : c + 256] = (hidden * share).astype(low_type)
            slope = share + (0.5 * hidden) * (1.0 - bent * bent) * (
                gelu_scale + (3.0 * gelu_scale * gelu_cube) * square
            )
            grad = pulled * slope
            grad_ref[side * rows : (side + 1) * rows, c : c + 256] = grad.astype(low_type)
            total = total + jnp.sum(grad, 0, keepdims=True)
        raise_grad_ref[0:1, c : c + 256] = total
    for c in range(0, width, 256):
        kept_ref[:, c : c + 256] = dot_nt(grad_ref[0:rows, :], w_ref[0, c : c + 256, :])
        sent_ref[:, c : c + 256] = dot_nt(grad_ref[rows : 2 * rows, :], w_ref[0, c : c + 256, :]).astype(low_type)


def hidden_weights_kernel(count, tab_ref, *refs):
    groups = [refs[6 * g : 6 * g + 6] for g in range(count)]
    out_ref, g_ref, inputs_ref, down_ref, active_ref, grad_ref, sems = refs[6 * count :]
    rows, width = groups[0][0].shape
    hidden_width = active_ref.shape[1]
    for g, (here, there, down_here, down_there, active, grad) in enumerate(groups):
        at = 2 * g * rows
        inputs_ref[at : at + rows, :] = here[...]
        inputs_ref[at + rows : at + 2 * rows, :] = there[...]
        down_ref[at : at + rows, :] = down_here[...]
        down_ref[at + rows : at + 2 * rows, :] = down_there[...]
        active_ref[at : at + 2 * rows, :] = active[...]
        grad_ref[at : at + 2 * rows, :] = grad[...]
    for k, (left, right) in enumerate(((inputs_ref, grad_ref), (down_ref, active_ref))):
        for c in range(0, hidden_width, 256):
            g_ref[k, :, c : c + 256] = dot_tn(left[...], right[:, c : c + 256]).astype(low_type)
        store_grads(tab_ref, g_ref, (out_ref,), sems, k)
    for k in range(2):
        wait_weights(g_ref, sems, k)


def head_kernel(final_ref, logit_ref, out_ref):
    width = final_ref.shape[1]
    logit = logit_ref[...]
    out_ref[0:width, :] = dot_tn(final_ref[...], logit.astype(low_type))
    out_ref[width : width + 1, :] = jnp.sum(logit, 0, keepdims=True)


smem = pl.BlockSpec(memory_space=pltpu.SMEM)
vmem = pl.BlockSpec(memory_space=pltpu.VMEM)
anywhere = pl.BlockSpec(memory_space=pl.ANY)


def call(kernel, in_specs, outs, scratch, flops, moved):
    return pl.pallas_call(
        kernel,
        out_shape=tuple(jax.ShapeDtypeStruct(shape, kind) for shape, kind, spec in outs),
        in_specs=in_specs,
        out_specs=tuple(spec for shape, kind, spec in outs),
        scratch_shapes=scratch,
        compiler_params=pltpu.CompilerParams(vmem_limit_bytes=48 * 1024 * 1024),
        cost_estimate=pl.CostEstimate(flops=flops, bytes_accessed=moved, transcendentals=0),
    )


def embed(places, chosen, base, halves):
    count, rows, width = halves[0].shape
    depth = chosen.shape[1]
    if rows % 16:
        order = jnp.zeros_like(places).at[places].set(jnp.arange(places.shape[0], dtype=jnp.int32))
        full = jnp.concatenate(halves, 0)[order].reshape(depth, width)
        return base + jnp.dot(chosen, full, preferred_element_type=wide_type)
    return call(
        embed_kernel,
        [smem] + [vmem] * 2 + [anywhere] * len(halves),
        [(base.shape, wide_type, vmem)],
        [pltpu.VMEM((depth, width), low_type), pltpu.SemaphoreType.DMA],
        2 * chosen.shape[0] * depth * width,
        4 * depth * width,
    )(places, chosen, base, *halves)[0]


def embed_weights(places, chosen, upper, half_shape):
    count, rows, width = half_shape
    depth = chosen.shape[1]
    if rows % 16:
        full = lax.dot_general(
            chosen, upper, (((0,), (0,)), ((), ())), preferred_element_type=wide_type
        )
        blocks = full.astype(low_type).reshape(-1, rows, width)[places]
        return tuple(blocks[k * count : (k + 1) * count] for k in range(4))
    return call(
        embed_weights_kernel,
        [smem] + [vmem] * 2,
        [(half_shape, low_type, anywhere)] * 4,
        [pltpu.VMEM((depth, width), low_type), pltpu.SemaphoreType.DMA],
        2 * chosen.shape[0] * depth * width,
        4 * depth * width,
    )(places, chosen, upper)


def attention_forward(stream, vec, shift, bias, gathered):
    tab, *halves = gathered
    rows, width = stream.shape
    return call(
        functools.partial(attention_forward_kernel, len(halves)),
        [smem] + [vmem] * 4 + [anywhere] * len(halves),
        [
            ((rows, width), wide_type, vmem),
            ((rows, width), low_type, vmem),
            ((rows, width), low_type, vmem),
            ((3, rows, width), low_type, vmem),
            ((rows, width), low_type, vmem),
        ],
        [pltpu.VMEM((4, width, width), low_type), pltpu.SemaphoreType.DMA((4,))],
        20 * rows * width * width,
        20 * width * width,
    )(tab, stream, vec, shift, bias, *halves)


def attention_chain(upper, pull, middle, stream, vec, bias, qkv, gathered):
    tab, *halves = gathered
    rows, width = stream.shape
    return call(
        functools.partial(attention_chain_kernel, len(halves)),
        [smem] + [vmem] * 7 + [anywhere] * len(halves),
        [
            ((rows, width), wide_type, vmem),
            ((rows, width), low_type, vmem),
            ((rows, width), low_type, vmem),
            ((3, rows, width), low_type, vmem),
            ((8, width), wide_type, vmem),
        ],
        [
            pltpu.VMEM((4, width, width), low_type),
            pltpu.SemaphoreType.DMA((4,)),
            pltpu.VMEM((rows, width), low_type),
            pltpu.VMEM((rows, width), wide_type),
            pltpu.VMEM((rows, width), wide_type),
        ],
        30 * rows * width * width,
        30 * width * width,
    )(tab, upper, pull, middle, stream, vec, bias, qkv, *halves)


def attention_weights(tab, first, joined, up, mixed, half_shape):
    rows, width = first.shape
    return call(
        attention_weights_kernel,
        [smem] + [vmem] * 4,
        [(half_shape, low_type, anywhere)] * 4,
        [pltpu.VMEM((4, width, width), low_type), pltpu.SemaphoreType.DMA((4,))],
        16 * rows * width * width,
        16 * width * width,
    )(tab, first, joined, up, mixed)


def hidden_forward(here, there, raise_row, gathered):
    tab, *halves = gathered
    rows, width = here.shape
    hidden_width = raise_row.shape[1]
    return call(
        functools.partial(hidden_forward_kernel, len(halves)),
        [smem] + [vmem] * 3 + [anywhere] * len(halves),
        [((rows, width), wide_type, vmem), ((rows, width), low_type, vmem)],
        [
            pltpu.VMEM((2, width, hidden_width), low_type),
            pltpu.VMEM((2 * rows, hidden_width), low_type),
            pltpu.SemaphoreType.DMA((2,)),
        ],
        16 * rows * width * hidden_width,
        10 * width * hidden_width,
    )(tab, here, there, raise_row, *halves)


def hidden_chain(here, there, down_here, down_there, raise_row, gathered):
    tab, *halves = gathered
    rows, width = here.shape
    hidden_width = raise_row.shape[1]
    return call(
        functools.partial(hidden_chain_kernel, len(halves)),
        [smem] + [vmem] * 5 + [anywhere] * len(halves),
        [
            ((rows, width), wide_type, vmem),
            ((rows, width), low_type, vmem),
            ((2 * rows, hidden_width), low_type, vmem),
            ((2 * rows, hidden_width), low_type, vmem),
            ((1, hidden_width), wide_type, vmem),
        ],
        [pltpu.VMEM((2, width, hidden_width), low_type), pltpu.SemaphoreType.DMA((2,))],
        20 * rows * width * hidden_width,
        20 * width * hidden_width,
    )(tab, here, there, down_here, down_there, raise_row, *halves)


def hidden_weights(tab, groups, out_shape):
    rows, width = groups[0][0].shape
    hidden_width = groups[0][4].shape[1]
    count = len(groups)
    return call(
        functools.partial(hidden_weights_kernel, count),
        [smem] + [vmem] * (6 * count),
        [(out_shape, low_type, anywhere)],
        [
            pltpu.VMEM((2, width, hidden_width), low_type),
            pltpu.VMEM((2 * count * rows, width), low_type),
            pltpu.VMEM((2 * count * rows, width), low_type),
            pltpu.VMEM((2 * count * rows, hidden_width), low_type),
            pltpu.VMEM((2 * count * rows, hidden_width), low_type),
            pltpu.SemaphoreType.DMA((2,)),
        ],
        16 * count * rows * width * hidden_width,
        20 * width * hidden_width,
    )(tab, *[member for group in groups for member in group])[0]


def pack_weights(joint, output, expand, shrink):
    rows, cut, local_hidden = joint.shape[2], joint.shape[3], expand.shape[2]
    return call(
        pack_kernel,
        [vmem] * 4,
        [
            ((LAYERS, rows, 4 * cut), low_type, vmem),
            ((LAYERS, rows, 2 * local_hidden), low_type, vmem),
        ],
        [],
        1 << 20,
        1 << 22,
    )(joint, output, expand, shrink)


def unpack_grads(attention, hidden, rows, cut, local_hidden):
    return call(
        unpack_kernel,
        [vmem] * 2,
        [
            ((LAYERS, 3, rows, cut), wide_type, vmem),
            ((LAYERS, cut, rows), wide_type, vmem),
            ((LAYERS, rows, local_hidden), wide_type, vmem),
            ((LAYERS, local_hidden, rows), wide_type, vmem),
            ((1, 1), wide_type, vmem),
        ],
        [],
        1 << 20,
        1 << 22,
    )(attention, hidden)


def head_gradient(final_every, logit_every):
    width = final_every.shape[1]
    return call(
        head_kernel,
        [vmem] * 2,
        [((width + 1, logit_every.shape[1]), wide_type, vmem)],
        [],
        1 << 28,
        1 << 23,
    )(final_every, logit_every)[0]


def layer_norm(values, gain_row, shift_row):
    centre = values - jnp.mean(values, -1, keepdims=True)
    spread = jnp.mean(centre * centre, -1, keepdims=True)
    return centre * lax.rsqrt(spread + norm_eps) * gain_row + shift_row


def product(form, left, right):
    return jnp.einsum(form, left, right, preferred_element_type=wide_type)


def adamw(weight, moment_one, moment_two, gradient, rate):
    first_new = beta_one * moment_one + (1.0 - beta_one) * gradient
    second_new = beta_two * moment_two + (1.0 - beta_two) * gradient * gradient
    corrected = first_new / (1.0 - beta_one**STEP)
    scaled = second_new / (1.0 - beta_two**STEP)
    weight_new = weight - rate * (corrected / (jnp.sqrt(scaled) + adam_eps) + decay_rate * weight)
    return (weight_new, first_new, second_new)


def on_device(
    patches,
    keep_list,
    keep_count,
    labels,
    patch_weight,
    vector_table,
    head_table,
    joint_weight,
    shift_table,
    output_weight,
    expand_weight,
    raise_table,
    shrink_weight,
    *moments,
):
    share_images = patches.shape[0]
    model_width = vector_table.shape[1]
    data, model = lax.axis_size("dp"), lax.axis_size("mp")
    devices = data * model
    total_images = share_images * devices
    real_rows = share_images * SLOTS
    rows = -(-real_rows // 16) * 16
    z_masks, y_masks, x_masks, c_masks = bit_masks()
    me = device_index()
    model_index = lax.axis_index("mp")
    local_hidden = expand_weight.shape[2]

    def column_of(devices_at):
        return devices_at // model

    def table(devices_at):
        return jnp.stack([devices_at // model, devices_at % model])

    flip_masks = y_masks + x_masks + c_masks
    turned_masks = x_masks + y_masks + c_masks
    every, turned = origins(flip_masks), origins(turned_masks)
    every_tab, turned_tab, direct_tab = table(every), table(turned), table(jnp.arange(devices, dtype=jnp.int32))
    column = jnp.arange(data, dtype=jnp.int32)
    column_tab = jnp.stack([column, jnp.zeros_like(column)])

    attention_packs, hidden_packs = pack_weights(
        joint_weight.transpose(0, 2, 1, 3), output_weight, expand_weight, shrink_weight
    )
    pack_rows, pack_width = attention_packs.shape[1:]
    first_pack = jnp.concatenate(
        [attention_packs[0], patch_weight.astype(low_type).reshape(-1, pack_width)], 0
    )
    first_move = Transfer(gather_z(first_pack))
    while first_move.wanted is not None:
        hidden_packs, attention_packs = advance([first_move], (hidden_packs, attention_packs))
    hidden_halves = [(column_tab, lax.all_gather(hidden_packs[0], "dp"))]
    attention_later = [
        (direct_tab, lax.all_gather(attention_packs[layer], AXES)) for layer in range(1, LAYERS)
    ]
    attention_blocks = first_move.result[:, :pack_rows]
    patch_blocks = first_move.result[:, pack_rows:].reshape(-1, *patch_weight.shape)
    attention_blocks, patch_blocks, later_packs = together(
        attention_blocks, patch_blocks, hidden_packs
    )
    attention_move = Transfer(gather_quarters(attention_blocks, flip_masks))
    patch_move = Transfer(gather_quarters(patch_blocks, turned_masks))
    later_moves = [Transfer(gather_all(later_packs[layer], y_masks)) for layer in range(1, LAYERS)]
    for step in range(len(flip_masks) - 2):
        advance([patch_move, attention_move])
    advance([patch_move, attention_move] + later_moves)
    patch_halves, attention_first = patch_move.finish(), attention_move.finish()
    attention_halves = [(every_tab,) + attention_first] + attention_later
    halves_tab = jnp.stack([column_of(origins(y_masks)), jnp.zeros_like(column)])

    patch_ids = jnp.arange(PATCHES, dtype=jnp.int32)
    kept_slot = patch_ids[None, :] < keep_count[:, None]
    selector = ((keep_list[:, :, None] == patch_ids[None, None, :]) & kept_slot[:, :, None]).astype(
        wide_type
    )
    selector = jnp.pad(selector, ((0, 0), (1, 0), (0, 0)))
    chosen = product("nsp,npc->nsc", selector.astype(low_type), patches).astype(low_type)
    chosen = jnp.pad(chosen.reshape(real_rows, -1), ((0, rows - real_rows), (0, 0)))
    slot_kept = jnp.pad(kept_slot, ((0, 0), (1, 0))).astype(wide_type)
    slot_first = jnp.zeros((share_images, SLOTS), wide_type).at[:, 0].set(1.0)
    spread = jnp.concatenate(
        [selector, slot_kept[:, :, None], slot_first[:, :, None]], 2
    ).reshape(real_rows, PATCHES + 2)
    spread = jnp.pad(spread, ((0, rows - real_rows), (0, 0)))
    sources = jnp.concatenate(
        [
            vector_table[1:SLOTS],
            vector_table[SLOTS + 1 : SLOTS + 2],
            vector_table[SLOTS : SLOTS + 1] + vector_table[0:1],
        ],
        0,
    )
    base = jnp.dot(spread, sources, precision=highest)
    stream = embed(turned, chosen, base, patch_halves)

    row_ids = jnp.arange(rows, dtype=jnp.int32)
    image_ids, slot_ids = row_ids // SLOTS, row_ids % SLOTS
    row_count = jnp.pad(jnp.repeat(keep_count, SLOTS), (0, rows - real_rows), constant_values=SLOTS)
    live = (image_ids[:, None] == image_ids[None, :]) & (slot_ids <= row_count)[None, :]
    bias = jnp.where(live, 0.0, -1e30).astype(wide_type)

    saved = []
    for layer in range(LAYERS):
        base = SLOTS + 4 + 6 * layer
        vec = vector_table[base : base + 6]
        shift = jnp.stack(
            [shift_table[layer, 0], jnp.zeros((model_width,), wide_type), shift_table[layer, 1]]
        )
        raise_row = lax.dynamic_slice_in_dim(
            raise_table[layer], model_index * local_hidden, local_hidden, 0
        )[None]
        middle, second, first, qkv, mixed = attention_forward(
            stream, vec, shift, bias, attention_halves[layer]
        )
        second = advance(later_moves, second)
        if layer > 0:
            hidden_halves.append((halves_tab,) + later_moves[layer - 1].finish())
        outer = near_far(second, x_masks)
        inner = [swap(outer[0], 1)]
        partials = [hidden_forward(outer[0], inner[0], raise_row, hidden_halves[layer])]
        partials, outer = advance(later_moves, (partials, outer))
        for k in range(1, len(outer)):
            inner.append(swap(outer[k], 1))
            partials.append(hidden_forward(outer[k], inner[k], raise_row, hidden_halves[layer]))
        pieces = (outer, inner)
        saved.append((stream, middle, first, qkv, mixed, pieces, vec, raise_row))
        mlp_out = group_sum(partials, x_masks)
        stream = middle + mlp_out + vec[5:6]

    lead_rows = stream[:real_rows].reshape(share_images, SLOTS, model_width)[:, 0]
    final_out, final_pull = jax.vjp(
        layer_norm, lead_rows, vector_table[SLOTS + 2], vector_table[SLOTS + 3]
    )
    final_low = final_out.astype(low_type)
    head_low = head_table[:model_width].astype(low_type)
    logits = product("nd,dc->nc", final_low, head_low) + head_table[model_width]
    target_hot = (labels[:, None] == jnp.arange(CLASSES, dtype=jnp.int32)[None, :]).astype(
        wide_type
    )
    loss_local = jnp.sum(jax.nn.logsumexp(logits, -1) - jnp.sum(logits * target_hot, -1))
    logit_grad = (jax.nn.softmax(logits, -1) - target_hot) / total_images
    logit_low = logit_grad.astype(low_type)
    head_every = gather_ordered(jnp.concatenate([final_low.astype(wide_type), logit_grad], 1))
    final_grad = product("nc,dc->nd", logit_low, head_low)
    lead_grad, gain_final, shift_final = final_pull(final_grad)
    upper = jnp.zeros((share_images, SLOTS, model_width), wide_type).at[:, 0].set(lead_grad)
    upper = jnp.pad(upper.reshape(real_rows, model_width), ((0, rows - real_rows), (0, 0)))
    upper_low = upper.astype(low_type)

    vector_rows, shift_rows, raise_rows = [None] * LAYERS, [None] * LAYERS, [None] * LAYERS
    attention_moves, hidden_sums = [None] * LAYERS, [None] * LAYERS
    waiting = None
    for layer in reversed(range(LAYERS)):
        stream_in, middle, first, qkv, mixed, pieces, vec, raise_row = saved[layer]
        outer, inner = pieces
        outer_down = near_far(upper_low, x_masks)
        inner_down = [swap(outer_down[0], 1)]
        partials, groups, raise_sum = [], [], 0.0
        if waiting is not None:
            waiting, inner_down = together(waiting, inner_down)
            attention_moves[layer + 1] = Transfer(reduce_all(waiting, turned_masks))
        for k in range(len(outer)):
            if k == 1:
                partials, outer_down = advance(attention_moves[layer + 1 :], (partials, outer_down))
            if k > 0:
                inner_down.append(swap(outer_down[k], 1))
            kept, sent, active, grad, raise_part = hidden_chain(
                outer[k], inner[k], outer_down[k], inner_down[k], raise_row, hidden_halves[layer]
            )
            partials.append((kept, sent))
            groups.append((outer[k], inner[k], outer_down[k], inner_down[k], active, grad))
            raise_sum = raise_sum + raise_part
        hidden_grads = hidden_weights(column_tab, groups, (data,) + hidden_packs[0].shape)
        pull = group_sum(partials, x_masks)
        pull, hidden_grads, head_every = together(pull, hidden_grads, head_every)
        hidden_sums[layer] = lax.psum_scatter(hidden_grads, "dp", scatter_dimension=0).astype(wide_type)
        upper, upper_low, up, joined, tail = attention_chain(
            upper, pull, middle, stream_in, vec, bias, qkv, attention_halves[layer]
        )
        upper, upper_low, up, joined = advance(
            attention_moves[layer + 1 :], (upper, upper_low, up, joined)
        )
        waiting = attention_weights(
            turned_tab if layer > 0 else every_tab, first, joined, up, mixed, (devices // 4, pack_rows, pack_width)
        )
        vector_rows[layer], shift_rows[layer] = tail[:6], tail[6:]
        raise_rows[layer] = lax.dynamic_update_slice_in_dim(
            jnp.zeros((model, local_hidden), wide_type), raise_sum, model_index, 0
        ).reshape(-1, model_width)

    place = lax.dot_general(
        spread, upper, (((0,), (0,)), ((), ())), precision=highest, preferred_element_type=wide_type
    )
    small = jnp.concatenate(
        [
            place[PATCHES + 1 :],
            place[:PATCHES],
            place[PATCHES + 1 :],
            place[PATCHES : PATCHES + 1],
            gain_final[None],
            shift_final[None],
        ]
        + vector_rows
        + shift_rows
        + raise_rows
        + [jnp.zeros((1, model_width), wide_type).at[0, 0].set(loss_local)],
        0,
    )
    patch_grads = embed_weights(turned, chosen, upper_low, patch_halves[0].shape)
    patch_move = Transfer(reduce_quarters(patch_grads, turned_masks))
    attention_move = Transfer(reduce_quarters(waiting, flip_masks))
    small_move = Transfer(sum_steps(small))
    while attention_move.wanted is not None:
        advance([patch_move, attention_move, small_move] + attention_moves[1:])
    head_sum = head_gradient(head_every[:, :model_width].astype(low_type), head_every[:, model_width:])
    last_blocks = jnp.concatenate(
        [attention_move.result, patch_move.result.reshape(data // sizes()[1], -1, pack_width)], 1
    )
    last_move = Transfer(reduce_z(last_blocks))
    while last_move.wanted is not None:
        advance([last_move, small_move] + attention_moves[1:])
    last_sum, small = last_move.result, small_move.finish()
    patch_sum = last_sum[pack_rows:].reshape(patch_weight.shape)
    attention_sums = [last_sum[:pack_rows]] + [m.finish() for m in attention_moves[1:]]
    joint_sum, output_sum, expand_sum, shrink_sum, shard_sq = unpack_grads(
        jnp.stack(attention_sums), jnp.stack(hidden_sums), pack_rows, pack_width // 4, local_hidden
    )
    joint_sum = joint_sum.transpose(0, 2, 1, 3)

    vector_count = vector_table.shape[0]
    vector_sum = small[:vector_count]
    shift_sum = small[vector_count : vector_count + 2 * LAYERS].reshape(shift_table.shape)
    raise_sum = small[vector_count + 2 * LAYERS : -1].reshape(raise_table.shape)
    loss_total = small[-1, 0]
    sharded_sq = shard_sq[0, 0] + jnp.sum(patch_sum * patch_sum)
    shared_sq = jnp.sum(head_sum * head_sum) + jnp.sum(small[:-1] * small[:-1])
    total_sq = sum_all(sharded_sq) + shared_sq
    gradient_norm = jnp.sqrt(total_sq)
    factor = jnp.minimum(1.0, clip_limit / (gradient_norm + norm_eps))
    weights_in = (
        patch_weight,
        vector_table,
        head_table,
        joint_weight,
        shift_table,
        output_weight,
        expand_weight,
        raise_table,
        shrink_weight,
    )
    reduced = (
        patch_sum,
        vector_sum,
        head_sum,
        joint_sum,
        shift_sum,
        output_sum,
        expand_sum,
        raise_sum,
        shrink_sum,
    )
    outputs = [loss_total, gradient_norm]
    for weight, moment_one, moment_two, gradient, rate in zip(
        weights_in, moments[:9], moments[9:], reduced, group_rates
    ):
        outputs.extend(adamw(weight, moment_one, moment_two, gradient * factor, rate))
    return tuple(outputs)


def solution(mesh):
    params = (
        P(("dp", "mp"), None),
        P(),
        P(),
        P(None, "dp", None, "mp"),
        P(),
        P(None, "mp", "dp"),
        P(None, "dp", "mp"),
        P(),
        P(None, "mp", "dp"),
    )
    in_specs = (
        P(("dp", "mp"), None, None),
        P(("dp", "mp"), None),
        P(("dp", "mp")),
        P(("dp", "mp")),
    ) + 3 * params
    out_specs = (P(), P()) + tuple(spec for spec in params for _ in range(3))
    return jax.shard_map(
        on_device, mesh=mesh, in_specs=in_specs, out_specs=out_specs, check_vma=False
    )
```

```python
import functools

import jax
import jax.numpy as jnp
from jax import lax
from jax.experimental import pallas as pl
from jax.experimental.pallas import tpu as pltpu
from jax.sharding import PartitionSpec as P

HEAD_DIM = 64
CLASSES = 1000
PATCHES = 49
LAYERS = 2
STEP = 10
SLOTS = 50
AXES = ("dp", "mp")

group_rates = (0.01, 0.2, 0.01, 0.01, 0.1, 0.03, 0.01, 0.1, 0.01)
beta_one = 0.9
beta_two = 0.95
adam_eps = 1e-08
decay_rate = 0.1
clip_limit = 0.02
norm_eps = 1e-06
highest = lax.Precision.HIGHEST
low_type = jnp.bfloat16
wide_type = jnp.float32


def move(values, pairs):
    return lax.ppermute(values, AXES, pairs)


def across(mask):
    return [(n, n ^ mask) for n in range(lax.axis_size("dp") * lax.axis_size("mp"))]


def swap(values, mask):
    return move(values, across(mask))


def device_index():
    return lax.axis_index("dp") * lax.axis_size("mp") + lax.axis_index("mp")


def sizes():
    model, data = lax.axis_size("mp"), lax.axis_size("dp")
    wide = 1 << ((data.bit_length() - 1) // 2)
    return data // wide, wide, model // 2, wide * model


def bit_masks():
    deep, wide, across_x, stride = sizes()
    model = lax.axis_size("mp")
    z_masks = [stride << b for b in range(deep.bit_length() - 1)]
    y_masks = [model << b for b in range(wide.bit_length() - 1)]
    x_masks = [2 << b for b in range(across_x.bit_length() - 1)]
    return (z_masks, y_masks, x_masks, [1])


def offsets(masks):
    table = [0]
    for mask in masks:
        table = table + [entry ^ mask for entry in table]
    return table


def origins(masks, early=()):
    deep, wide, across_x, stride = sizes()
    me = device_index()
    places = [
        (flip ^ first, t) for flip in offsets(masks) for t in range(deep) for first in offsets(early)
    ]
    flips = jnp.array([flip for flip, t in places], jnp.int32)
    turns = jnp.array([t for flip, t in places], jnp.int32)
    return (me // stride + turns) % deep * stride + ((me % stride) ^ flips)


def along_z(shift, first, last):
    deep, wide, across_x, stride = sizes()
    return [
        (z * stride + n, (z + shift) * stride + n) for z in range(first, last + 1) for n in range(stride)
    ]


def gather_z(values):
    deep, wide, across_x, stride = sizes()
    z = device_index() // stride
    up, down, ups, downs = values, values, [], []
    for k in range(1, deep):
        up, down = yield [
            (up, along_z(1, k - 1, deep - 2)),
            (down, along_z(-1, 1, deep - k)),
        ]
        ups.append(up)
        downs.append(down)
    return jnp.stack(
        [values] + [jnp.where(z + t < deep, downs[t - 1], ups[deep - t - 1]) for t in range(1, deep)]
    )


def gather_flips(blocks, masks):
    for mask in masks[:-1]:
        (arrived,) = yield [(blocks, across(mask))]
        blocks = jnp.concatenate([blocks, arrived], 0)
    (arrived,) = yield [(blocks, across(masks[-1]))]
    return blocks, arrived


def gather_quarters(blocks, masks):
    for mask in masks[:-2]:
        (arrived,) = yield [(blocks, across(mask))]
        blocks = jnp.concatenate([blocks, arrived], 0)
    arrived, beside = yield [(blocks, across(masks[-2])), (blocks, across(masks[-1]))]
    (last,) = yield [(arrived, across(masks[-1]))]
    return blocks, arrived, beside, last


def gather_all(values, masks):
    blocks = yield from gather_z(values)
    return (yield from gather_flips(blocks, masks))


def reduce_halves(parts, masks):
    kept, sent = parts
    (arrived,) = yield [(sent, across(masks[-1]))]
    terms = [kept, arrived]
    for mask in reversed(masks[:-1]):
        half = terms[0].shape[0] // 2
        sent = sum(term[half:].astype(wide_type) for term in terms).astype(low_type)
        kept = sum(term[:half].astype(wide_type) for term in terms)
        (arrived,) = yield [(sent, across(mask))]
        terms = [kept, arrived]
    return sum(term.astype(wide_type) for term in terms)


def reduce_z(blocks):
    deep = blocks.shape[0]
    up = down = None
    for k in range(deep - 1, 0, -1):
        rising, falling = blocks[k], blocks[deep - k]
        if up is not None:
            rising = rising.astype(wide_type) + up.astype(wide_type)
            falling = falling.astype(wide_type) + down.astype(wide_type)
        up, down = yield [
            (rising.astype(low_type), along_z(1, 0, deep - 1 - k)),
            (falling.astype(low_type), along_z(-1, k, deep - 1)),
        ]
    return blocks[0].astype(wide_type) + up.astype(wide_type) + down.astype(wide_type)


def reduce_deep(blocks, early):
    blocks = blocks.reshape((sizes()[0], -1) + blocks.shape[1:])
    blocks = yield from reduce_z(blocks)
    for mask in reversed(early):
        half = blocks.shape[0] // 2
        (arrived,) = yield [(blocks[half:].astype(low_type), across(mask))]
        blocks = blocks[:half] + arrived.astype(wide_type)
    return blocks[0]


def reduce_all(parts, masks):
    kept, sent = parts
    half = sent.shape[0] // 2
    (later,) = yield [(sent[half:], across(masks[-1]))]
    (sooner,) = yield [(sent[:half], across(masks[-1]))]
    onward = (kept[half:].astype(wide_type) + later.astype(wide_type)).astype(low_type)
    (arrived,) = yield [(onward, across(masks[-2]))]
    terms = [kept[:half], sooner, arrived]
    for mask in reversed(masks[:-2]):
        half = terms[0].shape[0] // 2
        onward = sum(term[half:].astype(wide_type) for term in terms).astype(low_type)
        kept = sum(term[:half].astype(wide_type) for term in terms)
        (arrived,) = yield [(onward, across(mask))]
        terms = [kept, arrived]
    return (yield from reduce_z(sum(term.astype(wide_type) for term in terms)))


class Transfer:
    def __init__(self, steps):
        self.steps = steps
        self.wanted = next(steps)
        self.result = None

    def send(self):
        return [move(*item) for item in self.wanted]

    def receive(self, arrived):
        try:
            self.wanted = self.steps.send(arrived)
        except StopIteration as end:
            self.wanted, self.result = None, end.value

    def finish(self):
        while self.wanted is not None:
            self.receive(self.send())
        return self.result


def advance(transfers, others=()):
    moving = [t for t in transfers if t.wanted is not None]
    arrived, others = lax.optimization_barrier(([t.send() for t in moving], others))
    for transfer, values in zip(moving, arrived):
        transfer.receive(values)
    return others


def gather_rows(values):
    z_masks, y_masks, x_masks, c_masks = bit_masks()
    masks = z_masks + y_masks + x_masks + c_masks
    blocks = values[None]
    for mask in masks:
        blocks = jnp.concatenate([blocks, swap(blocks, mask)], 0)
    return blocks


def in_order(blocks):
    z_masks, y_masks, x_masks, c_masks = bit_masks()
    masks = z_masks + y_masks + x_masks + c_masks
    inverse = [0] * blocks.shape[0]
    for place, entry in enumerate(offsets(masks)):
        inverse[entry] = place
    places = jnp.array(inverse, jnp.int32)
    order = places.at[jnp.arange(len(inverse)) ^ device_index()].get(mode="promise_in_bounds")
    return blocks.at[order].get(mode="promise_in_bounds").reshape((-1,) + blocks.shape[2:])


def together(*values):
    return lax.optimization_barrier(values)


def sum_steps(values):
    for masks in bit_masks():
        for mask in masks:
            rounded = values.astype(low_type)
            (arrived,) = yield [(rounded, across(mask))]
            values = rounded.astype(wide_type) + arrived.astype(wide_type)
    return values


def sum_all(values):
    for masks in reversed(bit_masks()):
        for mask in masks:
            values = jax.tree.map(lambda v: v + swap(v, mask), values)
    return values


def near_far(values, x_masks):
    pieces = [values]
    for mask in x_masks:
        pieces = pieces + [swap(piece, mask) for piece in pieces]
    return pieces


def group_sum(partials, x_masks):
    sums = [kept + swap(sent, 1).astype(wide_type) for kept, sent in partials]
    for mask in reversed(x_masks):
        half = len(sums) // 2
        sums = [
            near + swap(far.astype(low_type), mask).astype(wide_type)
            for near, far in zip(sums[:half], sums[half:])
        ]
    return sums[0]


def dot_nn(left, right):
    return jnp.dot(left, right, preferred_element_type=wide_type)


def dot_nt(left, right):
    return lax.dot_general(left, right, (((1,), (1,)), ((), ())), preferred_element_type=wide_type)


def dot_tn(left, right):
    return lax.dot_general(left, right, (((0,), (0,)), ((), ())), preferred_element_type=wide_type)


def normalise(values):
    centre = values - jnp.mean(values, -1, keepdims=True)
    spread = jnp.mean(centre * centre, -1, keepdims=True)
    scale = lax.rsqrt(spread + norm_eps)
    return centre * scale, scale


def normalise_back(hat, scale, gain, grad):
    lifted = grad * gain
    return scale * (
        lifted
        - jnp.mean(lifted, -1, keepdims=True)
        - hat * jnp.mean(lifted * hat, -1, keepdims=True)
    )


def start_weights(tab_ref, halves, w_ref, sems):
    count, rows, columns = halves[0].shape
    width = w_ref.shape[0]
    columns = columns // width
    for side, half in enumerate(halves):

        def step(r, carry):
            row = pl.multiple_of(tab_ref[0, side * count + r] * rows, rows)
            column = pl.multiple_of(tab_ref[1, side * count + r] * columns, columns)
            for k in range(width):
                pltpu.make_async_copy(
                    half.at[r, :, pl.ds(k * columns, columns)],
                    w_ref.at[k, pl.ds(row, rows), pl.ds(column, columns)],
                    sems.at[k],
                ).start()
            return carry

        lax.fori_loop(0, count, step, 0)


def wait_weights(w_ref, sems, k):
    pltpu.make_async_copy(w_ref.at[k], w_ref.at[k], sems.at[k]).wait()


def store_grads(tab_ref, g_ref, halves, sem, k):
    count, rows, columns = halves[0].shape
    columns = columns // g_ref.shape[0]
    for side, half in enumerate(halves):

        def step(r, carry):
            row = pl.multiple_of(tab_ref[0, side * count + r] * rows, rows)
            column = pl.multiple_of(tab_ref[1, side * count + r] * columns, columns)
            pltpu.make_async_copy(
                g_ref.at[k, pl.ds(row, rows), pl.ds(column, columns)],
                half.at[r, :, pl.ds(k * columns, columns)],
                sem.at[k],
            ).start()
            return carry

        lax.fori_loop(0, count, step, 0)


def lane_masks():
    lane = lax.broadcasted_iota(jnp.int32, (1, 2 * HEAD_DIM), 1)
    return (lane < HEAD_DIM, lane >= HEAD_DIM)


def softmax_columns(keys, query, bias):
    scores = dot_nt(keys, query) + bias
    powers = jnp.exp(scores - jnp.max(scores, 0, keepdims=True))
    return powers * (1.0 / jnp.sum(powers, 0, keepdims=True))


def attention_forward_kernel(count, tab_ref, stream_ref, vec_ref, shift_ref, bias_ref, *refs):
    middle_ref, second_ref, first_ref, qkv_ref, mixed_ref, w_ref, sems = refs[count:]
    start_weights(tab_ref, refs[:count], w_ref, sems)
    width = stream_ref.shape[1]
    hat, scale = normalise(stream_ref[...])
    first_ref[...] = (hat * vec_ref[0:1, :] + vec_ref[1:2, :]).astype(low_type)
    for k in range(3):
        wait_weights(w_ref, sems, k)
        for c in range(0, width, 256):
            part = dot_nn(first_ref[...], w_ref[k, :, c : c + 256]) + shift_ref[k : k + 1, c : c + 256]
            qkv_ref[k, :, c : c + 256] = part.astype(low_type)

    def pair(h, carry):
        at = pl.ds(pl.multiple_of(h * 128, 128), 128)
        query, keys, values = qkv_ref[0, :, at], qkv_ref[1, :, at], qkv_ref[2, :, at]
        query = query * 0.125
        outs = []
        for lanes in lane_masks():
            own = jnp.where(lanes, query, jnp.zeros_like(query))
            scores = dot_nt(own, keys) + bias_ref[...]
            powers = jnp.exp(scores - jnp.max(scores, -1, keepdims=True))
            probs = powers * (1.0 / jnp.sum(powers, -1, keepdims=True))
            outs.append(dot_nn(probs.astype(low_type), values))
        mixed_ref[:, at] = jnp.where(lane_masks()[0], outs[0], outs[1]).astype(low_type)
        return carry

    lax.fori_loop(0, width // 128, pair, 0, unroll=8)
    wait_weights(w_ref, sems, 3)
    for c in range(0, width, 256):
        middle_ref[:, c : c + 256] = (
            stream_ref[:, c : c + 256]
            + dot_nt(mixed_ref[...], w_ref[3, c : c + 256, :])
            + vec_ref[4:5, c : c + 256]
        )
    hat, scale = normalise(middle_ref[...])
    second_ref[...] = (hat * vec_ref[2:3, :] + vec_ref[3:4, :]).astype(low_type)


def attention_chain_kernel(
    count, tab_ref, upper_ref, pull_ref, middle_ref, stream_ref, vec_ref, bias_ref, qkv_ref, *refs
):
    below_ref, below_low_ref, up_ref, joined_ref, rows_ref, w_ref, sems = refs[count : count + 7]
    mixed_grad_ref, mid_grad_ref, norm_grad_ref = refs[count + 7 :]
    start_weights(tab_ref, refs[:count], w_ref, sems)
    width = stream_ref.shape[1]
    upper = upper_ref[...]
    rows_ref[5:6, :] = jnp.sum(upper, 0, keepdims=True)
    pull = pull_ref[...]
    hat, scale = normalise(middle_ref[...])
    rows_ref[2:3, :] = jnp.sum(pull * hat, 0, keepdims=True)
    rows_ref[3:4, :] = jnp.sum(pull, 0, keepdims=True)
    mid_grad = upper + normalise_back(hat, scale, vec_ref[2:3, :], pull)
    mid_grad_ref[...] = mid_grad
    rows_ref[4:5, :] = jnp.sum(mid_grad, 0, keepdims=True)
    up_ref[...] = mid_grad.astype(low_type)
    wait_weights(w_ref, sems, 3)
    for c in range(0, width, 256):
        mixed_grad_ref[:, c : c + 256] = dot_nn(up_ref[...], w_ref[3, :, c : c + 256]).astype(low_type)

    def pair(h, carry):
        at = pl.ds(pl.multiple_of(h * 128, 128), 128)
        query, keys, values = qkv_ref[0, :, at], qkv_ref[1, :, at], qkv_ref[2, :, at]
        grads = mixed_grad_ref[:, at]
        query = query * 0.125
        turned = keys.T
        outs = []
        for h, lanes in enumerate(lane_masks()):
            own = jnp.where(lanes, query, jnp.zeros_like(query))
            own_grad = jnp.where(lanes, grads, jnp.zeros_like(grads))
            probs = softmax_columns(keys, own, bias_ref[...])
            value_grad = dot_nn(probs.astype(low_type), grads)
            prob_grad = dot_nt(values, own_grad)
            drift = jnp.sum(probs * prob_grad, 0, keepdims=True)
            score_grad = (probs * (prob_grad - drift)).astype(low_type)
            query_grad = dot_nn(turned[h * HEAD_DIM : (h + 1) * HEAD_DIM], score_grad)
            outs.append((query_grad, dot_nn(score_grad, query), value_grad))
        first_head = lane_masks()[0]
        parts = (
            jnp.concatenate([outs[0][0], outs[1][0]], 0).T * 0.125,
            jnp.where(first_head, outs[0][1], outs[1][1]),
            jnp.where(first_head, outs[0][2], outs[1][2]),
        )
        for k in range(3):
            part = parts[k]
            joined_ref[k, :, at] = part.astype(low_type)
            if k != 1:
                rows_ref[6 + k // 2 : 7 + k // 2, at] = jnp.sum(part, 0, keepdims=True)
        return carry

    lax.fori_loop(0, width // 128, pair, 0, unroll=4)
    for k in range(3):
        wait_weights(w_ref, sems, k)
    for c in range(0, width, 256):
        norm_grad_ref[:, c : c + 256] = (
            dot_nt(joined_ref[0], w_ref[0, c : c + 256, :])
            + dot_nt(joined_ref[1], w_ref[1, c : c + 256, :])
            + dot_nt(joined_ref[2], w_ref[2, c : c + 256, :])
        )
    hat, scale = normalise(stream_ref[...])
    norm_grad = norm_grad_ref[...]
    rows_ref[0:1, :] = jnp.sum(norm_grad * hat, 0, keepdims=True)
    rows_ref[1:2, :] = jnp.sum(norm_grad, 0, keepdims=True)
    below = mid_grad_ref[...] + normalise_back(hat, scale, vec_ref[0:1, :], norm_grad)
    below_ref[...] = below
    below_low_ref[...] = below.astype(low_type)


def attention_weights_kernel(tab_ref, *refs):
    half_a, half_b, g_ref, first_all, joined_all, up_all, mixed_all, sems = refs[8:]
    rows, width = refs[0].shape
    for side in range(2):
        first_ref, joined_ref, up_ref, mixed_ref = refs[4 * side : 4 * side + 4]
        at = slice(side * rows, (side + 1) * rows)
        first_all[at, :] = first_ref[...]
        up_all[at, :] = up_ref[...]
        mixed_all[at, :] = mixed_ref[...]
        for k in range(3):
            joined_all[k, at, :] = joined_ref[k]
    for k in range(4):
        for c in range(0, width, 256):
            if k < 3:
                part = dot_tn(first_all[...], joined_all[k, :, c : c + 256])
            else:
                part = dot_tn(up_all[...], mixed_all[:, c : c + 256])
            g_ref[k, :, c : c + 256] = part.astype(low_type)
        store_grads(tab_ref, g_ref, (half_a, half_b), sems, k)
    done = g_ref.at[0, :, pl.ds(0, width // 2)]
    for k in range(4):
        pltpu.make_async_copy(done, done, sems.at[k]).wait()


def pack_attention_kernel(joint_ref, output_ref, attention_ref):
    cut = joint_ref.shape[3]
    for layer in range(joint_ref.shape[0]):
        for k in range(3):
            attention_ref[layer, :, k * cut : (k + 1) * cut] = joint_ref[layer, k].astype(low_type)
        attention_ref[layer, :, 3 * cut :] = output_ref[layer].T.astype(low_type)


def pack_hidden_kernel(expand_ref, shrink_ref, hidden_ref):
    local_hidden = expand_ref.shape[2]
    for layer in range(LAYERS):
        hidden_ref[layer, :, :local_hidden] = expand_ref[layer].astype(low_type)
        hidden_ref[layer, :, local_hidden:] = shrink_ref[layer].T.astype(low_type)


def unpack_attention_kernel(pack_ref, joint_ref, output_ref, square_ref):
    cut = joint_ref.shape[2]
    for k in range(3):
        joint_ref[k] = pack_ref[:, k * cut : (k + 1) * cut]
    output_ref[...] = pack_ref[:, 3 * cut :].T
    square_ref[...] = jnp.sum(pack_ref[...] * pack_ref[...], keepdims=True)


def unpack_hidden_kernel(*refs):
    expand_ref, shrink_ref, square_ref = refs[LAYERS:]
    local_hidden = expand_ref.shape[2]
    total = jnp.zeros((1, 1), wide_type)
    for layer, pack_ref in enumerate(refs[:LAYERS]):
        pack = pack_ref[...].astype(wide_type)
        expand_ref[layer] = pack[:, :local_hidden]
        shrink_ref[layer] = pack[:, local_hidden:].T
        total = total + jnp.sum(pack * pack, keepdims=True)
    square_ref[...] = total


def embed_kernel(tab_ref, chosen_ref, base_ref, *refs):
    out_ref, w_ref, sem = refs[-3:]
    count, rows, width = refs[0].shape
    for side, half in enumerate(refs[:-3]):

        def step(r, carry):
            row = pl.multiple_of(tab_ref[side * count + r] * rows, rows)
            pltpu.make_async_copy(half.at[r], w_ref.at[pl.ds(row, rows)], sem).start()
            return carry

        lax.fori_loop(0, count, step, 0)
    pltpu.make_async_copy(w_ref, w_ref, sem).wait()
    for c in range(0, width, 256):
        out_ref[:, c : c + 256] = base_ref[:, c : c + 256] + dot_nn(chosen_ref[...], w_ref[:, c : c + 256])


def embed_weights_kernel(
    tab_ref, chosen_ref, upper_ref, chosen_other, upper_other, half_a, half_b, g_ref, chosen_all, upper_all, sem
):
    count, rows, width = half_a.shape
    depth = chosen_ref.shape[0]
    chosen_all[0:depth, :] = chosen_ref[...]
    chosen_all[depth : 2 * depth, :] = chosen_other[...]
    upper_all[0:depth, :] = upper_ref[...]
    upper_all[depth : 2 * depth, :] = upper_other[...]
    for c in range(0, width, 256):
        g_ref[:, c : c + 256] = dot_tn(chosen_all[...], upper_all[:, c : c + 256]).astype(low_type)
    for side, half in enumerate((half_a, half_b)):

        def step(r, carry):
            row = pl.multiple_of(tab_ref[side * count + r] * rows, rows)
            pltpu.make_async_copy(g_ref.at[pl.ds(row, rows)], half.at[r], sem).start()
            return carry

        lax.fori_loop(0, count, step, 0)
    done = g_ref.at[pl.ds(0, 2 * count * rows)]
    pltpu.make_async_copy(done, done, sem).wait()


gelu_scale = 0.7978845608028654
gelu_cube = 0.044715


def hidden_forward_kernel(count, tab_ref, here_ref, there_ref, raise_ref, *refs):
    kept_ref, sent_ref, w_ref, active_ref, sems = refs[count:]
    start_weights(tab_ref, refs[:count], w_ref, sems)
    rows, width = here_ref.shape
    hidden_width = active_ref.shape[1]
    wait_weights(w_ref, sems, 0)
    for side, source in enumerate((here_ref, there_ref)):
        for c in range(0, hidden_width, 256):
            hidden = dot_nn(source[...], w_ref[0, :, c : c + 256]) + raise_ref[0:1, c : c + 256]
            bent = jnp.tanh(gelu_scale * (hidden + gelu_cube * (hidden * hidden * hidden)))
            active_ref[side * rows : (side + 1) * rows, c : c + 256] = (
                hidden * (0.5 * (1.0 + bent))
            ).astype(low_type)
    wait_weights(w_ref, sems, 1)
    for c in range(0, width, 256):
        kept_ref[:, c : c + 256] = dot_nt(active_ref[0:rows, :], w_ref[1, c : c + 256, :])
        sent_ref[:, c : c + 256] = dot_nt(active_ref[rows : 2 * rows, :], w_ref[1, c : c + 256, :]).astype(low_type)


def hidden_chain_kernel(
    count, tab_ref, here_ref, there_ref, down_here_ref, down_there_ref, raise_ref, *refs
):
    kept_ref, sent_ref, active_ref, grad_ref, raise_grad_ref, w_ref, sems = refs[count:]
    start_weights(tab_ref, refs[:count], w_ref, sems)
    rows, width = here_ref.shape
    hidden_width = active_ref.shape[1]
    wait_weights(w_ref, sems, 0)
    wait_weights(w_ref, sems, 1)
    pairs = ((here_ref, down_here_ref), (there_ref, down_there_ref))
    for c in range(0, hidden_width, 256):
        total = jnp.zeros((1, 256), wide_type)
        for side, (source, down) in enumerate(pairs):
            hidden = dot_nn(source[...], w_ref[0, :, c : c + 256]) + raise_ref[0:1, c : c + 256]
            pulled = dot_nn(down[...], w_ref[1, :, c : c + 256])
            square = hidden * hidden
            bent = jnp.tanh(gelu_scale * (hidden + gelu_cube * (square * hidden)))
            share = 0.5 * (1.0 + bent)
            active_ref[side * rows : (side + 1) * rows, c : c + 256] = (hidden * share).astype(low_type)
            slope = share + (0.5 * hidden) * (1.0 - bent * bent) * (
                gelu_scale + (3.0 * gelu_scale * gelu_cube) * square
            )
            grad = pulled * slope
            grad_ref[side * rows : (side + 1) * rows, c : c + 256] = grad.astype(low_type)
            total = total + jnp.sum(grad, 0, keepdims=True)
        raise_grad_ref[0:1, c : c + 256] = total
    for c in range(0, width, 256):
        kept_ref[:, c : c + 256] = dot_nt(grad_ref[0:rows, :], w_ref[0, c : c + 256, :])
        sent_ref[:, c : c + 256] = dot_nt(grad_ref[rows : 2 * rows, :], w_ref[0, c : c + 256, :]).astype(low_type)


def hidden_weights_kernel(count, tab_ref, *refs):
    groups = [refs[6 * g : 6 * g + 6] for g in range(count)]
    out_ref, g_ref, inputs_ref, down_ref, active_ref, grad_ref, sems = refs[6 * count :]
    rows, width = groups[0][0].shape
    hidden_width = active_ref.shape[1]
    for g, (here, there, down_here, down_there, active, grad) in enumerate(groups):
        at = 2 * g * rows
        inputs_ref[at : at + rows, :] = here[...]
        inputs_ref[at + rows : at + 2 * rows, :] = there[...]
        down_ref[at : at + rows, :] = down_here[...]
        down_ref[at + rows : at + 2 * rows, :] = down_there[...]
        active_ref[at : at + 2 * rows, :] = active[...]
        grad_ref[at : at + 2 * rows, :] = grad[...]
    for k, (left, right) in enumerate(((inputs_ref, grad_ref), (down_ref, active_ref))):
        for c in range(0, hidden_width, 256):
            g_ref[k, :, c : c + 256] = dot_tn(left[...], right[:, c : c + 256]).astype(low_type)
        store_grads(tab_ref, g_ref, (out_ref,), sems, k)
    for k in range(2):
        wait_weights(g_ref, sems, k)


def head_kernel(final_ref, logit_ref, out_ref):
    width = final_ref.shape[1]
    logit = logit_ref[...]
    out_ref[0:width, :] = dot_tn(final_ref[...], logit.astype(low_type))
    out_ref[width : width + 1, :] = jnp.sum(logit, 0, keepdims=True)


smem = pl.BlockSpec(memory_space=pltpu.SMEM)
vmem = pl.BlockSpec(memory_space=pltpu.VMEM)
anywhere = pl.BlockSpec(memory_space=pl.ANY)


def call(kernel, in_specs, outs, scratch, flops, moved):
    return pl.pallas_call(
        kernel,
        out_shape=tuple(jax.ShapeDtypeStruct(shape, kind) for shape, kind, spec in outs),
        in_specs=in_specs,
        out_specs=tuple(spec for shape, kind, spec in outs),
        scratch_shapes=scratch,
        compiler_params=pltpu.CompilerParams(vmem_limit_bytes=48 * 1024 * 1024),
        cost_estimate=pl.CostEstimate(flops=flops, bytes_accessed=moved, transcendentals=0),
    )


def embed(places, chosen, base, halves):
    count, rows, width = halves[0].shape
    depth = chosen.shape[1]
    if rows % 16:
        order = jnp.zeros_like(places).at[places].set(jnp.arange(places.shape[0], dtype=jnp.int32))
        full = jnp.concatenate(halves, 0)[order].reshape(depth, width)
        return base + jnp.dot(chosen, full, preferred_element_type=wide_type)
    return call(
        embed_kernel,
        [smem] + [vmem] * 2 + [anywhere] * len(halves),
        [(base.shape, wide_type, vmem)],
        [pltpu.VMEM((depth, width), low_type), pltpu.SemaphoreType.DMA],
        2 * chosen.shape[0] * depth * width,
        4 * depth * width,
    )(places, chosen, base, *halves)[0]


def embed_weights(places, chosen, upper, chosen_other, upper_other, half_shape):
    count, rows, width = half_shape
    depth, pixels = chosen.shape
    if rows % 16:
        full = lax.dot_general(
            jnp.concatenate([chosen, chosen_other], 0),
            jnp.concatenate([upper, upper_other], 0),
            (((0,), (0,)), ((), ())),
            preferred_element_type=wide_type,
        )
        blocks = full.astype(low_type).reshape(-1, rows, width)[places]
        return blocks[:count], blocks[count:]
    return call(
        embed_weights_kernel,
        [smem] + [vmem] * 4,
        [(half_shape, low_type, anywhere)] * 2,
        [
            pltpu.VMEM((pixels, width), low_type),
            pltpu.VMEM((2 * depth, pixels), low_type),
            pltpu.VMEM((2 * depth, width), low_type),
            pltpu.SemaphoreType.DMA,
        ],
        4 * depth * pixels * width,
        4 * pixels * width,
    )(places, chosen, upper, chosen_other, upper_other)


def attention_forward(stream, vec, shift, bias, gathered):
    tab, *halves = gathered
    rows, width = stream.shape
    return call(
        functools.partial(attention_forward_kernel, len(halves)),
        [smem] + [vmem] * 4 + [anywhere] * len(halves),
        [
            ((rows, width), wide_type, vmem),
            ((rows, width), low_type, vmem),
            ((rows, width), low_type, vmem),
            ((3, rows, width), low_type, vmem),
            ((rows, width), low_type, vmem),
        ],
        [pltpu.VMEM((4, width, width), low_type), pltpu.SemaphoreType.DMA((4,))],
        20 * rows * width * width,
        20 * width * width,
    )(tab, stream, vec, shift, bias, *halves)


def attention_chain(upper, pull, middle, stream, vec, bias, qkv, gathered):
    tab, *halves = gathered
    rows, width = stream.shape
    return call(
        functools.partial(attention_chain_kernel, len(halves)),
        [smem] + [vmem] * 7 + [anywhere] * len(halves),
        [
            ((rows, width), wide_type, vmem),
            ((rows, width), low_type, vmem),
            ((rows, width), low_type, vmem),
            ((3, rows, width), low_type, vmem),
            ((8, width), wide_type, vmem),
        ],
        [
            pltpu.VMEM((4, width, width), low_type),
            pltpu.SemaphoreType.DMA((4,)),
            pltpu.VMEM((rows, width), low_type),
            pltpu.VMEM((rows, width), wide_type),
            pltpu.VMEM((rows, width), wide_type),
        ],
        30 * rows * width * width,
        30 * width * width,
    )(tab, upper, pull, middle, stream, vec, bias, qkv, *halves)


def attention_weights(tab, own, other, half_shape):
    rows, width = own[0].shape
    return call(
        attention_weights_kernel,
        [smem] + [vmem] * 8,
        [(half_shape, low_type, anywhere)] * 2,
        [
            pltpu.VMEM((4, width, width), low_type),
            pltpu.VMEM((2 * rows, width), low_type),
            pltpu.VMEM((3, 2 * rows, width), low_type),
            pltpu.VMEM((2 * rows, width), low_type),
            pltpu.VMEM((2 * rows, width), low_type),
            pltpu.SemaphoreType.DMA((4,)),
        ],
        16 * rows * width * width,
        16 * width * width,
    )(tab, *own, *other)


def hidden_forward(here, there, raise_row, gathered):
    tab, *halves = gathered
    rows, width = here.shape
    hidden_width = raise_row.shape[1]
    return call(
        functools.partial(hidden_forward_kernel, len(halves)),
        [smem] + [vmem] * 3 + [anywhere] * len(halves),
        [((rows, width), wide_type, vmem), ((rows, width), low_type, vmem)],
        [
            pltpu.VMEM((2, width, hidden_width), low_type),
            pltpu.VMEM((2 * rows, hidden_width), low_type),
            pltpu.SemaphoreType.DMA((2,)),
        ],
        16 * rows * width * hidden_width,
        10 * width * hidden_width,
    )(tab, here, there, raise_row, *halves)


def hidden_chain(here, there, down_here, down_there, raise_row, gathered):
    tab, *halves = gathered
    rows, width = here.shape
    hidden_width = raise_row.shape[1]
    return call(
        functools.partial(hidden_chain_kernel, len(halves)),
        [smem] + [vmem] * 5 + [anywhere] * len(halves),
        [
            ((rows, width), wide_type, vmem),
            ((rows, width), low_type, vmem),
            ((2 * rows, hidden_width), low_type, vmem),
            ((2 * rows, hidden_width), low_type, vmem),
            ((1, hidden_width), wide_type, vmem),
        ],
        [pltpu.VMEM((2, width, hidden_width), low_type), pltpu.SemaphoreType.DMA((2,))],
        20 * rows * width * hidden_width,
        20 * width * hidden_width,
    )(tab, here, there, down_here, down_there, raise_row, *halves)


def hidden_weights(tab, groups, out_shape):
    rows, width = groups[0][0].shape
    hidden_width = groups[0][4].shape[1]
    count = len(groups)
    return call(
        functools.partial(hidden_weights_kernel, count),
        [smem] + [vmem] * (6 * count),
        [(out_shape, low_type, anywhere)],
        [
            pltpu.VMEM((2, width, hidden_width), low_type),
            pltpu.VMEM((2 * count * rows, width), low_type),
            pltpu.VMEM((2 * count * rows, width), low_type),
            pltpu.VMEM((2 * count * rows, hidden_width), low_type),
            pltpu.VMEM((2 * count * rows, hidden_width), low_type),
            pltpu.SemaphoreType.DMA((2,)),
        ],
        16 * count * rows * width * hidden_width,
        20 * width * hidden_width,
    )(tab, *[member for group in groups for member in group])[0]


def pack_attention(joint, output):
    layers, rows, cut = joint.shape[0], joint.shape[2], joint.shape[3]
    return call(
        pack_attention_kernel,
        [vmem] * 2,
        [((layers, rows, 4 * cut), low_type, vmem)],
        [],
        1 << 20,
        1 << 21,
    )(joint, output)[0]


def pack_hidden(expand, shrink):
    layers, rows, local_hidden = expand.shape
    return call(
        pack_hidden_kernel,
        [vmem] * 2,
        [((layers, rows, 2 * local_hidden), low_type, vmem)],
        [],
        1 << 20,
        1 << 22,
    )(expand, shrink)[0]


def unpack_attention(pack):
    rows, width = pack.shape
    cut = width // 4
    return call(
        unpack_attention_kernel,
        [vmem],
        [((3, rows, cut), wide_type, vmem), ((cut, rows), wide_type, vmem), ((1, 1), wide_type, vmem)],
        [],
        1 << 20,
        1 << 20,
    )(pack)


def unpack_hidden(packs):
    rows, width = packs[0].shape
    local_hidden = width // 2
    return call(
        unpack_hidden_kernel,
        [vmem] * LAYERS,
        [
            ((LAYERS, rows, local_hidden), wide_type, vmem),
            ((LAYERS, local_hidden, rows), wide_type, vmem),
            ((1, 1), wide_type, vmem),
        ],
        [],
        1 << 20,
        1 << 22,
    )(*packs)


def head_gradient(final_every, logit_every):
    width = final_every.shape[1]
    return call(
        head_kernel,
        [vmem] * 2,
        [((width + 1, logit_every.shape[1]), wide_type, vmem)],
        [],
        1 << 28,
        1 << 23,
    )(final_every, logit_every)[0]


def layer_norm(values, gain_row, shift_row):
    centre = values - jnp.mean(values, -1, keepdims=True)
    spread = jnp.mean(centre * centre, -1, keepdims=True)
    return centre * lax.rsqrt(spread + norm_eps) * gain_row + shift_row


def product(form, left, right):
    return jnp.einsum(form, left, right, preferred_element_type=wide_type)


def adamw(weight, moment_one, moment_two, gradient, rate):
    first_new = beta_one * moment_one + (1.0 - beta_one) * gradient
    second_new = beta_two * moment_two + (1.0 - beta_two) * gradient * gradient
    corrected = first_new / (1.0 - beta_one**STEP)
    scaled = second_new / (1.0 - beta_two**STEP)
    weight_new = weight - rate * (corrected / (jnp.sqrt(scaled) + adam_eps) + decay_rate * weight)
    return (weight_new, first_new, second_new)


def on_device(
    patches,
    keep_list,
    keep_count,
    labels,
    patch_weight,
    vector_table,
    head_table,
    joint_weight,
    shift_table,
    output_weight,
    expand_weight,
    raise_table,
    shrink_weight,
    *moments,
):
    share_images = patches.shape[0]
    model_width = vector_table.shape[1]
    data, model = lax.axis_size("dp"), lax.axis_size("mp")
    devices = data * model
    total_images = share_images * devices
    real_rows = share_images * SLOTS
    rows = -(-real_rows // 16) * 16
    z_masks, y_masks, x_masks, c_masks = bit_masks()
    me = device_index()
    model_index = lax.axis_index("mp")
    local_hidden = expand_weight.shape[2]

    def column_of(devices_at):
        return devices_at // model

    def table(devices_at):
        return jnp.stack([devices_at // model, devices_at % model])

    flip_masks = y_masks + x_masks + c_masks
    turned_masks = x_masks + y_masks + c_masks
    every, turned = origins(flip_masks), origins(turned_masks)
    every_tab, turned_tab, direct_tab = table(every), table(turned), table(jnp.arange(devices, dtype=jnp.int32))
    column = jnp.arange(data, dtype=jnp.int32)
    column_tab = jnp.stack([column, jnp.zeros_like(column)])

    joint_rows = joint_weight.transpose(0, 2, 1, 3)
    first_attention = pack_attention(joint_rows[:1], output_weight[:1])
    attention_packs = pack_attention(joint_rows[1:], output_weight[1:])
    hidden_packs = pack_hidden(expand_weight, shrink_weight)
    pack_rows, pack_width = attention_packs.shape[1:]
    first_pack = jnp.concatenate(
        [first_attention[0], patch_weight.astype(low_type).reshape(-1, pack_width)], 0
    )
    first_move = Transfer(gather_z(first_pack))
    while first_move.wanted is not None:
        hidden_packs, attention_packs = advance([first_move], (hidden_packs, attention_packs))
    hidden_halves = [(column_tab, lax.all_gather(hidden_packs[0], "dp"))]
    attention_later = [
        (direct_tab, lax.all_gather(attention_packs[layer - 1], AXES)) for layer in range(1, LAYERS)
    ]
    attention_blocks = first_move.result[:, :pack_rows]
    patch_blocks = first_move.result[:, pack_rows:].reshape(-1, *patch_weight.shape)
    attention_blocks, patch_blocks, later_packs = together(
        attention_blocks, patch_blocks, hidden_packs
    )
    attention_move = Transfer(gather_quarters(attention_blocks, flip_masks))
    patch_move = Transfer(gather_quarters(patch_blocks, turned_masks))
    later_moves = [Transfer(gather_all(later_packs[layer], y_masks)) for layer in range(1, LAYERS)]
    for step in range(len(flip_masks) - 2):
        advance([patch_move, attention_move] + (later_moves if step == 0 else []))
    advance([patch_move, attention_move])
    patch_halves, attention_first = patch_move.finish(), attention_move.finish()
    attention_halves = [(every_tab,) + attention_first] + attention_later
    first_tab = jnp.stack([column_of(origins((), y_masks)), jnp.zeros_like(column)])
    halves_tab = jnp.stack([column_of(origins(y_masks)), jnp.zeros_like(column)])

    patch_ids = jnp.arange(PATCHES, dtype=jnp.int32)
    kept_slot = patch_ids[None, :] < keep_count[:, None]
    selector = ((keep_list[:, :, None] == patch_ids[None, None, :]) & kept_slot[:, :, None]).astype(
        wide_type
    )
    selector = jnp.pad(selector, ((0, 0), (1, 0), (0, 0)))
    chosen = product("nsp,npc->nsc", selector.astype(low_type), patches).astype(low_type)
    chosen = jnp.pad(chosen.reshape(real_rows, -1), ((0, rows - real_rows), (0, 0)))
    slot_kept = jnp.pad(kept_slot, ((0, 0), (1, 0))).astype(wide_type)
    slot_first = jnp.zeros((share_images, SLOTS), wide_type).at[:, 0].set(1.0)
    spread = jnp.concatenate(
        [selector, slot_kept[:, :, None], slot_first[:, :, None]], 2
    ).reshape(real_rows, PATCHES + 2)
    spread = jnp.pad(spread, ((0, rows - real_rows), (0, 0)))
    sources = jnp.concatenate(
        [
            vector_table[1:SLOTS],
            vector_table[SLOTS + 1 : SLOTS + 2],
            vector_table[SLOTS : SLOTS + 1] + vector_table[0:1],
        ],
        0,
    )
    base = jnp.dot(spread, sources, precision=highest)
    chosen_other = swap(chosen, 1)
    stream = embed(turned, chosen, base, patch_halves)

    row_ids = jnp.arange(rows, dtype=jnp.int32)
    image_ids, slot_ids = row_ids // SLOTS, row_ids % SLOTS
    row_count = jnp.pad(jnp.repeat(keep_count, SLOTS), (0, rows - real_rows), constant_values=SLOTS)
    same_image = image_ids[:, None] == image_ids[None, :]
    live = slot_ids <= row_count
    bias = jnp.where(same_image & live[None, :], 0.0, -1e30).astype(wide_type)
    turned_bias = jnp.where(same_image & live[:, None], 0.0, -1e30).astype(wide_type)

    saved = []
    for layer in range(LAYERS):
        base = SLOTS + 4 + 6 * layer
        vec = vector_table[base : base + 6]
        shift = jnp.stack(
            [shift_table[layer, 0], jnp.zeros((model_width,), wide_type), shift_table[layer, 1]]
        )
        raise_row = lax.dynamic_slice_in_dim(
            raise_table[layer], model_index * local_hidden, local_hidden, 0
        )[None]
        middle, second, first, qkv, mixed = attention_forward(
            stream, vec, shift, bias, attention_halves[layer]
        )
        second = advance(later_moves, second)
        if layer > 0:
            hidden_halves.append((halves_tab,) + later_moves[layer - 1].finish())
        outer = near_far(second, x_masks)
        inner = [swap(outer[0], 1)]
        partials = [hidden_forward(outer[0], inner[0], raise_row, hidden_halves[layer])]
        partials, outer = advance(later_moves, (partials, outer))
        for k in range(1, len(outer)):
            inner.append(swap(outer[k], 1))
            partials.append(hidden_forward(outer[k], inner[k], raise_row, hidden_halves[layer]))
        pieces = (outer, inner)
        beside = (swap(first, 1), swap(mixed, 1))
        saved.append((stream, middle, first, qkv, mixed, beside, pieces, vec, raise_row))
        mlp_out = group_sum(partials, x_masks)
        stream = middle + mlp_out + vec[5:6]

    lead_rows = stream[:real_rows].reshape(share_images, SLOTS, model_width)[:, 0]
    final_out, final_pull = jax.vjp(
        layer_norm, lead_rows, vector_table[SLOTS + 2], vector_table[SLOTS + 3]
    )
    final_low = final_out.astype(low_type)
    head_low = head_table[:model_width].astype(low_type)
    logits = product("nd,dc->nc", final_low, head_low) + head_table[model_width]
    target_hot = (labels[:, None] == jnp.arange(CLASSES, dtype=jnp.int32)[None, :]).astype(
        wide_type
    )
    loss_local = jnp.sum(jax.nn.logsumexp(logits, -1) - jnp.sum(logits * target_hot, -1))
    logit_grad = (jax.nn.softmax(logits, -1) - target_hot) / total_images
    logit_low = logit_grad.astype(low_type)
    head_every = gather_rows(jnp.concatenate([final_low.astype(wide_type), logit_grad], 1))
    final_grad = product("nc,dc->nd", logit_low, head_low)
    lead_grad, gain_final, shift_final = final_pull(final_grad)
    upper = jnp.zeros((share_images, SLOTS, model_width), wide_type).at[:, 0].set(lead_grad)
    upper = jnp.pad(upper.reshape(real_rows, model_width), ((0, rows - real_rows), (0, 0)))
    upper_low = upper.astype(low_type)

    vector_rows, shift_rows, raise_rows = [None] * LAYERS, [None] * LAYERS, [None] * LAYERS
    attention_moves, hidden_sums = [None] * LAYERS, [None] * LAYERS
    waiting = None
    for layer in reversed(range(LAYERS)):
        stream_in, middle, first, qkv, mixed, beside, pieces, vec, raise_row = saved[layer]
        outer, inner = pieces
        outer_down = near_far(upper_low, x_masks)
        inner_down = [swap(outer_down[0], 1)]
        partials, groups, raise_sum = [], [], 0.0
        if waiting is not None:
            waiting, inner_down = together(waiting, inner_down)
            attention_moves[layer + 1] = Transfer(reduce_all(waiting, x_masks + y_masks))
        for k in range(len(outer)):
            if k == 1:
                partials, outer_down = together(partials, outer_down)
            if k > 0:
                inner_down.append(swap(outer_down[k], 1))
            kept, sent, active, grad, raise_part = hidden_chain(
                outer[k], inner[k], outer_down[k], inner_down[k], raise_row, hidden_halves[layer]
            )
            partials.append((kept, sent))
            groups.append((outer[k], inner[k], outer_down[k], inner_down[k], active, grad))
            raise_sum = raise_sum + raise_part
        hidden_grads = hidden_weights(
            column_tab if layer > 0 else first_tab, groups, (data,) + hidden_packs[0].shape
        )
        pull = group_sum(partials, x_masks)
        pull, hidden_grads, head_every = advance(
            attention_moves[layer + 1 :], (pull, hidden_grads, head_every)
        )
        if layer > 0:
            hidden_sums[layer] = lax.psum_scatter(hidden_grads, "dp", scatter_dimension=0)
        else:
            hidden_move = Transfer(reduce_deep(hidden_grads, y_masks))
        upper, upper_low, up, joined, tail = attention_chain(
            upper, pull, middle, stream_in, vec, turned_bias, qkv, attention_halves[layer]
        )
        upper, upper_low, up, joined = advance(
            attention_moves[layer + 1 :], (upper, upper_low, up, joined)
        )
        waiting = attention_weights(
            table(origins(x_masks + y_masks if layer > 0 else y_masks + x_masks)),
            (first, joined, up, mixed),
            (beside[0], swap(joined, 1), swap(up, 1), beside[1]),
            (devices // 4, pack_rows, pack_width),
        )
        vector_rows[layer], shift_rows[layer] = tail[:6], tail[6:]
        raise_rows[layer] = lax.dynamic_update_slice_in_dim(
            jnp.zeros((model, local_hidden), wide_type), raise_sum, model_index, 0
        ).reshape(-1, model_width)

    place = lax.dot_general(
        spread, upper, (((0,), (0,)), ((), ())), precision=highest, preferred_element_type=wide_type
    )
    small = jnp.concatenate(
        [
            place[PATCHES + 1 :],
            place[:PATCHES],
            place[PATCHES + 1 :],
            place[PATCHES : PATCHES + 1],
            gain_final[None],
            shift_final[None],
        ]
        + vector_rows
        + shift_rows
        + raise_rows,
        0,
    )
    chosen, waiting = advance(attention_moves[1:], (chosen, waiting))
    patch_grads = embed_weights(
        origins(x_masks + y_masks), chosen, upper_low, chosen_other, swap(upper_low, 1), patch_halves[0].shape
    )
    patch_grads = advance(attention_moves[1:], patch_grads)
    patch_move = Transfer(reduce_halves(patch_grads, x_masks + y_masks))
    attention_move = Transfer(reduce_halves(waiting, y_masks + x_masks))
    small_move = Transfer(sum_steps(small))
    head_every = in_order(head_every)
    head_sum = head_gradient(head_every[:, :model_width].astype(low_type), head_every[:, model_width:])
    head_sum = advance([patch_move, attention_move, hidden_move, small_move], head_sum)
    while attention_move.wanted is not None:
        advance([patch_move, attention_move, hidden_move, small_move])
    last_blocks = jnp.concatenate(
        [attention_move.result, patch_move.result.reshape(data // sizes()[1], -1, pack_width)], 1
    )
    last_move = Transfer(reduce_z(last_blocks))
    advance([last_move, hidden_move, small_move])
    advance([last_move, hidden_move] + attention_moves[1:])
    while last_move.wanted is not None:
        advance([last_move, small_move] + attention_moves[1:])
    hidden_sums[0] = hidden_move.finish()
    last_sum, small = last_move.result, small_move.finish()
    patch_sum = last_sum[pack_rows:].reshape(patch_weight.shape)
    attention_sums = [last_sum[:pack_rows]] + [m.finish() for m in attention_moves[1:]]
    expand_sum, shrink_sum, shard_sq = unpack_hidden(hidden_sums)
    unpacked = [unpack_attention(total) for total in attention_sums]
    joint_sum = jnp.stack([member[0] for member in unpacked])
    output_sum = jnp.stack([member[1] for member in unpacked])
    for member in unpacked:
        shard_sq = shard_sq + member[2]
    joint_sum = joint_sum.transpose(0, 2, 1, 3)

    vector_count = vector_table.shape[0]
    vector_sum = small[:vector_count]
    shift_sum = small[vector_count : vector_count + 2 * LAYERS].reshape(shift_table.shape)
    raise_sum = small[vector_count + 2 * LAYERS :].reshape(raise_table.shape)
    sharded_sq = shard_sq[0, 0] + jnp.sum(patch_sum * patch_sum)
    shared_sq = jnp.sum(head_sum * head_sum) + jnp.sum(small * small)
    sums = sum_all(jnp.stack([sharded_sq, loss_local]))
    total_sq, loss_total = sums[0] + shared_sq, sums[1]
    gradient_norm = jnp.sqrt(total_sq)
    factor = jnp.minimum(1.0, clip_limit / (gradient_norm + norm_eps))
    weights_in = (
        patch_weight,
        vector_table,
        head_table,
        joint_weight,
        shift_table,
        output_weight,
        expand_weight,
        raise_table,
        shrink_weight,
    )
    reduced = (
        patch_sum,
        vector_sum,
        head_sum,
        joint_sum,
        shift_sum,
        output_sum,
        expand_sum,
        raise_sum,
        shrink_sum,
    )
    outputs = [loss_total, gradient_norm]
    for weight, moment_one, moment_two, gradient, rate in zip(
        weights_in, moments[:9], moments[9:], reduced, group_rates
    ):
        outputs.extend(adamw(weight, moment_one, moment_two, gradient * factor, rate))
    return tuple(outputs)


def solution(mesh):
    params = (
        P(("dp", "mp"), None),
        P(),
        P(),
        P(None, "dp", None, "mp"),
        P(),
        P(None, "mp", "dp"),
        P(None, "dp", "mp"),
        P(),
        P(None, "mp", "dp"),
    )
    in_specs = (
        P(("dp", "mp"), None, None),
        P(("dp", "mp"), None),
        P(("dp", "mp")),
        P(("dp", "mp")),
    ) + 3 * params
    out_specs = (P(), P()) + tuple(spec for spec in params for _ in range(3))
    return jax.shard_map(
        on_device, mesh=mesh, in_specs=in_specs, out_specs=out_specs, check_vma=False
    )
```

```python
import functools

import jax
import jax.numpy as jnp
from jax import lax
from jax.experimental import pallas as pl
from jax.experimental.pallas import tpu as pltpu
from jax.sharding import PartitionSpec as P

HEAD_DIM = 64
CLASSES = 1000
PATCHES = 49
LAYERS = 2
STEP = 10
SLOTS = 50
AXES = ("dp", "mp")

group_rates = (0.01, 0.2, 0.01, 0.01, 0.1, 0.03, 0.01, 0.1, 0.01)
beta_one = 0.9
beta_two = 0.95
adam_eps = 1e-08
decay_rate = 0.1
clip_limit = 0.02
norm_eps = 1e-06
highest = lax.Precision.HIGHEST
low_type = jnp.bfloat16
wide_type = jnp.float32


def move(values, pairs):
    return lax.ppermute(values, AXES, pairs)


def across(mask):
    return [(n, n ^ mask) for n in range(lax.axis_size("dp") * lax.axis_size("mp"))]


def swap(values, mask):
    return move(values, across(mask))


def device_index():
    return lax.axis_index("dp") * lax.axis_size("mp") + lax.axis_index("mp")


def sizes():
    model, data = lax.axis_size("mp"), lax.axis_size("dp")
    wide = 1 << ((data.bit_length() - 1) // 2)
    return data // wide, wide, model // 2, wide * model


def bit_masks():
    deep, wide, across_x, stride = sizes()
    model = lax.axis_size("mp")
    z_masks = [stride << b for b in range(deep.bit_length() - 1)]
    y_masks = [model << b for b in range(wide.bit_length() - 1)]
    x_masks = [2 << b for b in range(across_x.bit_length() - 1)]
    return (z_masks, y_masks, x_masks, [1])


def offsets(masks):
    table = [0]
    for mask in masks:
        table = table + [entry ^ mask for entry in table]
    return table


def origins(masks, early=()):
    deep, wide, across_x, stride = sizes()
    me = device_index()
    places = [
        (flip ^ first, t) for flip in offsets(masks) for t in range(deep) for first in offsets(early)
    ]
    flips = jnp.array([flip for flip, t in places], jnp.int32)
    turns = jnp.array([t for flip, t in places], jnp.int32)
    return (me // stride + turns) % deep * stride + ((me % stride) ^ flips)


def along_z(shift, first, last):
    deep, wide, across_x, stride = sizes()
    return [
        (z * stride + n, (z + shift) * stride + n) for z in range(first, last + 1) for n in range(stride)
    ]


def gather_z(values):
    deep, wide, across_x, stride = sizes()
    z = device_index() // stride
    up, down, ups, downs = values, values, [], []
    for k in range(1, deep):
        up, down = yield [
            (up, along_z(1, k - 1, deep - 2)),
            (down, along_z(-1, 1, deep - k)),
        ]
        ups.append(up)
        downs.append(down)
    return jnp.stack(
        [values] + [jnp.where(z + t < deep, downs[t - 1], ups[deep - t - 1]) for t in range(1, deep)]
    )


def gather_flips(blocks, masks):
    for mask in masks[:-1]:
        (arrived,) = yield [(blocks, across(mask))]
        blocks = jnp.concatenate([blocks, arrived], 0)
    (arrived,) = yield [(blocks, across(masks[-1]))]
    return blocks, arrived


def gather_quarters(blocks, masks):
    for mask in masks[:-2]:
        (arrived,) = yield [(blocks, across(mask))]
        blocks = jnp.concatenate([blocks, arrived], 0)
    arrived, beside = yield [(blocks, across(masks[-2])), (blocks, across(masks[-1]))]
    (last,) = yield [(arrived, across(masks[-1]))]
    return blocks, arrived, beside, last


def gather_all(values, masks):
    blocks = yield from gather_z(values)
    return (yield from gather_flips(blocks, masks))


def reduce_halves(parts, masks):
    kept, sent = parts
    (arrived,) = yield [(sent, across(masks[-1]))]
    terms = [kept, arrived]
    for mask in reversed(masks[:-1]):
        half = terms[0].shape[0] // 2
        sent = sum(term[half:].astype(wide_type) for term in terms).astype(low_type)
        kept = sum(term[:half].astype(wide_type) for term in terms)
        (arrived,) = yield [(sent, across(mask))]
        terms = [kept, arrived]
    return sum(term.astype(wide_type) for term in terms)


def reduce_z(blocks):
    deep = blocks.shape[0]
    up = down = None
    for k in range(deep - 1, 0, -1):
        rising, falling = blocks[k], blocks[deep - k]
        if up is not None:
            rising = rising.astype(wide_type) + up.astype(wide_type)
            falling = falling.astype(wide_type) + down.astype(wide_type)
        up, down = yield [
            (rising.astype(low_type), along_z(1, 0, deep - 1 - k)),
            (falling.astype(low_type), along_z(-1, k, deep - 1)),
        ]
    return blocks[0].astype(wide_type) + up.astype(wide_type) + down.astype(wide_type)


def reduce_deep(blocks, early):
    blocks = blocks.reshape((sizes()[0], -1) + blocks.shape[1:])
    blocks = yield from reduce_z(blocks)
    for mask in reversed(early):
        half = blocks.shape[0] // 2
        (arrived,) = yield [(blocks[half:].astype(low_type), across(mask))]
        blocks = blocks[:half] + arrived.astype(wide_type)
    return blocks[0]


def reduce_all(parts, masks):
    kept, sent = parts
    half = sent.shape[0] // 2
    (later,) = yield [(sent[half:], across(masks[-1]))]
    (sooner,) = yield [(sent[:half], across(masks[-1]))]
    onward = (kept[half:].astype(wide_type) + later.astype(wide_type)).astype(low_type)
    (arrived,) = yield [(onward, across(masks[-2]))]
    terms = [kept[:half], sooner, arrived]
    for mask in reversed(masks[:-2]):
        half = terms[0].shape[0] // 2
        onward = sum(term[half:].astype(wide_type) for term in terms).astype(low_type)
        kept = sum(term[:half].astype(wide_type) for term in terms)
        (arrived,) = yield [(onward, across(mask))]
        terms = [kept, arrived]
    return (yield from reduce_z(sum(term.astype(wide_type) for term in terms)))


class Transfer:
    def __init__(self, steps):
        self.steps = steps
        self.wanted = next(steps)
        self.result = None

    def send(self):
        return [move(*item) for item in self.wanted]

    def receive(self, arrived):
        try:
            self.wanted = self.steps.send(arrived)
        except StopIteration as end:
            self.wanted, self.result = None, end.value

    def finish(self):
        while self.wanted is not None:
            self.receive(self.send())
        return self.result


def advance(transfers, others=()):
    moving = [t for t in transfers if t.wanted is not None]
    arrived, others = lax.optimization_barrier(([t.send() for t in moving], others))
    for transfer, values in zip(moving, arrived):
        transfer.receive(values)
    return others


def gather_rows(values):
    z_masks, y_masks, x_masks, c_masks = bit_masks()
    masks = z_masks + y_masks + x_masks + c_masks
    blocks = values[None]
    for mask in masks:
        blocks = jnp.concatenate([blocks, swap(blocks, mask)], 0)
    return blocks


def in_order(blocks):
    z_masks, y_masks, x_masks, c_masks = bit_masks()
    masks = z_masks + y_masks + x_masks + c_masks
    inverse = [0] * blocks.shape[0]
    for place, entry in enumerate(offsets(masks)):
        inverse[entry] = place
    places = jnp.array(inverse, jnp.int32)
    order = places.at[jnp.arange(len(inverse)) ^ device_index()].get(mode="promise_in_bounds")
    return blocks.at[order].get(mode="promise_in_bounds").reshape((-1,) + blocks.shape[2:])


def together(*values):
    return lax.optimization_barrier(values)


def sum_steps(values):
    for masks in bit_masks():
        for mask in masks:
            rounded = values.astype(low_type)
            (arrived,) = yield [(rounded, across(mask))]
            values = rounded.astype(wide_type) + arrived.astype(wide_type)
    return values


def sum_all(values):
    for masks in reversed(bit_masks()):
        for mask in masks:
            values = jax.tree.map(lambda v: v + swap(v, mask), values)
    return values


def near_far(values, x_masks):
    pieces = [values]
    for mask in x_masks:
        pieces = pieces + [swap(piece, mask) for piece in pieces]
    return pieces


def group_sum(partials, x_masks):
    sums = [kept + swap(sent, 1).astype(wide_type) for kept, sent in partials]
    for mask in reversed(x_masks):
        half = len(sums) // 2
        sums = [
            near + swap(far.astype(low_type), mask).astype(wide_type)
            for near, far in zip(sums[:half], sums[half:])
        ]
    return sums[0]


def dot_nn(left, right):
    return jnp.dot(left, right, preferred_element_type=wide_type)


def dot_nt(left, right):
    return lax.dot_general(left, right, (((1,), (1,)), ((), ())), preferred_element_type=wide_type)


def dot_tn(left, right):
    return lax.dot_general(left, right, (((0,), (0,)), ((), ())), preferred_element_type=wide_type)


def normalise(values):
    centre = values - jnp.mean(values, -1, keepdims=True)
    spread = jnp.mean(centre * centre, -1, keepdims=True)
    scale = lax.rsqrt(spread + norm_eps)
    return centre * scale, scale


def normalise_back(hat, scale, gain, grad):
    lifted = grad * gain
    return scale * (
        lifted
        - jnp.mean(lifted, -1, keepdims=True)
        - hat * jnp.mean(lifted * hat, -1, keepdims=True)
    )


def start_weights(tab_ref, halves, w_ref, sems):
    count, rows, columns = halves[0].shape
    width = w_ref.shape[0]
    columns = columns // width
    for side, half in enumerate(halves):

        def step(r, carry):
            row = pl.multiple_of(tab_ref[0, side * count + r] * rows, rows)
            column = pl.multiple_of(tab_ref[1, side * count + r] * columns, columns)
            for k in range(width):
                pltpu.make_async_copy(
                    half.at[r, :, pl.ds(k * columns, columns)],
                    w_ref.at[k, pl.ds(row, rows), pl.ds(column, columns)],
                    sems.at[k],
                ).start()
            return carry

        lax.fori_loop(0, count, step, 0)


def wait_weights(w_ref, sems, k):
    pltpu.make_async_copy(w_ref.at[k], w_ref.at[k], sems.at[k]).wait()


def store_grads(tab_ref, g_ref, halves, sem, k):
    count, rows, columns = halves[0].shape
    columns = columns // g_ref.shape[0]
    for side, half in enumerate(halves):

        def step(r, carry):
            row = pl.multiple_of(tab_ref[0, side * count + r] * rows, rows)
            column = pl.multiple_of(tab_ref[1, side * count + r] * columns, columns)
            pltpu.make_async_copy(
                g_ref.at[k, pl.ds(row, rows), pl.ds(column, columns)],
                half.at[r, :, pl.ds(k * columns, columns)],
                sem.at[k],
            ).start()
            return carry

        lax.fori_loop(0, count, step, 0)


def lane_masks():
    lane = lax.broadcasted_iota(jnp.int32, (1, 2 * HEAD_DIM), 1)
    return (lane < HEAD_DIM, lane >= HEAD_DIM)


def softmax_columns(keys, query, bias):
    scores = dot_nt(keys, query) + bias
    powers = jnp.exp(scores - jnp.max(scores, 0, keepdims=True))
    return powers * (1.0 / jnp.sum(powers, 0, keepdims=True))


def attention_forward_kernel(count, tab_ref, stream_ref, vec_ref, shift_ref, bias_ref, *refs):
    middle_ref, second_ref, first_ref, qkv_ref, mixed_ref, w_ref, sems = refs[count:]
    start_weights(tab_ref, refs[:count], w_ref, sems)
    width = stream_ref.shape[1]
    hat, scale = normalise(stream_ref[...])
    first_ref[...] = (hat * vec_ref[0:1, :] + vec_ref[1:2, :]).astype(low_type)
    for k in range(3):
        wait_weights(w_ref, sems, k)
        for c in range(0, width, 256):
            part = dot_nn(first_ref[...], w_ref[k, :, c : c + 256]) + shift_ref[k : k + 1, c : c + 256]
            qkv_ref[k, :, c : c + 256] = part.astype(low_type)

    def pair(h, carry):
        at = pl.ds(pl.multiple_of(h * 128, 128), 128)
        query, keys, values = qkv_ref[0, :, at], qkv_ref[1, :, at], qkv_ref[2, :, at]
        query = query * 0.125
        outs = []
        for lanes in lane_masks():
            own = jnp.where(lanes, query, jnp.zeros_like(query))
            scores = dot_nt(own, keys) + bias_ref[...]
            powers = jnp.exp(scores - jnp.max(scores, -1, keepdims=True))
            probs = powers * (1.0 / jnp.sum(powers, -1, keepdims=True))
            outs.append(dot_nn(probs.astype(low_type), values))
        mixed_ref[:, at] = jnp.where(lane_masks()[0], outs[0], outs[1]).astype(low_type)
        return carry

    lax.fori_loop(0, width // 128, pair, 0, unroll=8)
    wait_weights(w_ref, sems, 3)
    for c in range(0, width, 256):
        middle_ref[:, c : c + 256] = (
            stream_ref[:, c : c + 256]
            + dot_nt(mixed_ref[...], w_ref[3, c : c + 256, :])
            + vec_ref[4:5, c : c + 256]
        )
    hat, scale = normalise(middle_ref[...])
    second_ref[...] = (hat * vec_ref[2:3, :] + vec_ref[3:4, :]).astype(low_type)


def attention_chain_kernel(
    count, tab_ref, upper_ref, pull_ref, middle_ref, stream_ref, vec_ref, bias_ref, qkv_ref, *refs
):
    below_ref, below_low_ref, up_ref, joined_ref, rows_ref, w_ref, sems = refs[count : count + 7]
    mixed_grad_ref, mid_grad_ref, norm_grad_ref = refs[count + 7 :]
    start_weights(tab_ref, refs[:count], w_ref, sems)
    width = stream_ref.shape[1]
    upper = upper_ref[...]
    rows_ref[5:6, :] = jnp.sum(upper, 0, keepdims=True)
    pull = pull_ref[...]
    hat, scale = normalise(middle_ref[...])
    rows_ref[2:3, :] = jnp.sum(pull * hat, 0, keepdims=True)
    rows_ref[3:4, :] = jnp.sum(pull, 0, keepdims=True)
    mid_grad = upper + normalise_back(hat, scale, vec_ref[2:3, :], pull)
    mid_grad_ref[...] = mid_grad
    rows_ref[4:5, :] = jnp.sum(mid_grad, 0, keepdims=True)
    up_ref[...] = mid_grad.astype(low_type)
    wait_weights(w_ref, sems, 3)
    for c in range(0, width, 256):
        mixed_grad_ref[:, c : c + 256] = dot_nn(up_ref[...], w_ref[3, :, c : c + 256]).astype(low_type)

    def pair(h, carry):
        at = pl.ds(pl.multiple_of(h * 128, 128), 128)
        query, keys, values = qkv_ref[0, :, at], qkv_ref[1, :, at], qkv_ref[2, :, at]
        grads = mixed_grad_ref[:, at]
        query = query * 0.125
        turned = keys.T
        outs = []
        for h, lanes in enumerate(lane_masks()):
            own = jnp.where(lanes, query, jnp.zeros_like(query))
            own_grad = jnp.where(lanes, grads, jnp.zeros_like(grads))
            probs = softmax_columns(keys, own, bias_ref[...])
            value_grad = dot_nn(probs.astype(low_type), grads)
            prob_grad = dot_nt(values, own_grad)
            drift = jnp.sum(probs * prob_grad, 0, keepdims=True)
            score_grad = (probs * (prob_grad - drift)).astype(low_type)
            query_grad = dot_nn(turned[h * HEAD_DIM : (h + 1) * HEAD_DIM], score_grad)
            outs.append((query_grad, dot_nn(score_grad, query), value_grad))
        first_head = lane_masks()[0]
        parts = (
            jnp.concatenate([outs[0][0], outs[1][0]], 0).T * 0.125,
            jnp.where(first_head, outs[0][1], outs[1][1]),
            jnp.where(first_head, outs[0][2], outs[1][2]),
        )
        for k in range(3):
            part = parts[k]
            joined_ref[k, :, at] = part.astype(low_type)
            if k != 1:
                rows_ref[6 + k // 2 : 7 + k // 2, at] = jnp.sum(part, 0, keepdims=True)
        return carry

    lax.fori_loop(0, width // 128, pair, 0, unroll=4)
    for k in range(3):
        wait_weights(w_ref, sems, k)
    for c in range(0, width, 256):
        norm_grad_ref[:, c : c + 256] = (
            dot_nt(joined_ref[0], w_ref[0, c : c + 256, :])
            + dot_nt(joined_ref[1], w_ref[1, c : c + 256, :])
            + dot_nt(joined_ref[2], w_ref[2, c : c + 256, :])
        )
    hat, scale = normalise(stream_ref[...])
    norm_grad = norm_grad_ref[...]
    rows_ref[0:1, :] = jnp.sum(norm_grad * hat, 0, keepdims=True)
    rows_ref[1:2, :] = jnp.sum(norm_grad, 0, keepdims=True)
    below = mid_grad_ref[...] + normalise_back(hat, scale, vec_ref[0:1, :], norm_grad)
    below_ref[...] = below
    below_low_ref[...] = below.astype(low_type)


def attention_weights_kernel(tab_ref, *refs):
    half_a, half_b, g_ref, first_all, joined_all, up_all, mixed_all, sems = refs[8:]
    rows, width = refs[0].shape
    for side in range(2):
        first_ref, joined_ref, up_ref, mixed_ref = refs[4 * side : 4 * side + 4]
        at = slice(side * rows, (side + 1) * rows)
        first_all[at, :] = first_ref[...]
        up_all[at, :] = up_ref[...]
        mixed_all[at, :] = mixed_ref[...]
        for k in range(3):
            joined_all[k, at, :] = joined_ref[k]
    for k in range(4):
        for c in range(0, width, 256):
            if k < 3:
                part = dot_tn(first_all[...], joined_all[k, :, c : c + 256])
            else:
                part = dot_tn(up_all[...], mixed_all[:, c : c + 256])
            g_ref[k, :, c : c + 256] = part.astype(low_type)
        store_grads(tab_ref, g_ref, (half_a, half_b), sems, k)
    done = g_ref.at[0, :, pl.ds(0, width // 2)]
    for k in range(4):
        pltpu.make_async_copy(done, done, sems.at[k]).wait()


def pack_attention_kernel(joint_ref, output_ref, attention_ref):
    cut = joint_ref.shape[3]
    for layer in range(joint_ref.shape[0]):
        for k in range(3):
            attention_ref[layer, :, k * cut : (k + 1) * cut] = joint_ref[layer, k].astype(low_type)
        attention_ref[layer, :, 3 * cut :] = output_ref[layer].T.astype(low_type)


def pack_hidden_kernel(expand_ref, shrink_ref, hidden_ref):
    local_hidden = expand_ref.shape[2]
    for layer in range(LAYERS):
        hidden_ref[layer, :, :local_hidden] = expand_ref[layer].astype(low_type)
        hidden_ref[layer, :, local_hidden:] = shrink_ref[layer].T.astype(low_type)


def unpack_attention_kernel(pack_ref, joint_ref, output_ref, square_ref):
    cut = joint_ref.shape[2]
    for k in range(3):
        joint_ref[k] = pack_ref[:, k * cut : (k + 1) * cut]
    output_ref[...] = pack_ref[:, 3 * cut :].T
    square_ref[...] = jnp.sum(pack_ref[...] * pack_ref[...], keepdims=True)


def unpack_hidden_kernel(*refs):
    expand_ref, shrink_ref, square_ref = refs[LAYERS:]
    local_hidden = expand_ref.shape[2]
    total = jnp.zeros((1, 1), wide_type)
    for layer, pack_ref in enumerate(refs[:LAYERS]):
        pack = pack_ref[...].astype(wide_type)
        expand_ref[layer] = pack[:, :local_hidden]
        shrink_ref[layer] = pack[:, local_hidden:].T
        total = total + jnp.sum(pack * pack, keepdims=True)
    square_ref[...] = total


def embed_kernel(tab_ref, chosen_ref, base_ref, *refs):
    out_ref, w_ref, sem = refs[-3:]
    count, rows, width = refs[0].shape
    for side, half in enumerate(refs[:-3]):

        def step(r, carry):
            row = pl.multiple_of(tab_ref[side * count + r] * rows, rows)
            pltpu.make_async_copy(half.at[r], w_ref.at[pl.ds(row, rows)], sem).start()
            return carry

        lax.fori_loop(0, count, step, 0)
    pltpu.make_async_copy(w_ref, w_ref, sem).wait()
    for c in range(0, width, 256):
        out_ref[:, c : c + 256] = base_ref[:, c : c + 256] + dot_nn(chosen_ref[...], w_ref[:, c : c + 256])


def embed_weights_kernel(
    tab_ref, chosen_ref, upper_ref, chosen_other, upper_other, half_a, half_b, g_ref, chosen_all, upper_all, sem
):
    count, rows, width = half_a.shape
    depth = chosen_ref.shape[0]
    chosen_all[0:depth, :] = chosen_ref[...]
    chosen_all[depth : 2 * depth, :] = chosen_other[...]
    upper_all[0:depth, :] = upper_ref[...]
    upper_all[depth : 2 * depth, :] = upper_other[...]
    for c in range(0, width, 256):
        g_ref[:, c : c + 256] = dot_tn(chosen_all[...], upper_all[:, c : c + 256]).astype(low_type)
    for side, half in enumerate((half_a, half_b)):

        def step(r, carry):
            row = pl.multiple_of(tab_ref[side * count + r] * rows, rows)
            pltpu.make_async_copy(g_ref.at[pl.ds(row, rows)], half.at[r], sem).start()
            return carry

        lax.fori_loop(0, count, step, 0)
    done = g_ref.at[pl.ds(0, 2 * count * rows)]
    pltpu.make_async_copy(done, done, sem).wait()


gelu_scale = 0.7978845608028654
gelu_cube = 0.044715


def hidden_forward_kernel(count, tab_ref, here_ref, there_ref, raise_ref, *refs):
    kept_ref, sent_ref, w_ref, active_ref, sems = refs[count:]
    start_weights(tab_ref, refs[:count], w_ref, sems)
    rows, width = here_ref.shape
    hidden_width = active_ref.shape[1]
    wait_weights(w_ref, sems, 0)
    for side, source in enumerate((here_ref, there_ref)):
        for c in range(0, hidden_width, 256):
            hidden = dot_nn(source[...], w_ref[0, :, c : c + 256]) + raise_ref[0:1, c : c + 256]
            bent = jnp.tanh(gelu_scale * (hidden + gelu_cube * (hidden * hidden * hidden)))
            active_ref[side * rows : (side + 1) * rows, c : c + 256] = (
                hidden * (0.5 * (1.0 + bent))
            ).astype(low_type)
    wait_weights(w_ref, sems, 1)
    for c in range(0, width, 256):
        kept_ref[:, c : c + 256] = dot_nt(active_ref[0:rows, :], w_ref[1, c : c + 256, :])
        sent_ref[:, c : c + 256] = dot_nt(active_ref[rows : 2 * rows, :], w_ref[1, c : c + 256, :]).astype(low_type)


def hidden_chain_kernel(
    count, tab_ref, here_ref, there_ref, down_here_ref, down_there_ref, raise_ref, *refs
):
    kept_ref, sent_ref, active_ref, grad_ref, raise_grad_ref, w_ref, sems = refs[count:]
    start_weights(tab_ref, refs[:count], w_ref, sems)
    rows, width = here_ref.shape
    hidden_width = active_ref.shape[1]
    wait_weights(w_ref, sems, 0)
    wait_weights(w_ref, sems, 1)
    pairs = ((here_ref, down_here_ref), (there_ref, down_there_ref))
    for c in range(0, hidden_width, 256):
        total = jnp.zeros((1, 256), wide_type)
        for side, (source, down) in enumerate(pairs):
            hidden = dot_nn(source[...], w_ref[0, :, c : c + 256]) + raise_ref[0:1, c : c + 256]
            pulled = dot_nn(down[...], w_ref[1, :, c : c + 256])
            square = hidden * hidden
            bent = jnp.tanh(gelu_scale * (hidden + gelu_cube * (square * hidden)))
            share = 0.5 * (1.0 + bent)
            active_ref[side * rows : (side + 1) * rows, c : c + 256] = (hidden * share).astype(low_type)
            slope = share + (0.5 * hidden) * (1.0 - bent * bent) * (
                gelu_scale + (3.0 * gelu_scale * gelu_cube) * square
            )
            grad = pulled * slope
            grad_ref[side * rows : (side + 1) * rows, c : c + 256] = grad.astype(low_type)
            total = total + jnp.sum(grad, 0, keepdims=True)
        raise_grad_ref[0:1, c : c + 256] = total
    for c in range(0, width, 256):
        kept_ref[:, c : c + 256] = dot_nt(grad_ref[0:rows, :], w_ref[0, c : c + 256, :])
        sent_ref[:, c : c + 256] = dot_nt(grad_ref[rows : 2 * rows, :], w_ref[0, c : c + 256, :]).astype(low_type)


def hidden_weights_kernel(count, tab_ref, *refs):
    groups = [refs[6 * g : 6 * g + 6] for g in range(count)]
    out_ref, g_ref, inputs_ref, down_ref, active_ref, grad_ref, sems = refs[6 * count :]
    rows, width = groups[0][0].shape
    hidden_width = active_ref.shape[1]
    for g, (here, there, down_here, down_there, active, grad) in enumerate(groups):
        at = 2 * g * rows
        inputs_ref[at : at + rows, :] = here[...]
        inputs_ref[at + rows : at + 2 * rows, :] = there[...]
        down_ref[at : at + rows, :] = down_here[...]
        down_ref[at + rows : at + 2 * rows, :] = down_there[...]
        active_ref[at : at + 2 * rows, :] = active[...]
        grad_ref[at : at + 2 * rows, :] = grad[...]
    for k, (left, right) in enumerate(((inputs_ref, grad_ref), (down_ref, active_ref))):
        for c in range(0, hidden_width, 256):
            g_ref[k, :, c : c + 256] = dot_tn(left[...], right[:, c : c + 256]).astype(low_type)
        store_grads(tab_ref, g_ref, (out_ref,), sems, k)
    for k in range(2):
        wait_weights(g_ref, sems, k)


def head_kernel(final_ref, logit_ref, out_ref):
    width = final_ref.shape[1]
    logit = logit_ref[...]
    out_ref[0:width, :] = dot_tn(final_ref[...], logit.astype(low_type))
    out_ref[width : width + 1, :] = jnp.sum(logit, 0, keepdims=True)


smem = pl.BlockSpec(memory_space=pltpu.SMEM)
vmem = pl.BlockSpec(memory_space=pltpu.VMEM)
anywhere = pl.BlockSpec(memory_space=pl.ANY)


def call(kernel, in_specs, outs, scratch, flops, moved):
    return pl.pallas_call(
        kernel,
        out_shape=tuple(jax.ShapeDtypeStruct(shape, kind) for shape, kind, spec in outs),
        in_specs=in_specs,
        out_specs=tuple(spec for shape, kind, spec in outs),
        scratch_shapes=scratch,
        compiler_params=pltpu.CompilerParams(vmem_limit_bytes=48 * 1024 * 1024),
        cost_estimate=pl.CostEstimate(flops=flops, bytes_accessed=moved, transcendentals=0),
    )


def embed(places, chosen, base, halves):
    count, rows, width = halves[0].shape
    depth = chosen.shape[1]
    if rows % 16:
        order = jnp.zeros_like(places).at[places].set(jnp.arange(places.shape[0], dtype=jnp.int32))
        full = jnp.concatenate(halves, 0)[order].reshape(depth, width)
        return base + jnp.dot(chosen, full, preferred_element_type=wide_type)
    return call(
        embed_kernel,
        [smem] + [vmem] * 2 + [anywhere] * len(halves),
        [(base.shape, wide_type, vmem)],
        [pltpu.VMEM((depth, width), low_type), pltpu.SemaphoreType.DMA],
        2 * chosen.shape[0] * depth * width,
        4 * depth * width,
    )(places, chosen, base, *halves)[0]


def embed_weights(places, chosen, upper, chosen_other, upper_other, half_shape):
    count, rows, width = half_shape
    depth, pixels = chosen.shape
    if rows % 16:
        full = lax.dot_general(
            jnp.concatenate([chosen, chosen_other], 0),
            jnp.concatenate([upper, upper_other], 0),
            (((0,), (0,)), ((), ())),
            preferred_element_type=wide_type,
        )
        blocks = full.astype(low_type).reshape(-1, rows, width)[places]
        return blocks[:count], blocks[count:]
    return call(
        embed_weights_kernel,
        [smem] + [vmem] * 4,
        [(half_shape, low_type, anywhere)] * 2,
        [
            pltpu.VMEM((pixels, width), low_type),
            pltpu.VMEM((2 * depth, pixels), low_type),
            pltpu.VMEM((2 * depth, width), low_type),
            pltpu.SemaphoreType.DMA,
        ],
        4 * depth * pixels * width,
        4 * pixels * width,
    )(places, chosen, upper, chosen_other, upper_other)


def attention_forward(stream, vec, shift, bias, gathered):
    tab, *halves = gathered
    rows, width = stream.shape
    return call(
        functools.partial(attention_forward_kernel, len(halves)),
        [smem] + [vmem] * 4 + [anywhere] * len(halves),
        [
            ((rows, width), wide_type, vmem),
            ((rows, width), low_type, vmem),
            ((rows, width), low_type, vmem),
            ((3, rows, width), low_type, vmem),
            ((rows, width), low_type, vmem),
        ],
        [pltpu.VMEM((4, width, width), low_type), pltpu.SemaphoreType.DMA((4,))],
        20 * rows * width * width,
        20 * width * width,
    )(tab, stream, vec, shift, bias, *halves)


def attention_chain(upper, pull, middle, stream, vec, bias, qkv, gathered):
    tab, *halves = gathered
    rows, width = stream.shape
    return call(
        functools.partial(attention_chain_kernel, len(halves)),
        [smem] + [vmem] * 7 + [anywhere] * len(halves),
        [
            ((rows, width), wide_type, vmem),
            ((rows, width), low_type, vmem),
            ((rows, width), low_type, vmem),
            ((3, rows, width), low_type, vmem),
            ((8, width), wide_type, vmem),
        ],
        [
            pltpu.VMEM((4, width, width), low_type),
            pltpu.SemaphoreType.DMA((4,)),
            pltpu.VMEM((rows, width), low_type),
            pltpu.VMEM((rows, width), wide_type),
            pltpu.VMEM((rows, width), wide_type),
        ],
        30 * rows * width * width,
        30 * width * width,
    )(tab, upper, pull, middle, stream, vec, bias, qkv, *halves)


def attention_weights(tab, own, other, half_shape):
    rows, width = own[0].shape
    return call(
        attention_weights_kernel,
        [smem] + [vmem] * 8,
        [(half_shape, low_type, anywhere)] * 2,
        [
            pltpu.VMEM((4, width, width), low_type),
            pltpu.VMEM((2 * rows, width), low_type),
            pltpu.VMEM((3, 2 * rows, width), low_type),
            pltpu.VMEM((2 * rows, width), low_type),
            pltpu.VMEM((2 * rows, width), low_type),
            pltpu.SemaphoreType.DMA((4,)),
        ],
        16 * rows * width * width,
        16 * width * width,
    )(tab, *own, *other)


def hidden_forward(here, there, raise_row, gathered):
    tab, *halves = gathered
    rows, width = here.shape
    hidden_width = raise_row.shape[1]
    return call(
        functools.partial(hidden_forward_kernel, len(halves)),
        [smem] + [vmem] * 3 + [anywhere] * len(halves),
        [((rows, width), wide_type, vmem), ((rows, width), low_type, vmem)],
        [
            pltpu.VMEM((2, width, hidden_width), low_type),
            pltpu.VMEM((2 * rows, hidden_width), low_type),
            pltpu.SemaphoreType.DMA((2,)),
        ],
        16 * rows * width * hidden_width,
        10 * width * hidden_width,
    )(tab, here, there, raise_row, *halves)


def hidden_chain(here, there, down_here, down_there, raise_row, gathered):
    tab, *halves = gathered
    rows, width = here.shape
    hidden_width = raise_row.shape[1]
    return call(
        functools.partial(hidden_chain_kernel, len(halves)),
        [smem] + [vmem] * 5 + [anywhere] * len(halves),
        [
            ((rows, width), wide_type, vmem),
            ((rows, width), low_type, vmem),
            ((2 * rows, hidden_width), low_type, vmem),
            ((2 * rows, hidden_width), low_type, vmem),
            ((1, hidden_width), wide_type, vmem),
        ],
        [pltpu.VMEM((2, width, hidden_width), low_type), pltpu.SemaphoreType.DMA((2,))],
        20 * rows * width * hidden_width,
        20 * width * hidden_width,
    )(tab, here, there, down_here, down_there, raise_row, *halves)


def hidden_weights(tab, groups, out_shape):
    rows, width = groups[0][0].shape
    hidden_width = groups[0][4].shape[1]
    count = len(groups)
    return call(
        functools.partial(hidden_weights_kernel, count),
        [smem] + [vmem] * (6 * count),
        [(out_shape, low_type, anywhere)],
        [
            pltpu.VMEM((2, width, hidden_width), low_type),
            pltpu.VMEM((2 * count * rows, width), low_type),
            pltpu.VMEM((2 * count * rows, width), low_type),
            pltpu.VMEM((2 * count * rows, hidden_width), low_type),
            pltpu.VMEM((2 * count * rows, hidden_width), low_type),
            pltpu.SemaphoreType.DMA((2,)),
        ],
        16 * count * rows * width * hidden_width,
        20 * width * hidden_width,
    )(tab, *[member for group in groups for member in group])[0]


def pack_attention(joint, output):
    layers, rows, cut = joint.shape[0], joint.shape[2], joint.shape[3]
    return call(
        pack_attention_kernel,
        [vmem] * 2,
        [((layers, rows, 4 * cut), low_type, vmem)],
        [],
        1 << 20,
        1 << 21,
    )(joint, output)[0]


def pack_hidden(expand, shrink):
    layers, rows, local_hidden = expand.shape
    return call(
        pack_hidden_kernel,
        [vmem] * 2,
        [((layers, rows, 2 * local_hidden), low_type, vmem)],
        [],
        1 << 20,
        1 << 22,
    )(expand, shrink)[0]


def unpack_attention(pack):
    rows, width = pack.shape
    cut = width // 4
    return call(
        unpack_attention_kernel,
        [vmem],
        [((3, rows, cut), wide_type, vmem), ((cut, rows), wide_type, vmem), ((1, 1), wide_type, vmem)],
        [],
        1 << 20,
        1 << 20,
    )(pack)


def unpack_hidden(packs):
    rows, width = packs[0].shape
    local_hidden = width // 2
    return call(
        unpack_hidden_kernel,
        [vmem] * LAYERS,
        [
            ((LAYERS, rows, local_hidden), wide_type, vmem),
            ((LAYERS, local_hidden, rows), wide_type, vmem),
            ((1, 1), wide_type, vmem),
        ],
        [],
        1 << 20,
        1 << 22,
    )(*packs)


def head_gradient(final_every, logit_every):
    width = final_every.shape[1]
    return call(
        head_kernel,
        [vmem] * 2,
        [((width + 1, logit_every.shape[1]), wide_type, vmem)],
        [],
        1 << 28,
        1 << 23,
    )(final_every, logit_every)[0]


def layer_norm(values, gain_row, shift_row):
    centre = values - jnp.mean(values, -1, keepdims=True)
    spread = jnp.mean(centre * centre, -1, keepdims=True)
    return centre * lax.rsqrt(spread + norm_eps) * gain_row + shift_row


def product(form, left, right):
    return jnp.einsum(form, left, right, preferred_element_type=wide_type)


def adamw(weight, moment_one, moment_two, gradient, rate):
    first_new = beta_one * moment_one + (1.0 - beta_one) * gradient
    second_new = beta_two * moment_two + (1.0 - beta_two) * gradient * gradient
    corrected = first_new / (1.0 - beta_one**STEP)
    scaled = second_new / (1.0 - beta_two**STEP)
    weight_new = weight - rate * (corrected / (jnp.sqrt(scaled) + adam_eps) + decay_rate * weight)
    return (weight_new, first_new, second_new)


def on_device(
    patches,
    keep_list,
    keep_count,
    labels,
    patch_weight,
    vector_table,
    head_table,
    joint_weight,
    shift_table,
    output_weight,
    expand_weight,
    raise_table,
    shrink_weight,
    *moments,
):
    share_images = patches.shape[0]
    model_width = vector_table.shape[1]
    data, model = lax.axis_size("dp"), lax.axis_size("mp")
    devices = data * model
    total_images = share_images * devices
    real_rows = share_images * SLOTS
    rows = -(-real_rows // 16) * 16
    z_masks, y_masks, x_masks, c_masks = bit_masks()
    me = device_index()
    model_index = lax.axis_index("mp")
    local_hidden = expand_weight.shape[2]

    def column_of(devices_at):
        return devices_at // model

    def table(devices_at):
        return jnp.stack([devices_at // model, devices_at % model])

    flip_masks = y_masks + x_masks + c_masks
    turned_masks = x_masks + y_masks + c_masks
    every, turned = origins(flip_masks), origins(turned_masks)
    every_tab, turned_tab, direct_tab = table(every), table(turned), table(jnp.arange(devices, dtype=jnp.int32))
    column = jnp.arange(data, dtype=jnp.int32)
    column_tab = jnp.stack([column, jnp.zeros_like(column)])

    joint_rows = joint_weight.transpose(0, 2, 1, 3)
    first_attention = pack_attention(joint_rows[:1], output_weight[:1])
    attention_packs = pack_attention(joint_rows[1:], output_weight[1:])
    hidden_packs = pack_hidden(expand_weight, shrink_weight)
    pack_rows, pack_width = attention_packs.shape[1:]
    first_pack = jnp.concatenate(
        [first_attention[0], patch_weight.astype(low_type).reshape(-1, pack_width)], 0
    )
    first_move = Transfer(gather_z(first_pack))
    while first_move.wanted is not None:
        hidden_packs, attention_packs = advance([first_move], (hidden_packs, attention_packs))
    hidden_halves = [(column_tab, lax.all_gather(hidden_packs[0], "dp"))]
    attention_later = [
        (direct_tab, lax.all_gather(attention_packs[layer - 1], AXES)) for layer in range(1, LAYERS)
    ]
    attention_blocks = first_move.result[:, :pack_rows]
    patch_blocks = first_move.result[:, pack_rows:].reshape(-1, *patch_weight.shape)
    attention_blocks, patch_blocks, later_packs = together(
        attention_blocks, patch_blocks, hidden_packs
    )
    attention_move = Transfer(gather_quarters(attention_blocks, flip_masks))
    patch_move = Transfer(gather_quarters(patch_blocks, turned_masks))
    later_moves = [Transfer(gather_all(later_packs[layer], y_masks)) for layer in range(1, LAYERS)]
    for step in range(len(flip_masks) - 2):
        advance([patch_move, attention_move] + (later_moves if step == 0 else []))
    advance([patch_move, attention_move])
    patch_halves, attention_first = patch_move.finish(), attention_move.finish()
    attention_halves = [(every_tab,) + attention_first] + attention_later
    first_tab = jnp.stack([column_of(origins((), y_masks)), jnp.zeros_like(column)])
    halves_tab = jnp.stack([column_of(origins(y_masks)), jnp.zeros_like(column)])

    patch_ids = jnp.arange(PATCHES, dtype=jnp.int32)
    kept_slot = patch_ids[None, :] < keep_count[:, None]
    selector = ((keep_list[:, :, None] == patch_ids[None, None, :]) & kept_slot[:, :, None]).astype(
        wide_type
    )
    selector = jnp.pad(selector, ((0, 0), (1, 0), (0, 0)))
    chosen = product("nsp,npc->nsc", selector.astype(low_type), patches).astype(low_type)
    chosen = jnp.pad(chosen.reshape(real_rows, -1), ((0, rows - real_rows), (0, 0)))
    slot_kept = jnp.pad(kept_slot, ((0, 0), (1, 0))).astype(wide_type)
    slot_first = jnp.zeros((share_images, SLOTS), wide_type).at[:, 0].set(1.0)
    spread = jnp.concatenate(
        [selector, slot_kept[:, :, None], slot_first[:, :, None]], 2
    ).reshape(real_rows, PATCHES + 2)
    spread = jnp.pad(spread, ((0, rows - real_rows), (0, 0)))
    sources = jnp.concatenate(
        [
            vector_table[1:SLOTS],
            vector_table[SLOTS + 1 : SLOTS + 2],
            vector_table[SLOTS : SLOTS + 1] + vector_table[0:1],
        ],
        0,
    )
    base = jnp.dot(spread, sources, precision=highest)
    chosen_other = swap(chosen, 1)
    stream = embed(turned, chosen, base, patch_halves)

    row_ids = jnp.arange(rows, dtype=jnp.int32)
    image_ids, slot_ids = row_ids // SLOTS, row_ids % SLOTS
    row_count = jnp.pad(jnp.repeat(keep_count, SLOTS), (0, rows - real_rows), constant_values=SLOTS)
    same_image = image_ids[:, None] == image_ids[None, :]
    live = slot_ids <= row_count
    bias = jnp.where(same_image & live[None, :], 0.0, -1e30).astype(wide_type)
    turned_bias = jnp.where(same_image & live[:, None], 0.0, -1e30).astype(wide_type)

    saved = []
    for layer in range(LAYERS):
        base = SLOTS + 4 + 6 * layer
        vec = vector_table[base : base + 6]
        shift = jnp.stack(
            [shift_table[layer, 0], jnp.zeros((model_width,), wide_type), shift_table[layer, 1]]
        )
        raise_row = lax.dynamic_slice_in_dim(
            raise_table[layer], model_index * local_hidden, local_hidden, 0
        )[None]
        middle, second, first, qkv, mixed = attention_forward(
            stream, vec, shift, bias, attention_halves[layer]
        )
        second = advance(later_moves, second)
        if layer > 0:
            hidden_halves.append((halves_tab,) + later_moves[layer - 1].finish())
        outer = near_far(second, x_masks)
        inner = [swap(outer[0], 1)]
        partials = [hidden_forward(outer[0], inner[0], raise_row, hidden_halves[layer])]
        partials, outer = advance(later_moves, (partials, outer))
        for k in range(1, len(outer)):
            inner.append(swap(outer[k], 1))
            partials.append(hidden_forward(outer[k], inner[k], raise_row, hidden_halves[layer]))
        pieces = (outer, inner)
        beside = (swap(first, 1), swap(mixed, 1))
        saved.append((stream, middle, first, qkv, mixed, beside, pieces, vec, raise_row))
        mlp_out = group_sum(partials, x_masks)
        stream = middle + mlp_out + vec[5:6]

    lead_rows = stream[:real_rows:SLOTS]
    final_out, final_pull = jax.vjp(
        layer_norm, lead_rows, vector_table[SLOTS + 2], vector_table[SLOTS + 3]
    )
    final_low = final_out.astype(low_type)
    head_low = head_table[:model_width].astype(low_type)
    logits = product("nd,dc->nc", final_low, head_low) + head_table[model_width]
    target_hot = (labels[:, None] == jnp.arange(CLASSES, dtype=jnp.int32)[None, :]).astype(
        wide_type
    )
    loss_local = jnp.sum(jax.nn.logsumexp(logits, -1) - jnp.sum(logits * target_hot, -1))
    logit_grad = (jax.nn.softmax(logits, -1) - target_hot) / total_images
    logit_low = logit_grad.astype(low_type)
    head_every = gather_rows(jnp.concatenate([final_low.astype(wide_type), logit_grad], 1))
    final_grad = product("nc,dc->nd", logit_low, head_low)
    lead_grad, gain_final, shift_final = final_pull(final_grad)
    last_row = (share_images - 1) * SLOTS + 1
    upper = lax.pad(
        lead_grad, jnp.zeros((), wide_type), ((0, rows - last_row, SLOTS - 1), (0, 0, 0))
    )
    upper_low = upper.astype(low_type)

    vector_rows, shift_rows, raise_rows = [None] * LAYERS, [None] * LAYERS, [None] * LAYERS
    attention_moves, hidden_sums = [None] * LAYERS, [None] * LAYERS
    waiting = None
    for layer in reversed(range(LAYERS)):
        stream_in, middle, first, qkv, mixed, beside, pieces, vec, raise_row = saved[layer]
        outer, inner = pieces
        outer_down = near_far(upper_low, x_masks)
        inner_down = [swap(outer_down[0], 1)]
        partials, groups, raise_sum = [], [], 0.0
        if waiting is not None:
            waiting, inner_down = together(waiting, inner_down)
            attention_moves[layer + 1] = Transfer(reduce_all(waiting, x_masks + y_masks))
        for k in range(len(outer)):
            if k == 1:
                partials, outer_down = together(partials, outer_down)
            if k > 0:
                inner_down.append(swap(outer_down[k], 1))
            kept, sent, active, grad, raise_part = hidden_chain(
                outer[k], inner[k], outer_down[k], inner_down[k], raise_row, hidden_halves[layer]
            )
            partials.append((kept, sent))
            groups.append((outer[k], inner[k], outer_down[k], inner_down[k], active, grad))
            raise_sum = raise_sum + raise_part
        hidden_grads = hidden_weights(
            column_tab if layer > 0 else first_tab, groups, (data,) + hidden_packs[0].shape
        )
        pull = group_sum(partials, x_masks)
        pull, hidden_grads, head_every = advance(
            attention_moves[layer + 1 :], (pull, hidden_grads, head_every)
        )
        if layer > 0:
            hidden_sums[layer] = lax.psum_scatter(hidden_grads, "dp", scatter_dimension=0)
        else:
            hidden_move = Transfer(reduce_deep(hidden_grads, y_masks))
        upper, upper_low, up, joined, tail = attention_chain(
            upper, pull, middle, stream_in, vec, turned_bias, qkv, attention_halves[layer]
        )
        upper, upper_low, up, joined = advance(
            attention_moves[layer + 1 :], (upper, upper_low, up, joined)
        )
        waiting = attention_weights(
            table(origins(x_masks + y_masks if layer > 0 else y_masks + x_masks)),
            (first, joined, up, mixed),
            (beside[0], swap(joined, 1), swap(up, 1), beside[1]),
            (devices // 4, pack_rows, pack_width),
        )
        vector_rows[layer], shift_rows[layer] = tail[:6], tail[6:]
        raise_rows[layer] = lax.dynamic_update_slice_in_dim(
            jnp.zeros((model, local_hidden), wide_type), raise_sum, model_index, 0
        ).reshape(-1, model_width)

    place = lax.dot_general(
        spread, upper, (((0,), (0,)), ((), ())), precision=highest, preferred_element_type=wide_type
    )
    small = jnp.concatenate(
        [
            place[PATCHES + 1 :],
            place[:PATCHES],
            place[PATCHES + 1 :],
            place[PATCHES : PATCHES + 1],
            gain_final[None],
            shift_final[None],
        ]
        + vector_rows
        + shift_rows
        + raise_rows,
        0,
    )
    chosen, waiting = advance(attention_moves[1:], (chosen, waiting))
    patch_grads = embed_weights(
        origins(x_masks + y_masks), chosen, upper_low, chosen_other, swap(upper_low, 1), patch_halves[0].shape
    )
    patch_grads = advance(attention_moves[1:], patch_grads)
    patch_move = Transfer(reduce_halves(patch_grads, x_masks + y_masks))
    attention_move = Transfer(reduce_halves(waiting, y_masks + x_masks))
    small_move = Transfer(sum_steps(small))
    head_every = in_order(head_every)
    head_sum = head_gradient(head_every[:, :model_width].astype(low_type), head_every[:, model_width:])
    head_sum = advance([patch_move, attention_move, hidden_move, small_move], head_sum)
    while attention_move.wanted is not None:
        advance([patch_move, attention_move, hidden_move, small_move])
    last_blocks = jnp.concatenate(
        [attention_move.result, patch_move.result.reshape(data // sizes()[1], -1, pack_width)], 1
    )
    last_move = Transfer(reduce_z(last_blocks))
    advance([last_move, hidden_move, small_move])
    advance([last_move, hidden_move] + attention_moves[1:])
    while last_move.wanted is not None:
        advance([last_move, small_move] + attention_moves[1:])
    hidden_sums[0] = hidden_move.finish()
    last_sum, small = last_move.result, small_move.finish()
    patch_sum = last_sum[pack_rows:].reshape(patch_weight.shape)
    attention_sums = [last_sum[:pack_rows]] + [m.finish() for m in attention_moves[1:]]
    expand_sum, shrink_sum, shard_sq = unpack_hidden(hidden_sums)
    unpacked = [unpack_attention(total) for total in attention_sums]
    joint_sum = jnp.stack([member[0] for member in unpacked])
    output_sum = jnp.stack([member[1] for member in unpacked])
    for member in unpacked:
        shard_sq = shard_sq + member[2]
    joint_sum = joint_sum.transpose(0, 2, 1, 3)

    vector_count = vector_table.shape[0]
    vector_sum = small[:vector_count]
    shift_sum = small[vector_count : vector_count + 2 * LAYERS].reshape(shift_table.shape)
    raise_sum = small[vector_count + 2 * LAYERS :].reshape(raise_table.shape)
    sharded_sq = shard_sq[0, 0] + jnp.sum(patch_sum * patch_sum)
    shared_sq = jnp.sum(head_sum * head_sum) + jnp.sum(small * small)
    sums = sum_all(jnp.stack([sharded_sq, loss_local]))
    total_sq, loss_total = sums[0] + shared_sq, sums[1]
    gradient_norm = jnp.sqrt(total_sq)
    factor = jnp.minimum(1.0, clip_limit / (gradient_norm + norm_eps))
    weights_in = (
        patch_weight,
        vector_table,
        head_table,
        joint_weight,
        shift_table,
        output_weight,
        expand_weight,
        raise_table,
        shrink_weight,
    )
    reduced = (
        patch_sum,
        vector_sum,
        head_sum,
        joint_sum,
        shift_sum,
        output_sum,
        expand_sum,
        raise_sum,
        shrink_sum,
    )
    outputs = [loss_total, gradient_norm]
    for weight, moment_one, moment_two, gradient, rate in zip(
        weights_in, moments[:9], moments[9:], reduced, group_rates
    ):
        outputs.extend(adamw(weight, moment_one, moment_two, gradient * factor, rate))
    return tuple(outputs)


def solution(mesh):
    params = (
        P(("dp", "mp"), None),
        P(),
        P(),
        P(None, "dp", None, "mp"),
        P(),
        P(None, "mp", "dp"),
        P(None, "dp", "mp"),
        P(),
        P(None, "mp", "dp"),
    )
    in_specs = (
        P(("dp", "mp"), None, None),
        P(("dp", "mp"), None),
        P(("dp", "mp")),
        P(("dp", "mp")),
    ) + 3 * params
    out_specs = (P(), P()) + tuple(spec for spec in params for _ in range(3))
    return jax.shard_map(
        on_device, mesh=mesh, in_specs=in_specs, out_specs=out_specs, check_vma=False
    )
```
